32 devices in a mesh: groups: 2 (over y), graph: 4 (over z), mp: 4 (over x, core).
Axes of the slice: x: 2, y: 2, z: 4, core: 2. Of those that a mesh axis runs over, the one named last changes fastest.
Arguments:
- node_state: float32 [1536, 512], P(('groups', 'graph'), 'mp'), parts along dimension 0, may hold values from -6 to 6
- edge_state: float32 [12288, 512], P(('groups', 'graph'), 'mp'), parts along dimension 0, may hold values from -6 to 6
- edge_first: bfloat16 [2, 1536, 512], P(None, None, 'mp'), may hold values from -0.15625 to 0.15625
- edge_second: bfloat16 [2, 512, 512], P(None, 'mp'), may hold values from -0.25 to 0.25
- node_first: bfloat16 [2, 1024, 512], P(None, None, 'mp'), may hold values from -0.1875 to 0.1875
- node_second: bfloat16 [2, 512, 512], P(None, 'mp'), may hold values from -0.25 to 0.25
- senders: int32 [6144], P('graph'), may hold values from 0 to 303, as said below
- receivers: int32 [6144], P('graph'), may hold values from 0 to 191, as said below
- boundary_rows: int32 [256], P('graph'), may hold values from 0 to 191, as said below
Outputs:
- node_result: float32 [1536, 512], P(('groups', 'graph'), 'mp'), parts along dimension 0
- edge_result: float32 [12288, 512], P(('groups', 'graph'), 'mp'), parts along dimension 0
The draws below stay inside these ranges and needn't reach their ends.
There are 2 independent parts, one for each index of `groups`. The reference program is written for one: setup_inputs(seed, part) draws one part's arguments, and reference() takes and returns one part's arrays. A program takes and returns all parts, laid end to end along the dimension named above; an argument that names none is the same for every part. Nothing has to cross between parts.
Inputs may be any that keep to these rules, and one draw needn't show every extreme that they name: Entries index the node table of the edge's block: below 192 the block's own nodes, then 32 rows of the previous block's list for its next neighbour, then 32 rows of the next block's list for its previous neighbour (blocks taken cyclically), then the 48 coarse nodes, block by block, each block's last 12 nodes in order. In every block the last 192 edges have coarse senders and the others do not. `receivers`: receivers are nodes of the edge's own block; the last 192 edges of every block go to one of its last 12 nodes. `boundary_rows`: entry b * 2 * 32 + j is a node of block b: for j < 32 one that block b - 1 reads, else one that block b + 1 reads (cyclically).
All inputs are finite; a program needn't handle non-finite values.
Results may differ from the reference program's by a relative error of at most 0.014.
Values may be sent and summed in bfloat16 or wider, within the bound.
No kernel may reach another device: no remote copies, remote signals or barrier semaphores. Data moves between devices by JAX's collectives and lax.ppermute only.
A program may use at most 64 MiB of HBM per device.

```python
import jax
import jax.numpy as jnp
from jax import lax

D = 512
HID = 512
NODE_DEV = 192
LAYERS = 2
BLOCKS = 4
HID_PART = 128
NODES = 768
COARSE_DEV = 12
COARSE = 48
HALO = 32
EDGE_DEV = 1536
COARSE_EDGE_DEV = 192
EDGES = 6144
N_MP = 4


def draw_senders(key, part):
    key = jax.random.fold_in(key, 11)
    keys = jax.random.split(key, 4)
    position = jnp.arange(EDGES, dtype=jnp.int32) % EDGE_DEV
    table_start = NODE_DEV + 2 * HALO
    own_index = jax.random.randint(keys[0], (EDGES,), 0, NODE_DEV, dtype=jnp.int32)
    halo_index = jax.random.randint(keys[1], (EDGES,), NODE_DEV, table_start, dtype=jnp.int32)
    selector = jax.random.randint(keys[2], (EDGES,), 0, 4, dtype=jnp.int32)
    coarse_index = jax.random.randint(keys[3], (EDGES,), table_start, table_start + COARSE, dtype=jnp.int32)
    fine_index = jnp.where(selector == 0, halo_index, own_index)
    chosen = jnp.where(position < EDGE_DEV - COARSE_EDGE_DEV, fine_index, coarse_index)
    chosen = chosen.at[0].set(0).at[EDGES - 1].set(table_start + COARSE - 1)
    return chosen.astype(jnp.int32)


def draw_receivers(key, part):
    key = jax.random.fold_in(key, 12)
    keys = jax.random.split(key, 2)
    position = jnp.arange(EDGES, dtype=jnp.int32) % EDGE_DEV
    fine_index = jax.random.randint(keys[0], (EDGES,), 0, NODE_DEV, dtype=jnp.int32)
    coarse_index = jax.random.randint(keys[1], (EDGES,), NODE_DEV - COARSE_DEV, NODE_DEV, dtype=jnp.int32)
    chosen = jnp.where(position < EDGE_DEV - COARSE_EDGE_DEV, fine_index, coarse_index)
    chosen = chosen.at[0].set(0).at[EDGES - 1].set(NODE_DEV - 1)
    return chosen.astype(jnp.int32)


def draw_boundary_rows(key, part):
    key = jax.random.fold_in(key, 13)
    block_keys = jax.random.split(key, BLOCKS)
    listed = jax.vmap(lambda sub_key: jax.random.permutation(sub_key, NODE_DEV)[:2 * HALO])(block_keys)
    flat_list = listed.reshape(-1).astype(jnp.int32)
    flat_list = flat_list.at[0].set(0).at[1].set(NODE_DEV - 1)
    return flat_list.astype(jnp.int32)


def block_scale(key, dims, pieces, low, high):
    def one(axis_at, shards_of):
        steps = jax.random.uniform(jax.random.fold_in(jax.random.fold_in(key, 6), axis_at), (shards_of,), jnp.float32, low / len(pieces), high / len(pieces))
        return jnp.repeat(jnp.exp(steps), dims[axis_at] // shards_of).reshape((-1,) + (1,) * (len(dims) - axis_at - 1))

    gain = one(*pieces[0])
    for cut in pieces[1:]:
        gain = gain * one(*cut)
    return gain


def centred(own_key, dims, width, most, shards=(), kind=jnp.bfloat16):
    values = width * jax.random.normal(own_key, dims, jnp.float32)
    if shards:
        values = values * block_scale(own_key, dims, shards, -0.22, 0.18)
    return jnp.clip(values, -most, most).astype(kind)


def setup_inputs(seed: int = 0, part: int = 0) -> dict:
    arg_keys = jax.random.split(jax.random.key(seed), 10)
    own_keys = jax.random.split(jax.random.fold_in(arg_keys[9], part), 10)
    return {
        "node_state": centred(own_keys[0], (NODES, D), 1.0, 6.0, ((0, 4), (1, 4)), jnp.float32),
        "edge_state": centred(own_keys[1], (EDGES, D), 1.0, 6.0, ((0, 4), (1, 4)), jnp.float32),
        "edge_first": centred(arg_keys[2], (LAYERS, 3 * D, HID), (3 * D) ** -0.5, 0.15625, ((2, 4),)),
        "edge_second": centred(arg_keys[3], (LAYERS, HID, D), HID ** -0.5, 0.25, ((1, 4),)),
        "node_first": centred(arg_keys[4], (LAYERS, 2 * D, HID), (2 * D) ** -0.5, 0.1875, ((2, 4),)),
        "node_second": centred(arg_keys[5], (LAYERS, HID, D), HID ** -0.5, 0.25, ((1, 4),)),
        "senders": draw_senders(jax.random.fold_in(arg_keys[9], 71), part),
        "receivers": draw_receivers(jax.random.fold_in(arg_keys[9], 71), part),
        "boundary_rows": draw_boundary_rows(jax.random.fold_in(arg_keys[9], 71), part),
    }


def endpoints(senders, receivers, boundary_rows):
    block_index = jnp.arange(EDGES, dtype=jnp.int32) // EDGE_DEV
    left_block = (block_index - 1) % BLOCKS
    right_block = (block_index + 1) % BLOCKS
    offset_left = jnp.clip(senders - NODE_DEV, 0, HALO - 1)
    offset_right = jnp.clip(senders - NODE_DEV - HALO, 0, HALO - 1)
    from_left = boundary_rows[left_block * 2 * HALO + HALO + offset_left]
    from_right = boundary_rows[right_block * 2 * HALO + offset_right]
    coarse_index = jnp.clip(senders - NODE_DEV - 2 * HALO, 0, COARSE - 1)
    coarse_node = coarse_index // COARSE_DEV * NODE_DEV + NODE_DEV - COARSE_DEV + coarse_index % COARSE_DEV
    source = jnp.where(senders < NODE_DEV, block_index * NODE_DEV + senders, jnp.where(senders < NODE_DEV + HALO, left_block * NODE_DEV + from_left, jnp.where(senders < NODE_DEV + 2 * HALO, right_block * NODE_DEV + from_right, coarse_node)))
    target = block_index * NODE_DEV + receivers
    return (source.astype(jnp.int32), target.astype(jnp.int32))

def grouped_product(hidden, weight):
    summed = jnp.zeros((hidden.shape[0], weight.shape[1]), jnp.float32)
    for group_index in range(N_MP):
        lower = group_index * HID_PART
        term = jnp.dot(hidden[:, lower:lower + HID_PART], weight[lower:lower + HID_PART], preferred_element_type=jnp.float32)
        summed = summed + lax.optimization_barrier(term.astype(jnp.bfloat16)).astype(jnp.float32)
    return summed

def row_normalize(summed):
    feature_count = summed.shape[1]
    row_mean = lax.optimization_barrier(jnp.sum(summed, axis=1, keepdims=True)) / feature_count
    squares = lax.optimization_barrier(jnp.sum(summed * summed, axis=1, keepdims=True)) / feature_count
    return (summed - row_mean) * lax.rsqrt(squares - row_mean * row_mean + 1e-05)

def reference(node_state, edge_state, edge_first, edge_second, node_first, node_second, senders, receivers, boundary_rows):
    source, target = endpoints(senders, receivers, boundary_rows)
    node_latent = node_state
    edge_latent = edge_state
    for layer_index in range(LAYERS):
        node_bf = node_latent.astype(jnp.bfloat16)
        edge_bf = edge_latent.astype(jnp.bfloat16)
        first = edge_first[layer_index]
        preact = jnp.dot(edge_bf, first[:D], preferred_element_type=jnp.float32)
        preact = preact + jnp.dot(node_bf[source], first[D:2 * D], preferred_element_type=jnp.float32)
        preact = preact + jnp.dot(node_bf[target], first[2 * D:], preferred_element_type=jnp.float32)
        hidden = jax.nn.silu(preact).astype(jnp.bfloat16)
        edge_latent = edge_latent + row_normalize(grouped_product(hidden, edge_second[layer_index]))
        incoming = jax.ops.segment_sum(edge_latent, target, num_segments=NODES)
        incoming_bf = incoming.astype(jnp.bfloat16)
        second_first = node_first[layer_index]
        preact = jnp.dot(node_bf, second_first[:D], preferred_element_type=jnp.float32)
        preact = preact + jnp.dot(incoming_bf, second_first[D:], preferred_element_type=jnp.float32)
        hidden = jax.nn.silu(preact).astype(jnp.bfloat16)
        node_latent = node_latent + row_normalize(grouped_product(hidden, node_second[layer_index]))
    return (node_latent, edge_latent)
```

```python
import functools

import jax
import jax.numpy as jnp
from jax import lax
from jax.experimental import pallas as pl
from jax.experimental.pallas import tpu as pltpu
from jax.sharding import PartitionSpec as P

COARSE_DEV = 12
COARSE_PAD = 16
EPS = 1e-05
TILE = 256
F32 = jnp.float32
BF16 = jnp.bfloat16


def silu(x):
    half = 0.5 * x
    return half + half * jnp.tanh(half)


def normalize(msg):
    width = msg.shape[1]
    mean = jnp.sum(msg, axis=1, keepdims=True) / width
    square = jnp.sum(msg * msg, axis=1, keepdims=True) / width
    return (msg - mean) * lax.rsqrt(square - mean * mean + EPS)


def dot(a, b):
    return jnp.dot(a, b, preferred_element_type=F32)


def fill_weights(spot_ref, pieces, full_ref, second_ref, first_rows):
    own, core, x_near, x_far, d_near, d_far = pieces
    rows, part = own.shape
    half = rows // 2
    near = pl.multiple_of(spot_ref[1] * half, half)
    far = pl.multiple_of((1 - spot_ref[1]) * half, half)
    full_ref[:, 0:part] = own[...]
    full_ref[:, part : 2 * part] = core[...]
    full_ref[pl.ds(near, half), 2 * part : 3 * part] = x_near[...]
    full_ref[pl.ds(far, half), 2 * part : 3 * part] = x_far[...]
    full_ref[pl.ds(near, half), 3 * part : 4 * part] = d_near[...]
    full_ref[pl.ds(far, half), 3 * part : 4 * part] = d_far[...]
    for j in range(4):
        for q in range(4):
            second_ref[j * part : (j + 1) * part, q * part : (q + 1) * part] = full_ref[
                first_rows + q * part : first_rows + (q + 1) * part, j * part : (j + 1) * part
            ]


def fill_features(spot_ref, shards, full_ref):
    part = shards[0].shape[1]
    for j, shard in enumerate(shards):
        column = pl.multiple_of((spot_ref[0] ^ j) * part, part)
        full_ref[:, pl.ds(column, part)] = shard[...]


def pick_rows(wanted_ref, node_bf):
    wanted = wanted_ref[...]
    lanes = lax.broadcasted_iota(jnp.int32, (wanted.shape[0], node_bf.shape[0]), 1)
    return dot(jnp.where(lanes == wanted, 1.0, 0.0).astype(BF16), node_bf).astype(BF16)


def send_rows(wanted_ref, node_bf, outs):
    picked = pick_rows(wanted_ref, node_bf)
    start = 0
    for out in outs:
        out[...] = picked[start : start + out.shape[0]]
        start += out.shape[0]


def start_kernel(spot_ref, own, core, far, diag, wanted_ref, node_ref, right_ref, left_ref, coarse_ref):
    fill_features(spot_ref, (own, core, far, diag), node_ref)
    send_rows(wanted_ref, node_ref[...], (right_ref, left_ref, coarse_ref))


def edge_kernel(pieces, shards, layer_last, *refs):
    refs = list(refs)
    spot_ref = refs.pop(0)
    weights = [refs.pop(0) for _ in range(6)]
    edges = [refs.pop(0) for _ in range(shards)]
    own_ref = refs.pop(0)
    tables = [refs.pop(0) for _ in range(pieces)]
    index_ref, receiver_ref = refs.pop(0), refs.pop(0)
    own_out, incoming_out = refs.pop(0), refs.pop(0)
    full_out = None if layer_last else refs.pop(0)
    w_ref, second_ref, product_ref, table_ref, norm_ref = refs[:5]
    feature_count = second_ref.shape[1]
    node_count = incoming_out.shape[0]
    first_rows = 3 * feature_count
    fill_weights(spot_ref, weights, w_ref, second_ref, first_rows)
    if shards == 1:
        edge_ref = edges[0]
    else:
        edge_ref = refs[5]
        fill_features(spot_ref, edges, edge_ref)
    start = 0
    for table in tables:
        table_ref[start : start + table.shape[0], :] = table[...]
        start += table.shape[0]
    product_ref[0:start, :] = dot(
        table_ref[...], w_ref[feature_count : 2 * feature_count, :]
    ).astype(BF16)
    product_ref[start : start + node_count, :] = dot(
        tables[0][...], w_ref[2 * feature_count : first_rows, :]
    ).astype(BF16)
    used = start + node_count
    lanes_all = product_ref.shape[0]
    if used < lanes_all:
        product_ref[used:, :] = jnp.zeros((lanes_all - used, feature_count), BF16)
    part = own_ref.shape[1]
    column = pl.multiple_of(spot_ref[0] * part, part)
    incoming = jnp.zeros((node_count, feature_count), F32)
    for at in range(0, edge_ref.shape[0], TILE):
        rows = slice(at, at + TILE)
        edge_bf = edge_ref[rows, :]
        index = index_ref[rows, :]
        lanes = lax.broadcasted_iota(jnp.int32, (TILE, lanes_all), 1)
        hot = (lanes == index[:, 0:1]) | (lanes == index[:, 1:2])
        pre = dot(edge_bf, w_ref[0:feature_count, :]) + dot(
            jnp.where(hot, 1.0, 0.0).astype(BF16), product_ref[...]
        )
        norm = normalize(dot(silu(pre).astype(BF16), second_ref[...]))
        norm_ref[rows, :] = norm
        edge_new = (edge_bf.astype(F32) + norm).astype(BF16)
        if full_out is not None:
            full_out[rows, :] = edge_new
        own_out[rows, :] = own_ref[rows, :] + norm_ref[rows, pl.ds(column, part)]
        nodes = lax.broadcasted_iota(jnp.int32, (node_count, TILE), 0)
        incidence = jnp.where(nodes == receiver_ref[:, rows], 1.0, 0.0).astype(BF16)
        incoming = incoming + dot(incidence, edge_new)
    incoming_out[...] = incoming.astype(BF16)


def node_kernel(layer_last, *refs):
    refs = list(refs)
    spot_ref = refs.pop(0)
    weights = [refs.pop(0) for _ in range(6)]
    node_ref, own_ref, incoming_ref = refs.pop(0), refs.pop(0), refs.pop(0)
    wanted_ref = None if layer_last else refs.pop(0)
    own_out = refs.pop(0)
    outs = [] if layer_last else [refs.pop(0) for _ in range(4)]
    w_ref, second_ref, norm_ref = refs
    feature_count = second_ref.shape[1]
    first_rows = 2 * feature_count
    fill_weights(spot_ref, weights, w_ref, second_ref, first_rows)
    node_bf = node_ref[...]
    pre = dot(node_bf, w_ref[0:feature_count, :]) + dot(
        incoming_ref[...], w_ref[feature_count:first_rows, :]
    )
    norm = normalize(dot(silu(pre).astype(BF16), second_ref[...]))
    norm_ref[...] = norm
    part = own_ref.shape[1]
    column = pl.multiple_of(spot_ref[0] * part, part)
    own_out[...] = own_ref[...] + norm_ref[:, pl.ds(column, part)]
    if not layer_last:
        node_new = (node_bf.astype(F32) + norm).astype(BF16)
        outs[0][...] = node_new
        send_rows(wanted_ref, node_new, outs[1:])


def call(kernel, out_shape, args, scratch, flops, name):
    in_specs = [pl.BlockSpec(memory_space=pltpu.SMEM)]
    in_specs += [pl.BlockSpec(memory_space=pltpu.VMEM)] * (len(args) - 1)
    moved = sum(a.size * a.dtype.itemsize for a in list(args) + list(out_shape))
    return pl.pallas_call(
        kernel,
        out_shape=out_shape,
        in_specs=in_specs,
        out_specs=[pl.BlockSpec(memory_space=pltpu.VMEM)] * len(out_shape),
        scratch_shapes=scratch,
        compiler_params=pltpu.CompilerParams(vmem_limit_bytes=48 * 1024 * 1024),
        cost_estimate=pl.CostEstimate(flops=flops, bytes_accessed=moved, transcendentals=0),
        name=name,
    )(*args)


def swap(x, mask):
    size = lax.axis_size("mp")
    return lax.ppermute(x, "mp", [(i, i ^ mask) for i in range(size)])


def pack(first, second):
    part = first.shape[1]
    blocks = [second[:, q : q + part] for q in range(0, second.shape[1], part)]
    return jnp.concatenate([first] + blocks, axis=0)


def gather_weights(packed):
    half = packed.shape[0] // 2
    near = lax.dynamic_slice_in_dim(packed, lax.axis_index("groups") * half, half, axis=0)
    x_near = swap(near, 2)
    x_far = lax.ppermute(x_near, "groups", [(0, 1), (1, 0)])
    return (packed, swap(packed, 1), x_near, x_far, swap(x_near, 1), swap(x_far, 1))


def shift(x, by):
    size = lax.axis_size("graph")
    return lax.ppermute(x, "graph", [(i, (i + by) % size) for i in range(size)])


def neighbour_rows(right, left, coarse, halo):
    if lax.axis_size("graph") == 4:
        return [shift(right, 1), shift(left, -1), shift(coarse, 2)]
    everyone = lax.all_gather(coarse, "graph", axis=0, tiled=True)
    return [shift(right[:halo], 1), shift(left[:halo], -1), everyone]


def table_index(senders, node_count, halo):
    size = lax.axis_size("graph")
    coarse_start = node_count + 2 * halo
    number = jnp.maximum(senders - coarse_start, 0)
    block, row = number // COARSE_DEV, number % COARSE_DEV
    if size != 4:
        return jnp.where(senders < coarse_start, senders, coarse_start + block * COARSE_PAD + row)
    wide = halo + COARSE_PAD
    away = (block - lax.axis_index("graph")) % size
    starts = (node_count - COARSE_DEV, node_count + wide + halo, node_count + 2 * wide, node_count + halo)
    base = jnp.where(
        away < 2,
        jnp.where(away == 0, starts[0], starts[1]),
        jnp.where(away == 2, starts[2], starts[3]),
    )
    fine = jnp.where(senders < node_count + halo, senders, senders + COARSE_PAD)
    return jnp.where(senders < coarse_start, fine, base + row)


def on_device(
    node_state,
    edge_state,
    edge_first,
    edge_second,
    node_first,
    node_second,
    senders,
    receivers,
    boundary_rows,
):
    node_count, part = node_state.shape
    edge_count = edge_state.shape[0]
    layer_count = edge_first.shape[0]
    feature_count = edge_second.shape[2]
    halo = boundary_rows.shape[0] // 2
    shape = jax.ShapeDtypeStruct
    spot = jnp.stack([lax.axis_index("mp"), lax.axis_index("groups")]).astype(jnp.int32)

    node_bf = node_state.astype(BF16)
    node_shards = (node_bf, swap(node_bf, 1), swap(node_bf, 2), swap(node_bf, 3))
    edge_bf = edge_state.astype(BF16)
    edge_far = swap(edge_bf, 2)
    edges = (edge_bf, swap(edge_bf, 1), edge_far, swap(edge_far, 1))

    own_coarse = jnp.arange(node_count - COARSE_DEV, node_count, dtype=jnp.int32)
    padding = jnp.full((COARSE_PAD - COARSE_DEV,), -1, jnp.int32)
    coarse_list = jnp.concatenate([own_coarse, padding])
    wanted = jnp.concatenate(
        [boundary_rows[halo:], coarse_list, boundary_rows[:halo], coarse_list, coarse_list]
    )[:, None]
    sent = [
        shape((halo + COARSE_PAD, feature_count), BF16),
        shape((halo + COARSE_PAD, feature_count), BF16),
        shape((COARSE_PAD, feature_count), BF16),
    ]
    full_node = shape((node_count, feature_count), BF16)
    picking = 2 * wanted.shape[0] * node_count * feature_count
    node_full, right, left, coarse = call(
        start_kernel, [full_node] + sent, [spot, *node_shards, wanted], [], picking, "boundary_rows"
    )

    edge_weights = [
        gather_weights(pack(edge_first[layer], edge_second[layer])) for layer in range(layer_count)
    ]
    node_weights = [
        gather_weights(pack(node_first[layer], node_second[layer])) for layer in range(layer_count)
    ]

    node_own, edge_own = node_state, edge_state
    receiver_row = receivers[None, :]
    for layer in range(layer_count):
        last = layer == layer_count - 1
        tables = [node_full] + neighbour_rows(right, left, coarse, halo)
        table_rows = sum(t.shape[0] for t in tables)
        lanes = -(-(table_rows + node_count) // 128) * 128
        index = jnp.stack(
            [table_index(senders, node_count, halo), receivers + table_rows], axis=1
        )
        outs = [shape((edge_count, part), F32), shape((node_count, feature_count), BF16)]
        if not last:
            outs.append(shape((edge_count, feature_count), BF16))
        scratch = [
            pltpu.VMEM((4 * feature_count, feature_count), BF16),
            pltpu.VMEM((feature_count, feature_count), BF16),
            pltpu.VMEM((lanes, feature_count), BF16),
            pltpu.VMEM((table_rows, feature_count), BF16),
            pltpu.VMEM((edge_count, feature_count), F32),
        ]
        if len(edges) > 1:
            scratch.append(pltpu.VMEM((edge_count, feature_count), BF16))
        done = call(
            functools.partial(edge_kernel, len(tables), len(edges), last),
            outs,
            [spot, *edge_weights[layer], *edges, edge_own, *tables, index, receiver_row],
            scratch,
            2 * edge_count * feature_count * (2 * feature_count + lanes + node_count),
            "edge_layer",
        )
        edge_own, incoming = done[0], done[1]
        edges = done[2:]
        outs = [shape((node_count, part), F32)]
        args = [spot, *node_weights[layer], node_full, node_own, incoming]
        if not last:
            outs += [full_node] + sent
            args.append(wanted)
        done = call(
            functools.partial(node_kernel, last),
            outs,
            args,
            [
                pltpu.VMEM((3 * feature_count, feature_count), BF16),
                pltpu.VMEM((feature_count, feature_count), BF16),
                pltpu.VMEM((node_count, feature_count), F32),
            ],
            2 * node_count * feature_count * 3 * feature_count,
            "node_layer",
        )
        node_own = done[0]
        if not last:
            node_full, right, left, coarse = done[1:]
    return (node_own, edge_own)


def solution(mesh):
    in_specs = (
        P(("groups", "graph"), "mp"),
        P(("groups", "graph"), "mp"),
        P(None, None, "mp"),
        P(None, "mp", None),
        P(None, None, "mp"),
        P(None, "mp", None),
        P("graph"),
        P("graph"),
        P("graph"),
    )
    out_specs = (P(("groups", "graph"), "mp"), P(("groups", "graph"), "mp"))
    return jax.shard_map(
        on_device, mesh=mesh, in_specs=in_specs, out_specs=out_specs, check_vma=False
    )
```

```python
import functools

import jax
import jax.numpy as jnp
from jax import lax
from jax.experimental import pallas as pl
from jax.experimental.pallas import tpu as pltpu
from jax.sharding import PartitionSpec as P

COARSE_DEV = 12
COARSE_PAD = 16
EPS = 1e-05
TILE = 256
F32 = jnp.float32
BF16 = jnp.bfloat16


def silu(x):
    half = 0.5 * x
    return half + half * jnp.tanh(half)


def normalize(msg):
    width = msg.shape[1]
    mean = jnp.sum(msg, axis=1, keepdims=True) * (1.0 / width)
    square = jnp.sum(msg * msg, axis=1, keepdims=True) * (1.0 / width)
    return (msg - mean) * lax.rsqrt(square - mean * mean + EPS)


def dot(a, b):
    return jnp.dot(a, b, preferred_element_type=F32)


def own_columns(full, spot_ref, part):
    mine = spot_ref[0]
    out = full[:, 0:part]
    for j in range(1, full.shape[1] // part):
        out = jnp.where(mine == j, full[:, j * part : (j + 1) * part], out)
    return out


class Copies:
    def __init__(self, sems):
        self.sems, self.started = sems, []

    def start(self, source, target):
        copy = pltpu.make_async_copy(source, target, self.sems.at[len(self.started)])
        copy.start()
        self.started.append(copy)

    def wait(self):
        for copy in self.started:
            copy.wait()


def load_weights(copies, shards, base, first_ref, second_ref, y):
    first_rows = first_ref.shape[0]
    hidden, features = second_ref.shape
    part = hidden // 4
    for j, shard in enumerate(shards):
        columns = pl.ds(j * part, part)
        if len(shard) == 1:
            copies.start(shard[0].at[pl.ds(base, first_rows)], first_ref.at[:, columns])
        for q in range(features // part):
            target = second_ref.at[pl.ds(j * part, part), pl.ds(q * part, part)]
            at = first_rows + q * part
            if len(shard) == 1:
                copies.start(shard[0].at[pl.ds(base + at, part)], target)


def pack_kernel(spot_ref, ef, es, nf, ns, edge_out, node_out, late_out, ride_out, big, sems):
    features = es.shape[2]
    part = es.shape[1]
    copies = Copies(sems)
    at = 0
    for layer in range(ef.shape[0]):
        for first, second in ((ef, es), (nf, ns)):
            rows = first.shape[1]
            copies.start(first.at[layer], big.at[pl.ds(at, rows)])
            at += rows
            for q in range(features // part):
                copies.start(second.at[layer, :, pl.ds(q * part, part)], big.at[pl.ds(at, part)])
                at += part
    copies.wait()
    copies = Copies(sems)
    at = 0
    for out in (edge_out, node_out, late_out):
        copies.start(big.at[pl.ds(at, out.shape[0])], out)
        at += out.shape[0]
    if ride_out is not None:
        y, eighth = spot_ref[1], spot_ref[2]
        half = edge_out.shape[0] // 2
        copies.start(big.at[pl.ds(pl.multiple_of(y * half, half), half)], ride_out.at[pl.ds(0, half)])
        to, at = half, edge_out.shape[0]
        for out in (node_out, late_out):
            size = out.shape[0] // 8
            start = pl.multiple_of(at + eighth * size, 16)
            copies.start(big.at[pl.ds(start, size)], ride_out.at[pl.ds(to, size)])
            to += size
            at += out.shape[0]
    copies.wait()


def pack_kernel_plain(spot_ref, ef, es, nf, ns, edge_out, node_out, late_out, big, sems):
    pack_kernel(spot_ref, ef, es, nf, ns, edge_out, node_out, late_out, None, big, sems)


def pick_rows(wanted_ref, node_bf, outs):
    wanted = wanted_ref[...]
    lanes = lax.broadcasted_iota(jnp.int32, (wanted.shape[0], node_bf.shape[0]), 1)
    picked = dot(jnp.where(lanes == wanted, 1.0, 0.0).astype(BF16), node_bf).astype(BF16)
    start = 0
    for out in outs:
        out[...] = picked[start : start + out.shape[0]]
        start += out.shape[0]


def start_kernel(edge_ref, node_ref, wanted_ref, edge_out, node_out, right, left, coarse):
    edge_out[...] = edge_ref[...].astype(BF16)
    node_bf = node_ref[...].astype(BF16)
    node_out[...] = node_bf
    pick_rows(wanted_ref, node_bf, (right, left, coarse))


def load_first_weights(copies, spot_ref, own, core, x_pair, d_pair, w_ref, blocks_ref):
    rows = own.shape[0]
    part = own.shape[1]
    copies.start(own, w_ref.at[:, pl.ds(0, part)])
    copies.start(core, w_ref.at[:, pl.ds(part, part)])
    for j, pair in ((2, x_pair), (3, d_pair)):
        columns = pl.ds(j * part, part)
        if len(pair) == 1:
            copies.start(pair[0], w_ref.at[:, columns])
            continue
        half = rows // 2
        near = pl.multiple_of(spot_ref[1] * half, half)
        far = pl.multiple_of((1 - spot_ref[1]) * half, half)
        copies.start(pair[0], w_ref.at[pl.ds(near, half), columns])
        copies.start(pair[1], w_ref.at[pl.ds(far, half), columns])


def edge_rows(spot_ref, edge_ref, table, nodes, own_ref, index_ref, receiver_ref, first_ref, second_ref, product_ref, own_out, full_out):
    features = second_ref.shape[1]
    node_count = nodes.shape[0]
    table_rows = table.shape[0]
    lanes_all = product_ref.shape[0]
    used = table_rows + node_count
    part = own_ref.shape[1]
    product_ref[0:table_rows, :] = dot(table, first_ref[features : 2 * features, :]).astype(BF16)
    product_ref[table_rows:used, :] = dot(
        nodes, first_ref[2 * features : 3 * features, :]
    ).astype(BF16)
    if used < lanes_all:
        product_ref[used:, :] = jnp.zeros((lanes_all - used, features), BF16)
    incoming = jnp.zeros((node_count, features), F32)
    for at in range(0, own_ref.shape[0], TILE):
        rows = slice(at, at + TILE)
        edge_bf = edge_ref[rows, :]
        index = index_ref[rows, :]
        lanes = lax.broadcasted_iota(jnp.int32, (TILE, lanes_all), 1)
        hot = (lanes == index[:, 0:1]) | (lanes == index[:, 1:2])
        pre = dot(edge_bf, first_ref[0:features, :]) + dot(
            jnp.where(hot, 1.0, 0.0).astype(BF16), product_ref[...]
        )
        norm = normalize(dot(silu(pre).astype(BF16), second_ref[...]))
        edge_new = (edge_bf.astype(F32) + norm).astype(BF16)
        if full_out is not None:
            full_out[rows, :] = edge_new
        own_out[rows, :] = own_ref[rows, :] + own_columns(norm, spot_ref, part)
        node_ids = lax.broadcasted_iota(jnp.int32, (node_count, TILE), 0)
        incidence = jnp.where(node_ids == receiver_ref[:, rows], 1.0, 0.0).astype(BF16)
        incoming = incoming + dot(incidence, edge_new)
    return incoming.astype(BF16)


def first_edge_kernel(halves, spot_ref, *refs):
    refs = list(refs)
    own_w, core_w = refs.pop(0), refs.pop(0)
    x_pair = [refs.pop(0) for _ in range(halves)]
    d_pair = [refs.pop(0) for _ in range(halves)]
    shards = [refs.pop(0) for _ in range(4)]
    own_ref, index_ref, receiver_ref = [refs.pop(0) for _ in range(3)]
    own_out, incoming_out, full_out, node_out = [refs.pop(0) for _ in range(4)]
    w_ref, second_ref, product_ref, x_ref, sems = refs
    hidden, features = second_ref.shape
    part = own_ref.shape[1]
    edge_count = own_ref.shape[0]
    node_count = node_out.shape[0]
    copies = Copies(sems)
    load_first_weights(copies, spot_ref, own_w, core_w, x_pair, d_pair, w_ref, second_ref)
    for j, shard in enumerate(shards):
        column = pl.multiple_of((spot_ref[0] ^ j) * part, part)
        copies.start(shard, x_ref.at[:, pl.ds(column, part)])
    copies.wait()
    first_rows = 3 * features
    for j in range(4):
        for q in range(features // part):
            second_ref[j * part : (j + 1) * part, q * part : (q + 1) * part] = w_ref[
                first_rows + q * part : first_rows + (q + 1) * part, j * part : (j + 1) * part
            ]
    nodes = x_ref[edge_count : edge_count + node_count, :]
    node_out[...] = nodes
    incoming_out[...] = edge_rows(
        spot_ref, x_ref, x_ref[edge_count:, :], nodes, own_ref, index_ref, receiver_ref,
        w_ref, second_ref, product_ref, own_out, full_out,
    )


def late_edge_kernel(last, pieces, base, spot_ref, *refs):
    refs = list(refs)
    shards = [(refs.pop(0),) for _ in range(4)]
    edge_ref, own_ref = refs.pop(0), refs.pop(0)
    tables = [refs.pop(0) for _ in range(pieces)]
    index_ref, receiver_ref = refs.pop(0), refs.pop(0)
    own_out, incoming_out = refs.pop(0), refs.pop(0)
    full_out = None if last else refs.pop(0)
    first_ref, second_ref, product_ref, table_ref, sems = refs
    copies = Copies(sems)
    load_weights(copies, shards, base, first_ref, second_ref, None)
    start = 0
    for table in tables:
        table_ref[start : start + table.shape[0], :] = table[...]
        start += table.shape[0]
    copies.wait()
    incoming_out[...] = edge_rows(
        spot_ref, edge_ref, table_ref[...], tables[0][...], own_ref, index_ref, receiver_ref,
        first_ref, second_ref, product_ref, own_out, full_out,
    )


def node_kernel(last, base, spot_ref, *refs):
    refs = list(refs)
    shards = [(refs.pop(0),) for _ in range(4)]
    node_ref, own_ref, incoming_ref = [refs.pop(0) for _ in range(3)]
    wanted_ref = None if last else refs.pop(0)
    own_out = refs.pop(0)
    outs = [] if last else [refs.pop(0) for _ in range(4)]
    first_ref, second_ref, sems = refs
    features = second_ref.shape[1]
    copies = Copies(sems)
    load_weights(copies, shards, base, first_ref, second_ref, None)
    copies.wait()
    node_bf = node_ref[...]
    pre = dot(node_bf, first_ref[0:features, :]) + dot(incoming_ref[...], first_ref[features:, :])
    norm = normalize(dot(silu(pre).astype(BF16), second_ref[...]))
    own_out[...] = own_ref[...] + own_columns(norm, spot_ref, own_ref.shape[1])
    if not last:
        node_new = (node_bf.astype(F32) + norm).astype(BF16)
        outs[0][...] = node_new
        pick_rows(wanted_ref, node_new, outs[1:])


SMEM, VMEM, ANY = "smem", "vmem", "any"
SPACES = {SMEM: pltpu.SMEM, VMEM: pltpu.VMEM, ANY: pl.ANY}


def call(kernel, out_shape, args, scratch, flops, name, out_space=VMEM):
    arrays = [a for _, a in args]
    moved = sum(a.size * a.dtype.itemsize for a in arrays + list(out_shape))
    return pl.pallas_call(
        kernel,
        out_shape=out_shape,
        in_specs=[pl.BlockSpec(memory_space=SPACES[s]) for s, _ in args],
        out_specs=[pl.BlockSpec(memory_space=SPACES[out_space])] * len(out_shape),
        scratch_shapes=scratch,
        compiler_params=pltpu.CompilerParams(vmem_limit_bytes=40 * 1024 * 1024),
        cost_estimate=pl.CostEstimate(flops=flops, bytes_accessed=moved, transcendentals=0),
        name=name,
    )(*arrays)


def swap(x, mask):
    size = lax.axis_size("mp")
    return lax.ppermute(x, "mp", [(i, i ^ mask) for i in range(size)])


def shift(x, by):
    size = lax.axis_size("graph")
    return lax.ppermute(x, "graph", [(i, (i + by) % size) for i in range(size)])


def after(x, *others):
    return lax.optimization_barrier((x, *others))[0]


def neighbour_rows(right, left, coarse, halo):
    if lax.axis_size("graph") == 4:
        return [shift(right, 1), shift(left, -1), shift(coarse, 2)]
    everyone = lax.all_gather(coarse, "graph", axis=0, tiled=True)
    return [shift(right[:halo], 1), shift(left[:halo], -1), everyone]


def table_index(senders, node_count, halo):
    size = lax.axis_size("graph")
    coarse_start = node_count + 2 * halo
    number = jnp.maximum(senders - coarse_start, 0)
    block, row = number // COARSE_DEV, number % COARSE_DEV
    if size != 4:
        return jnp.where(senders < coarse_start, senders, coarse_start + block * COARSE_PAD + row)
    wide = halo + COARSE_PAD
    away = (block - lax.axis_index("graph")) % size
    starts = (node_count - COARSE_DEV, node_count + wide + halo, node_count + 2 * wide, node_count + halo)
    base = jnp.where(
        away < 2,
        jnp.where(away == 0, starts[0], starts[1]),
        jnp.where(away == 2, starts[2], starts[3]),
    )
    fine = jnp.where(senders < node_count + halo, senders, senders + COARSE_PAD)
    return jnp.where(senders < coarse_start, fine, base + row)


def on_device(
    node_state,
    edge_state,
    edge_first,
    edge_second,
    node_first,
    node_second,
    senders,
    receivers,
    boundary_rows,
):
    node_count, part = node_state.shape
    edge_count = edge_state.shape[0]
    features = edge_second.shape[2]
    hidden = 4 * part
    halo = boundary_rows.shape[0] // 2
    blocks = lax.axis_size("graph")
    split = blocks == 4
    shape = jax.ShapeDtypeStruct
    dma = pltpu.SemaphoreType.DMA
    block = lax.axis_index("graph")
    group = lax.axis_index("groups")
    spot = jnp.stack([lax.axis_index("mp"), group, group * blocks + block]).astype(jnp.int32)

    own_coarse = jnp.arange(node_count - COARSE_DEV, node_count, dtype=jnp.int32)
    padding = jnp.full((COARSE_PAD - COARSE_DEV,), -1, jnp.int32)
    coarse_list = jnp.concatenate([own_coarse, padding])
    wanted = jnp.concatenate(
        [boundary_rows[halo:], coarse_list, boundary_rows[:halo], coarse_list, coarse_list]
    )[:, None]
    wide = halo + COARSE_PAD

    def sent(width):
        return [shape((n, width), BF16) for n in (wide, wide, COARSE_PAD)]

    edge_bf, node_bf, right, left, coarse = call(
        start_kernel,
        [shape((edge_count, part), BF16), shape((node_count, part), BF16)] + sent(part),
        [(VMEM, edge_state), (VMEM, node_state), (VMEM, wanted)],
        [],
        2 * wanted.shape[0] * node_count * part,
        "boundary_rows",
    )

    edge_pack = edge_first.shape[1] + features
    node_pack = node_first.shape[1] + features
    late_pack = edge_pack + node_pack
    pack_shapes = [shape((n, part), BF16) for n in (edge_pack, node_pack, late_pack)]
    ride_rows = (edge_pack // 2, node_pack // 8, late_pack // 8)
    if split:
        pack_shapes.append(shape((sum(ride_rows), part), BF16))
    packs = call(
        pack_kernel if split else pack_kernel_plain,
        pack_shapes,
        [(SMEM, spot), (ANY, edge_first), (ANY, edge_second), (ANY, node_first), (ANY, node_second)],
        [pltpu.VMEM((edge_pack + node_pack + late_pack, part), BF16), dma((24,))],
        0,
        "packed_weights",
        ANY,
    )
    edge_w, node_w, late_w = packs[:3]
    if split:
        came = swap(packs[3], 2)
        near = came[: ride_rows[0]]
        node_eighth = came[ride_rows[0] : ride_rows[0] + ride_rows[1]]
        late_eighth = came[ride_rows[0] + ride_rows[1] :]
    halo_rows = neighbour_rows(right, left, coarse, halo)
    latents = jnp.concatenate([edge_bf, node_bf] + halo_rows, axis=0)
    table_rows = latents.shape[0] - edge_count
    if split:
        far_latents = swap(after(latents, came), 2)
        far = lax.ppermute(near, "groups", [(0, 1), (1, 0)])
        x_pair, d_pair = [near, far], [swap(near, 1), swap(far, 1)]
        node_x = lax.all_gather(node_eighth, ("groups", "graph"), axis=0, tiled=True)
        late_x = lax.all_gather(late_eighth, ("groups", "graph"), axis=0, tiled=True)
    else:
        far_latents = swap(latents, 2)
        x_pair = [swap(edge_w, 2)]
        d_pair = [swap(x_pair[0], 1)]
        node_x, late_x = swap(node_w, 2), swap(late_w, 2)
    shards = [latents, swap(latents, 1), far_latents, swap(far_latents, 1)]
    node_ws = [node_w, swap(node_w, 1), node_x, swap(node_x, 1)]
    late_ws = [late_w, swap(late_w, 1), late_x, swap(late_x, 1)]

    index = jnp.stack([table_index(senders, node_count, halo), receivers + table_rows], axis=1)
    receiver_row = receivers[None, :]
    lanes = -(-(table_rows + node_count) // 128) * 128
    edge_flops = 2 * edge_count * features * (2 * features + lanes + node_count)
    node_flops = 2 * node_count * features * 3 * features
    full_edge = shape((edge_count, features), BF16)
    full_node = shape((node_count, features), BF16)
    own_edge = shape((edge_count, part), F32)
    own_node = shape((node_count, part), F32)

    edge_own, incoming, edge_full, node_full = call(
        functools.partial(first_edge_kernel, len(x_pair)),
        [own_edge, full_node, full_edge, full_node],
        [(SMEM, spot), (ANY, edge_w), (ANY, swap(edge_w, 1))]
        + [(ANY, w) for w in x_pair + d_pair]
        + [(ANY, s) for s in shards]
        + [(VMEM, edge_state), (VMEM, index), (VMEM, receiver_row)],
        [
            pltpu.VMEM((edge_pack, hidden), BF16),
            pltpu.VMEM((hidden, features), BF16),
            pltpu.VMEM((lanes, hidden), BF16),
            pltpu.VMEM((edge_count + table_rows, features), BF16),
            dma((10,)),
        ],
        edge_flops,
        "edge_layer",
    )
    node_scratch = [
        pltpu.VMEM((node_first.shape[1], hidden), BF16),
        pltpu.VMEM((hidden, features), BF16),
        dma((20,)),
    ]
    node_own, node_full, right, left, coarse = call(
        functools.partial(node_kernel, False, 0),
        [own_node, full_node] + sent(features),
        [(SMEM, spot)]
        + [(ANY, w) for w in node_ws]
        + [(VMEM, node_full), (VMEM, node_state), (VMEM, incoming), (VMEM, wanted)],
        node_scratch,
        node_flops,
        "node_layer",
    )
    tables = [node_full] + neighbour_rows(right, left, coarse, halo)
    edge_own, incoming = call(
        functools.partial(late_edge_kernel, True, len(tables), 0),
        [own_edge, full_node],
        [(SMEM, spot)]
        + [(ANY, w) for w in late_ws]
        + [(VMEM, edge_full), (VMEM, edge_own)]
        + [(VMEM, t) for t in tables]
        + [(VMEM, index), (VMEM, receiver_row)],
        [
            pltpu.VMEM((edge_first.shape[1], hidden), BF16),
            pltpu.VMEM((hidden, features), BF16),
            pltpu.VMEM((lanes, hidden), BF16),
            pltpu.VMEM((table_rows, features), BF16),
            dma((20,)),
        ],
        edge_flops,
        "edge_layer",
    )
    (node_own,) = call(
        functools.partial(node_kernel, True, edge_pack),
        [own_node],
        [(SMEM, spot)]
        + [(ANY, w) for w in late_ws]
        + [(VMEM, node_full), (VMEM, node_own), (VMEM, incoming)],
        node_scratch,
        node_flops,
        "node_layer",
    )
    return (node_own, edge_own)


def solution(mesh):
    in_specs = (
        P(("groups", "graph"), "mp"),
        P(("groups", "graph"), "mp"),
        P(None, None, "mp"),
        P(None, "mp", None),
        P(None, None, "mp"),
        P(None, "mp", None),
        P("graph"),
        P("graph"),
        P("graph"),
    )
    out_specs = (P(("groups", "graph"), "mp"), P(("groups", "graph"), "mp"))
    return jax.shard_map(
        on_device, mesh=mesh, in_specs=in_specs, out_specs=out_specs, check_vma=False
    )
```

```python
import functools

import jax
import jax.numpy as jnp
from jax import lax
from jax.experimental import pallas as pl
from jax.experimental.pallas import tpu as pltpu
from jax.sharding import PartitionSpec as P

COARSE_DEV = 12
COARSE_PAD = 16
EPS = 1e-05
TILE = 256
F32 = jnp.float32
BF16 = jnp.bfloat16


def silu(x):
    half = 0.5 * x
    return half + half * jnp.tanh(half)


def normalize(msg):
    width = msg.shape[1]
    mean = jnp.sum(msg, axis=1, keepdims=True) * (1.0 / width)
    square = jnp.sum(msg * msg, axis=1, keepdims=True) * (1.0 / width)
    return (msg - mean) * lax.rsqrt(square - mean * mean + EPS)


def dot(a, b):
    return jnp.dot(a, b, preferred_element_type=F32)


def own_columns(full, spot_ref, part):
    mine = spot_ref[0]
    out = full[:, 0:part]
    for j in range(1, full.shape[1] // part):
        out = jnp.where(mine == j, full[:, j * part : (j + 1) * part], out)
    return out


class Copies:
    def __init__(self, sems):
        self.sems, self.started = sems, []

    def start(self, source, target):
        copy = pltpu.make_async_copy(source, target, self.sems.at[len(self.started)])
        copy.start()
        self.started.append(copy)

    def wait(self):
        for copy in self.started:
            copy.wait()


def load_shard(copies, layer, first, second, j, first_ref, second_ref):
    part = second.shape[1]
    copies.start(first.at[layer], first_ref.at[:, pl.ds(j * part, part)])
    copies.start(second.at[layer], second_ref.at[pl.ds(j * part, part)])


def load_packed(copies, packed, j, first_ref, second_ref):
    rows = first_ref.shape[0]
    hidden, features = second_ref.shape
    part = hidden // 4
    copies.start(packed.at[pl.ds(0, rows)], first_ref.at[:, pl.ds(j * part, part)])
    for q in range(features // part):
        copies.start(
            packed.at[pl.ds(rows + q * part, part)],
            second_ref.at[pl.ds(j * part, part), pl.ds(q * part, part)],
        )


def load_half(copies, packed, base, half, j, first_ref, second_ref):
    rows = first_ref.shape[0] // 2
    hidden, features = second_ref.shape
    part = hidden // 4
    deep = part // 2
    at = pl.multiple_of(half * rows, rows)
    copies.start(packed.at[pl.ds(base, rows)], first_ref.at[pl.ds(at, rows), pl.ds(j * part, part)])
    at = pl.multiple_of(j * part + half * deep, deep)
    for q in range(features // part):
        copies.start(
            packed.at[pl.ds(base + rows + q * deep, deep)],
            second_ref.at[pl.ds(at, deep), pl.ds(q * part, part)],
        )
    return base + rows + features // part * deep


def ride_kernel(spot_ref, ef, es, nf, ns, ride_out, sems):
    y = spot_ref[1]
    part, features = es.shape[1:]
    copies = Copies(sems)
    at = 0
    for first, second in ((ef, es), (nf, ns)):
        rows = first.shape[1] // 2
        source = first.at[0, pl.ds(pl.multiple_of(y * rows, rows), rows)]
        copies.start(source, ride_out.at[pl.ds(at, rows)])
        at += rows
        deep = part // 2
        for q in range(features // part):
            source = second.at[0, pl.ds(pl.multiple_of(y * deep, deep), deep), pl.ds(q * part, part)]
            copies.start(source, ride_out.at[pl.ds(at, deep)])
            at += deep
    copies.wait()


def pack_kernel(ef, es, nf, ns, edge_out, node_out, sems):
    part, features = es.shape[1:]
    copies = Copies(sems)
    for first, second, out in ((ef, es, edge_out), (nf, ns, node_out)):
        rows = first.shape[1]
        copies.start(first.at[1], out.at[pl.ds(0, rows)])
        for q in range(features // part):
            copies.start(second.at[1, :, pl.ds(q * part, part)], out.at[pl.ds(rows + q * part, part)])
    copies.wait()


def pick_rows(wanted_ref, node_bf, outs):
    wanted = wanted_ref[...]
    lanes = lax.broadcasted_iota(jnp.int32, (wanted.shape[0], node_bf.shape[0]), 1)
    picked = dot(jnp.where(lanes == wanted, 1.0, 0.0).astype(BF16), node_bf).astype(BF16)
    start = 0
    for out in outs:
        out[...] = picked[start : start + out.shape[0]]
        start += out.shape[0]


def start_kernel(node_ref, wanted_ref, node_out, right, left, coarse):
    node_bf = node_ref[...].astype(BF16)
    node_out[...] = node_bf
    pick_rows(wanted_ref, node_bf, (right, left, coarse))


def latent_kernel(edge_ref, *refs):
    rows, out = refs[:-1], refs[-1]
    at = edge_ref.shape[0]
    out[0:at, :] = edge_ref[...].astype(BF16)
    for piece in rows:
        out[at : at + piece.shape[0], :] = piece[...]
        at += piece.shape[0]


def edge_rows(spot_ref, edge_ref, table, nodes, own_ref, index_ref, receiver_ref, first_ref, second_ref, product_ref, own_out, full_out):
    features = second_ref.shape[1]
    node_count = nodes.shape[0]
    table_rows = table.shape[0]
    lanes_all = product_ref.shape[0]
    used = table_rows + node_count
    part = own_ref.shape[1]
    product_ref[0:table_rows, :] = dot(table, first_ref[features : 2 * features, :]).astype(BF16)
    product_ref[table_rows:used, :] = dot(
        nodes, first_ref[2 * features : 3 * features, :]
    ).astype(BF16)
    if used < lanes_all:
        product_ref[used:, :] = jnp.zeros((lanes_all - used, features), BF16)
    incoming = jnp.zeros((node_count, features), F32)
    for at in range(0, own_ref.shape[0], TILE):
        rows = slice(at, at + TILE)
        edge_bf = edge_ref[rows, :]
        index = index_ref[rows, :]
        lanes = lax.broadcasted_iota(jnp.int32, (TILE, lanes_all), 1)
        hot = (lanes == index[:, 0:1]) | (lanes == index[:, 1:2])
        pre = dot(edge_bf, first_ref[0:features, :]) + dot(
            jnp.where(hot, 1.0, 0.0).astype(BF16), product_ref[...]
        )
        norm = normalize(dot(silu(pre).astype(BF16), second_ref[...]))
        edge_new = (edge_bf.astype(F32) + norm).astype(BF16)
        if full_out is not None:
            full_out[rows, :] = edge_new
        own_out[rows, :] = own_ref[rows, :] + own_columns(norm, spot_ref, part)
        node_ids = lax.broadcasted_iota(jnp.int32, (node_count, TILE), 0)
        incidence = jnp.where(node_ids == receiver_ref[:, rows], 1.0, 0.0).astype(BF16)
        incoming = incoming + dot(incidence, edge_new)
    return incoming.astype(BF16)


def node_rows(spot_ref, node_bf, incoming, own_ref, first_ref, second_ref, own_out):
    features = second_ref.shape[1]
    pre = dot(node_bf, first_ref[0:features, :]) + dot(incoming, first_ref[features:, :])
    norm = normalize(dot(silu(pre).astype(BF16), second_ref[...]))
    own_out[...] = own_ref[...] + own_columns(norm, spot_ref, own_ref.shape[1])
    return (node_bf.astype(F32) + norm).astype(BF16)


def first_kernel(spot_ref, *refs):
    refs = list(refs)
    own_w = [refs.pop(0) for _ in range(4)]
    core_w = [refs.pop(0) for _ in range(4)]
    halves = [[refs.pop(0) for _ in range(2)] for _ in range(2)]
    shards = [refs.pop(0) for _ in range(4)]
    edge_own, node_own, index_ref, receiver_ref, wanted_ref = [refs.pop(0) for _ in range(5)]
    edge_out, full_out, node_out, node_full = [refs.pop(0) for _ in range(4)]
    sends = [refs.pop(0) for _ in range(3)]
    edge_w, edge_w2, node_w, node_w2, product_ref, x_ref, edge_sems, node_sems = refs
    part = edge_own.shape[1]
    edge_count = edge_own.shape[0]
    node_count = node_own.shape[0]
    edge_copies, node_copies = Copies(edge_sems), Copies(node_sems)
    for j, shard in enumerate(shards):
        column = pl.multiple_of((spot_ref[0] ^ j) * part, part)
        edge_copies.start(shard, x_ref.at[:, pl.ds(column, part)])
    y = spot_ref[1]
    starts = [0, 0]
    for base, copies, (first, second), at in (
        (0, edge_copies, (edge_w, edge_w2), 0),
        (1, node_copies, (node_w, node_w2), 2),
    ):
        load_shard(copies, 0, own_w[at], own_w[at + 1], 0, first, second)
        load_shard(copies, 0, core_w[at], core_w[at + 1], 1, first, second)
        for j, pair in enumerate(halves):
            for k, piece in enumerate(pair):
                half = y if k == 0 else 1 - y
                end = load_half(copies, piece, starts[base], half, 2 + j, first, second)
        starts[1] = end
    edge_copies.wait()
    nodes = x_ref[edge_count : edge_count + node_count, :]
    incoming = edge_rows(
        spot_ref, x_ref, x_ref[edge_count:, :], nodes, edge_own, index_ref, receiver_ref,
        edge_w, edge_w2, product_ref, edge_out, full_out,
    )
    node_copies.wait()
    node_new = node_rows(spot_ref, nodes, incoming, node_own, node_w, node_w2, node_out)
    node_full[...] = node_new
    pick_rows(wanted_ref, node_new, sends)


def late_weights(copies, refs, first, second):
    load_shard(copies, 1, refs[0], refs[1], 0, first, second)
    load_shard(copies, 1, refs[2], refs[3], 1, first, second)
    load_packed(copies, refs[4], 2, first, second)
    load_packed(copies, refs[5], 3, first, second)


def late_edge_kernel(pieces, spot_ref, *refs):
    refs = list(refs)
    weights = [refs.pop(0) for _ in range(6)]
    edge_ref, own_ref = refs.pop(0), refs.pop(0)
    tables = [refs.pop(0) for _ in range(pieces)]
    index_ref, receiver_ref = refs.pop(0), refs.pop(0)
    own_out, incoming_out = refs.pop(0), refs.pop(0)
    first_ref, second_ref, product_ref, table_ref, sems = refs
    copies = Copies(sems)
    late_weights(copies, weights, first_ref, second_ref)
    start = 0
    for table in tables:
        table_ref[start : start + table.shape[0], :] = table[...]
        start += table.shape[0]
    copies.wait()
    incoming_out[...] = edge_rows(
        spot_ref, edge_ref, table_ref[...], tables[0][...], own_ref, index_ref, receiver_ref,
        first_ref, second_ref, product_ref, own_out, None,
    )


def late_node_kernel(spot_ref, *refs):
    refs = list(refs)
    weights = [refs.pop(0) for _ in range(6)]
    node_ref, own_ref, incoming_ref, own_out, first_ref, second_ref, sems = refs
    copies = Copies(sems)
    late_weights(copies, weights, first_ref, second_ref)
    copies.wait()
    node_rows(spot_ref, node_ref[...], incoming_ref[...], own_ref, first_ref, second_ref, own_out)


SMEM, VMEM, HBM = pltpu.SMEM, pltpu.VMEM, pltpu.HBM


def call(kernel, out_shape, args, scratch, flops, name, out_space=VMEM):
    arrays = [a for _, a in args]
    moved = sum(a.size * a.dtype.itemsize for a in arrays + list(out_shape))
    return pl.pallas_call(
        kernel,
        out_shape=out_shape,
        in_specs=[pl.BlockSpec(memory_space=s) for s, _ in args],
        out_specs=[pl.BlockSpec(memory_space=out_space)] * len(out_shape),
        scratch_shapes=scratch,
        compiler_params=pltpu.CompilerParams(vmem_limit_bytes=40 * 1024 * 1024),
        cost_estimate=pl.CostEstimate(flops=flops, bytes_accessed=moved, transcendentals=0),
        name=name,
    )(*arrays)


def swap(x, mask):
    size = lax.axis_size("mp")
    return lax.ppermute(x, "mp", [(i, i ^ mask) for i in range(size)])


def shift(x, by):
    size = lax.axis_size("graph")
    return lax.ppermute(x, "graph", [(i, (i + by) % size) for i in range(size)])


def after(x, *others):
    return lax.optimization_barrier((x, *others))[0]


def neighbour_rows(right, left, coarse, halo):
    if lax.axis_size("graph") == 4:
        return [shift(right, 1), shift(left, -1), shift(coarse, 2)]
    everyone = lax.all_gather(coarse, "graph", axis=0, tiled=True)
    return [shift(right[:halo], 1), shift(left[:halo], -1), everyone]


def table_index(senders, node_count, halo):
    size = lax.axis_size("graph")
    coarse_start = node_count + 2 * halo
    number = jnp.maximum(senders - coarse_start, 0)
    block, row = number // COARSE_DEV, number % COARSE_DEV
    if size != 4:
        return jnp.where(senders < coarse_start, senders, coarse_start + block * COARSE_PAD + row)
    wide = halo + COARSE_PAD
    away = (block - lax.axis_index("graph")) % size
    starts = (node_count - COARSE_DEV, node_count + wide + halo, node_count + 2 * wide, node_count + halo)
    base = jnp.where(
        away < 2,
        jnp.where(away == 0, starts[0], starts[1]),
        jnp.where(away == 2, starts[2], starts[3]),
    )
    fine = jnp.where(senders < node_count + halo, senders, senders + COARSE_PAD)
    return jnp.where(senders < coarse_start, fine, base + row)


def on_device(
    node_state,
    edge_state,
    edge_first,
    edge_second,
    node_first,
    node_second,
    senders,
    receivers,
    boundary_rows,
):
    node_count, part = node_state.shape
    edge_count = edge_state.shape[0]
    features = edge_second.shape[2]
    hidden = 4 * part
    halo = boundary_rows.shape[0] // 2
    blocks = lax.axis_size("graph")
    shape = jax.ShapeDtypeStruct
    dma = pltpu.SemaphoreType.DMA
    block = lax.axis_index("graph")
    group = lax.axis_index("groups")
    spot = jnp.stack([lax.axis_index("mp"), group, group * blocks + block]).astype(jnp.int32)

    own_coarse = jnp.arange(node_count - COARSE_DEV, node_count, dtype=jnp.int32)
    padding = jnp.full((COARSE_PAD - COARSE_DEV,), -1, jnp.int32)
    coarse_list = jnp.concatenate([own_coarse, padding])
    wanted = jnp.concatenate(
        [boundary_rows[halo:], coarse_list, boundary_rows[:halo], coarse_list, coarse_list]
    )[:, None]
    wide = halo + COARSE_PAD

    def sent(width):
        return [shape((n, width), BF16) for n in (wide, wide, COARSE_PAD)]

    weights = (edge_first, edge_second, node_first, node_second)
    edge_pack = edge_first.shape[1] + features
    node_pack = node_first.shape[1] + features
    (ride,) = call(
        ride_kernel,
        [shape(((edge_pack + node_pack) // 2, part), BF16)],
        [(SMEM, spot)] + [(HBM, w) for w in weights],
        [dma((10,))],
        0,
        "layer_0_half",
        HBM,
    )
    near = swap(ride, 2)
    node_bf, right, left, coarse = call(
        start_kernel,
        [shape((node_count, part), BF16)] + sent(part),
        [(VMEM, after(node_state, ride)), (VMEM, wanted)],
        [],
        2 * wanted.shape[0] * node_count * part,
        "boundary_rows",
    )
    halo_rows = neighbour_rows(right, left, coarse, halo)
    edge_late, node_late = call(
        pack_kernel,
        [shape((edge_pack, part), BF16), shape((node_pack, part), BF16)],
        [(HBM, after(weights[0], right))] + [(HBM, w) for w in weights[1:]],
        [dma((10,))],
        0,
        "layer_1_packed",
        HBM,
    )
    core_w = [swap(after(w, right), 1) for w in weights]
    table_rows = node_count + sum(r.shape[0] for r in halo_rows)
    (latents,) = call(
        latent_kernel,
        [shape((edge_count + table_rows, part), BF16)],
        [(VMEM, edge_state), (VMEM, node_bf)] + [(VMEM, r) for r in halo_rows],
        [],
        0,
        "latents",
    )
    far_latents = swap(after(latents, near), 2)
    shards = [latents, swap(latents, 1), far_latents, swap(far_latents, 1)]
    far = lax.ppermute(near, "groups", [(0, 1), (1, 0)])
    pairs = [near, far, swap(near, 1), swap(far, 1)]
    edge_late_x = swap(after(edge_late, far_latents), 2)

    index = jnp.stack([table_index(senders, node_count, halo), receivers + table_rows], axis=1)
    receiver_row = receivers[None, :]
    lanes = -(-(table_rows + node_count) // 128) * 128
    edge_flops = 2 * edge_count * features * (2 * features + lanes + node_count)
    node_flops = 2 * node_count * features * 3 * features
    full_edge = shape((edge_count, features), BF16)
    full_node = shape((node_count, features), BF16)
    own_edge = shape((edge_count, part), F32)
    own_node = shape((node_count, part), F32)
    second_shape = pltpu.VMEM((hidden, features), BF16)
    edge_shape = pltpu.VMEM((edge_first.shape[1], hidden), BF16)
    node_shape = pltpu.VMEM((node_first.shape[1], hidden), BF16)

    edge_own, edge_full, node_own, node_full, right, left, coarse = call(
        first_kernel,
        [own_edge, full_edge, own_node, full_node] + sent(features),
        [(SMEM, spot)]
        + [(HBM, w) for w in list(weights) + core_w + pairs + shards]
        + [(VMEM, a) for a in (edge_state, node_state, index, receiver_row, wanted)],
        [
            edge_shape,
            second_shape,
            node_shape,
            second_shape,
            pltpu.VMEM((lanes, hidden), BF16),
            pltpu.VMEM((edge_count + table_rows, features), BF16),
            dma((28,)),
            dma((24,)),
        ],
        edge_flops + node_flops,
        "layer_0",
    )
    edge_late_d = swap(after(edge_late_x, right), 1)
    node_late_x = swap(after(node_late, edge_late_x, right), 2)
    node_late_d = swap(node_late_x, 1)
    tables = [node_full] + neighbour_rows(right, left, coarse, halo)
    edge_own, incoming = call(
        functools.partial(late_edge_kernel, len(tables)),
        [own_edge, full_node],
        [(SMEM, spot)]
        + [(HBM, w) for w in (*weights[:2], *core_w[:2], edge_late_x, edge_late_d)]
        + [(VMEM, edge_full), (VMEM, edge_own)]
        + [(VMEM, t) for t in tables]
        + [(VMEM, index), (VMEM, receiver_row)],
        [
            edge_shape,
            second_shape,
            pltpu.VMEM((lanes, hidden), BF16),
            pltpu.VMEM((table_rows, features), BF16),
            dma((14,)),
        ],
        edge_flops,
        "layer_1_edges",
    )
    (node_own,) = call(
        late_node_kernel,
        [own_node],
        [(SMEM, spot)]
        + [(HBM, w) for w in (*weights[2:], *core_w[2:], node_late_x, node_late_d)]
        + [(VMEM, node_full), (VMEM, node_own), (VMEM, incoming)],
        [node_shape, second_shape, dma((14,))],
        node_flops,
        "layer_1_nodes",
    )
    return (node_own, edge_own)


def solution(mesh):
    in_specs = (
        P(("groups", "graph"), "mp"),
        P(("groups", "graph"), "mp"),
        P(None, None, "mp"),
        P(None, "mp", None),
        P(None, None, "mp"),
        P(None, "mp", None),
        P("graph"),
        P("graph"),
        P("graph"),
    )
    out_specs = (P(("groups", "graph"), "mp"), P(("groups", "graph"), "mp"))
    return jax.shard_map(
        on_device, mesh=mesh, in_specs=in_specs, out_specs=out_specs, check_vma=False
    )
```

```python
import functools

import jax
import jax.numpy as jnp
from jax import lax
from jax.experimental import pallas as pl
from jax.experimental.pallas import tpu as pltpu
from jax.sharding import PartitionSpec as P

COARSE_DEV = 12
COARSE_PAD = 16
EPS = 1e-05
TILE = 256
F32 = jnp.float32
BF16 = jnp.bfloat16


def silu(x):
    half = 0.5 * x
    return half + half * jnp.tanh(half)


def normalize(msg):
    width = msg.shape[1]
    mean = jnp.sum(msg, axis=1, keepdims=True) * (1.0 / width)
    square = jnp.sum(msg * msg, axis=1, keepdims=True) * (1.0 / width)
    return (msg - mean) * lax.rsqrt(square - mean * mean + EPS)


def dot(a, b):
    return jnp.dot(a, b, preferred_element_type=F32)


def own_columns(full, spot_ref, part):
    mine = spot_ref[0]
    out = full[:, 0:part]
    for j in range(1, full.shape[1] // part):
        out = jnp.where(mine == j, full[:, j * part : (j + 1) * part], out)
    return out


class Copies:
    def __init__(self, sems):
        self.sems, self.started = sems, []

    def start(self, source, target):
        copy = pltpu.make_async_copy(source, target, self.sems.at[len(self.started)])
        copy.start()
        self.started.append(copy)

    def wait(self):
        for copy in self.started:
            copy.wait()


def load_shard(copies, layer, first, second, j, first_ref, second_ref):
    part = second.shape[1]
    copies.start(first.at[layer], first_ref.at[:, pl.ds(j * part, part)])
    copies.start(second.at[layer], second_ref.at[pl.ds(j * part, part)])


def load_packed(copies, packed, base, j, first_ref, second_ref):
    rows = first_ref.shape[0]
    hidden, features = second_ref.shape
    part = hidden // 4
    copies.start(packed.at[pl.ds(base, rows)], first_ref.at[:, pl.ds(j * part, part)])
    for q in range(features // part):
        copies.start(
            packed.at[pl.ds(base + rows + q * part, part)],
            second_ref.at[pl.ds(j * part, part), pl.ds(q * part, part)],
        )


def load_half(copies, packed, base, half, j, first_ref, second_ref):
    rows = first_ref.shape[0] // 2
    hidden, features = second_ref.shape
    part = hidden // 4
    deep = part // 2
    at = pl.multiple_of(half * rows, rows)
    copies.start(packed.at[pl.ds(base, rows)], first_ref.at[pl.ds(at, rows), pl.ds(j * part, part)])
    at = pl.multiple_of(j * part + half * deep, deep)
    for q in range(features // part):
        copies.start(
            packed.at[pl.ds(base + rows + q * deep, deep)],
            second_ref.at[pl.ds(at, deep), pl.ds(q * part, part)],
        )
    return base + rows + features // part * deep


def ride_kernel(spot_ref, ef, es, nf, ns, ride_out, sems):
    y = spot_ref[1]
    part, features = es.shape[1:]
    copies = Copies(sems)
    at = 0
    for first, second in ((ef, es), (nf, ns)):
        rows = first.shape[1] // 2
        source = first.at[0, pl.ds(pl.multiple_of(y * rows, rows), rows)]
        copies.start(source, ride_out.at[pl.ds(at, rows)])
        at += rows
        deep = part // 2
        for q in range(features // part):
            source = second.at[0, pl.ds(pl.multiple_of(y * deep, deep), deep), pl.ds(q * part, part)]
            copies.start(source, ride_out.at[pl.ds(at, deep)])
            at += deep
    copies.wait()


def prepare_kernel(index_ref, receiver_ref, ef, es, nf, ns, hot_out, incidence_out, late_out, sems):
    part, features = es.shape[1:]
    copies = Copies(sems)
    at = 0
    for first, second in ((ef, es), (nf, ns)):
        rows = first.shape[1]
        copies.start(first.at[1], late_out.at[pl.ds(at, rows)])
        at += rows
        for q in range(features // part):
            copies.start(second.at[1, :, pl.ds(q * part, part)], late_out.at[pl.ds(at, part)])
            at += part
    for at in range(0, hot_out.shape[0], TILE):
        rows = slice(at, at + TILE)
        index = index_ref[rows, :]
        lanes = lax.broadcasted_iota(jnp.int32, (TILE, hot_out.shape[1]), 1)
        hot = (lanes == index[:, 0:1]) | (lanes == index[:, 1:2])
        hot_out[rows, :] = jnp.where(hot, 1.0, 0.0).astype(BF16)
        node_ids = lax.broadcasted_iota(jnp.int32, (incidence_out.shape[0], TILE), 0)
        hit = node_ids == receiver_ref[:, rows]
        incidence_out[:, rows] = jnp.where(hit, 1.0, 0.0).astype(BF16)
    copies.wait()


def pick_rows(wanted_ref, node_bf, outs):
    wanted = wanted_ref[...]
    lanes = lax.broadcasted_iota(jnp.int32, (wanted.shape[0], node_bf.shape[0]), 1)
    picked = dot(jnp.where(lanes == wanted, 1.0, 0.0).astype(BF16), node_bf).astype(BF16)
    start = 0
    for out in outs:
        out[...] = picked[start : start + out.shape[0]]
        start += out.shape[0]


def start_kernel(node_ref, wanted_ref, node_out, right, left, coarse):
    node_bf = node_ref[...].astype(BF16)
    node_out[...] = node_bf
    pick_rows(wanted_ref, node_bf, (right, left, coarse))


def latent_kernel(edge_ref, *refs):
    rows, out = refs[:-1], refs[-1]
    at = edge_ref.shape[0]
    out[0:at, :] = edge_ref[...].astype(BF16)
    for piece in rows:
        out[at : at + piece.shape[0], :] = piece[...]
        at += piece.shape[0]


def edge_rows(spot_ref, edge_ref, table, nodes, own_ref, hot_ref, incidence_ref, first_ref, second_ref, product_ref, own_out, full_out):
    features = second_ref.shape[1]
    node_count = nodes.shape[0]
    table_rows = table.shape[0]
    lanes_all = product_ref.shape[0]
    used = table_rows + node_count
    part = own_ref.shape[1]
    product_ref[0:table_rows, :] = dot(table, first_ref[features : 2 * features, :]).astype(BF16)
    product_ref[table_rows:used, :] = dot(
        nodes, first_ref[2 * features : 3 * features, :]
    ).astype(BF16)
    if used < lanes_all:
        product_ref[used:, :] = jnp.zeros((lanes_all - used, features), BF16)
    incoming = jnp.zeros((node_count, features), F32)
    for at in range(0, own_ref.shape[0], TILE):
        rows = slice(at, at + TILE)
        edge_bf = edge_ref[rows, :]
        pre = dot(edge_bf, first_ref[0:features, :]) + dot(hot_ref[rows, :], product_ref[...])
        norm = normalize(dot(silu(pre).astype(BF16), second_ref[...]))
        edge_new = (edge_bf.astype(F32) + norm).astype(BF16)
        if full_out is not None:
            full_out[rows, :] = edge_new
        own_out[rows, :] = own_ref[rows, :] + own_columns(norm, spot_ref, part)
        incoming = incoming + dot(incidence_ref[:, rows], edge_new)
    return incoming.astype(BF16)


def node_rows(spot_ref, node_bf, incoming, own_ref, first_ref, second_ref, own_out):
    features = second_ref.shape[1]
    pre = dot(node_bf, first_ref[0:features, :]) + dot(incoming, first_ref[features:, :])
    norm = normalize(dot(silu(pre).astype(BF16), second_ref[...]))
    own_out[...] = own_ref[...] + own_columns(norm, spot_ref, own_ref.shape[1])
    return (node_bf.astype(F32) + norm).astype(BF16)


def first_kernel(spot_ref, *refs):
    refs = list(refs)
    own_w = [refs.pop(0) for _ in range(4)]
    core_w = [refs.pop(0) for _ in range(4)]
    halves = [[refs.pop(0) for _ in range(2)] for _ in range(2)]
    shards = [refs.pop(0) for _ in range(4)]
    edge_own, node_own, hot_ref, incidence_ref, wanted_ref = [refs.pop(0) for _ in range(5)]
    edge_out, full_out, node_out, node_full = [refs.pop(0) for _ in range(4)]
    sends = [refs.pop(0) for _ in range(3)]
    edge_w, edge_w2, node_w, node_w2, product_ref, x_ref, edge_sems, node_sems = refs
    part = edge_own.shape[1]
    edge_count = edge_own.shape[0]
    node_count = node_own.shape[0]
    edge_copies, node_copies = Copies(edge_sems), Copies(node_sems)
    for j, shard in enumerate(shards):
        column = pl.multiple_of((spot_ref[0] ^ j) * part, part)
        edge_copies.start(shard, x_ref.at[:, pl.ds(column, part)])
    y = spot_ref[1]
    starts = [0, 0]
    for base, copies, (first, second), at in (
        (0, edge_copies, (edge_w, edge_w2), 0),
        (1, node_copies, (node_w, node_w2), 2),
    ):
        load_shard(copies, 0, own_w[at], own_w[at + 1], 0, first, second)
        load_shard(copies, 0, core_w[at], core_w[at + 1], 1, first, second)
        for j, pair in enumerate(halves):
            for k, piece in enumerate(pair):
                half = y if k == 0 else 1 - y
                end = load_half(copies, piece, starts[base], half, 2 + j, first, second)
        starts[1] = end
    edge_copies.wait()
    nodes = x_ref[edge_count : edge_count + node_count, :]
    incoming = edge_rows(
        spot_ref, x_ref, x_ref[edge_count:, :], nodes, edge_own, hot_ref, incidence_ref,
        edge_w, edge_w2, product_ref, edge_out, full_out,
    )
    node_copies.wait()
    node_new = node_rows(spot_ref, nodes, incoming, node_own, node_w, node_w2, node_out)
    node_full[...] = node_new
    pick_rows(wanted_ref, node_new, sends)


def late_kernel(pieces, spot_ref, *refs):
    refs = list(refs)
    own_w = [refs.pop(0) for _ in range(4)]
    core_w = [refs.pop(0) for _ in range(4)]
    packed = [refs.pop(0) for _ in range(2)]
    edge_ref, edge_own, node_own = [refs.pop(0) for _ in range(3)]
    tables = [refs.pop(0) for _ in range(pieces)]
    hot_ref, incidence_ref, edge_out, node_out = [refs.pop(0) for _ in range(4)]
    edge_w, edge_w2, node_w, node_w2, product_ref, table_ref, edge_sems, node_sems = refs
    edge_copies, node_copies = Copies(edge_sems), Copies(node_sems)
    base = 0
    for copies, first, second, at in (
        (edge_copies, edge_w, edge_w2, 0),
        (node_copies, node_w, node_w2, 2),
    ):
        load_shard(copies, 1, own_w[at], own_w[at + 1], 0, first, second)
        load_shard(copies, 1, core_w[at], core_w[at + 1], 1, first, second)
        for j, pack in enumerate(packed):
            load_packed(copies, pack, base, 2 + j, first, second)
        base = edge_w.shape[0] + edge_w2.shape[1]
    start = 0
    for table in tables:
        table_ref[start : start + table.shape[0], :] = table[...]
        start += table.shape[0]
    edge_copies.wait()
    nodes = tables[0][...]
    incoming = edge_rows(
        spot_ref, edge_ref, table_ref[...], nodes, edge_own, hot_ref, incidence_ref,
        edge_w, edge_w2, product_ref, edge_out, None,
    )
    node_copies.wait()
    node_rows(spot_ref, nodes, incoming, node_own, node_w, node_w2, node_out)


SMEM, VMEM, HBM = pltpu.SMEM, pltpu.VMEM, pltpu.HBM


def call(kernel, out_shape, args, scratch, flops, name, out_space=VMEM):
    arrays = [a for _, a in args]
    out_spaces = out_space if isinstance(out_space, list) else [out_space] * len(out_shape)
    moved = sum(a.size * a.dtype.itemsize for a in arrays + list(out_shape))
    return pl.pallas_call(
        kernel,
        out_shape=out_shape,
        in_specs=[pl.BlockSpec(memory_space=s) for s, _ in args],
        out_specs=[pl.BlockSpec(memory_space=s) for s in out_spaces],
        scratch_shapes=scratch,
        compiler_params=pltpu.CompilerParams(vmem_limit_bytes=60 * 1024 * 1024),
        cost_estimate=pl.CostEstimate(flops=flops, bytes_accessed=moved, transcendentals=0),
        name=name,
    )(*arrays)


def swap(x, mask):
    size = lax.axis_size("mp")
    return lax.ppermute(x, "mp", [(i, i ^ mask) for i in range(size)])


def shift(x, by):
    size = lax.axis_size("graph")
    return lax.ppermute(x, "graph", [(i, (i + by) % size) for i in range(size)])


def after(x, *others):
    return lax.optimization_barrier((x, *others))[0]


def neighbour_rows(right, left, coarse, halo):
    if lax.axis_size("graph") == 4:
        return [shift(right, 1), shift(left, -1), shift(coarse, 2)]
    everyone = lax.all_gather(coarse, "graph", axis=0, tiled=True)
    return [shift(right[:halo], 1), shift(left[:halo], -1), everyone]


def table_index(senders, node_count, halo):
    size = lax.axis_size("graph")
    coarse_start = node_count + 2 * halo
    number = jnp.maximum(senders - coarse_start, 0)
    block, row = number // COARSE_DEV, number % COARSE_DEV
    if size != 4:
        return jnp.where(senders < coarse_start, senders, coarse_start + block * COARSE_PAD + row)
    wide = halo + COARSE_PAD
    away = (block - lax.axis_index("graph")) % size
    starts = (node_count - COARSE_DEV, node_count + wide + halo, node_count + 2 * wide, node_count + halo)
    base = jnp.where(
        away < 2,
        jnp.where(away == 0, starts[0], starts[1]),
        jnp.where(away == 2, starts[2], starts[3]),
    )
    fine = jnp.where(senders < node_count + halo, senders, senders + COARSE_PAD)
    return jnp.where(senders < coarse_start, fine, base + row)


def on_device(
    node_state,
    edge_state,
    edge_first,
    edge_second,
    node_first,
    node_second,
    senders,
    receivers,
    boundary_rows,
):
    node_count, part = node_state.shape
    edge_count = edge_state.shape[0]
    features = edge_second.shape[2]
    hidden = 4 * part
    halo = boundary_rows.shape[0] // 2
    blocks = lax.axis_size("graph")
    shape = jax.ShapeDtypeStruct
    dma = pltpu.SemaphoreType.DMA
    block = lax.axis_index("graph")
    group = lax.axis_index("groups")
    spot = jnp.stack([lax.axis_index("mp"), group, group * blocks + block]).astype(jnp.int32)

    own_coarse = jnp.arange(node_count - COARSE_DEV, node_count, dtype=jnp.int32)
    padding = jnp.full((COARSE_PAD - COARSE_DEV,), -1, jnp.int32)
    coarse_list = jnp.concatenate([own_coarse, padding])
    wanted = jnp.concatenate(
        [boundary_rows[halo:], coarse_list, boundary_rows[:halo], coarse_list, coarse_list]
    )[:, None]
    wide = halo + COARSE_PAD

    def sent(width):
        return [shape((n, width), BF16) for n in (wide, wide, COARSE_PAD)]

    weights = (edge_first, edge_second, node_first, node_second)
    edge_pack = edge_first.shape[1] + features
    node_pack = node_first.shape[1] + features
    (ride,) = call(
        ride_kernel,
        [shape(((edge_pack + node_pack) // 2, part), BF16)],
        [(SMEM, spot)] + [(HBM, w) for w in weights],
        [dma((10,))],
        0,
        "layer_0_half",
        HBM,
    )
    near = swap(ride, 2)
    node_bf, right, left, coarse = call(
        start_kernel,
        [shape((node_count, part), BF16)] + sent(part),
        [(VMEM, after(node_state, ride)), (VMEM, wanted)],
        [],
        2 * wanted.shape[0] * node_count * part,
        "boundary_rows",
    )
    halo_rows = neighbour_rows(right, left, coarse, halo)
    table_rows = node_count + sum(r.shape[0] for r in halo_rows)
    lanes = -(-(table_rows + node_count) // 128) * 128
    index = jnp.stack([table_index(senders, node_count, halo), receivers + table_rows], axis=1)
    hot, incidence, late_w = call(
        prepare_kernel,
        [
            shape((edge_count, lanes), BF16),
            shape((node_count, edge_count), BF16),
            shape((edge_pack + node_pack, part), BF16),
        ],
        [(VMEM, after(index, right)), (VMEM, receivers[None, :])] + [(HBM, w) for w in weights],
        [dma((10,))],
        0,
        "one_hot",
        [VMEM, VMEM, HBM],
    )
    core_w = [swap(after(w, right), 1) for w in weights]
    (latents,) = call(
        latent_kernel,
        [shape((edge_count + table_rows, part), BF16)],
        [(VMEM, after(edge_state, late_w)), (VMEM, node_bf)] + [(VMEM, r) for r in halo_rows],
        [],
        0,
        "latents",
    )
    far_latents = swap(after(latents, near, *core_w), 2)
    shards = [latents, swap(latents, 1), far_latents, swap(far_latents, 1)]
    far = lax.ppermute(near, "groups", [(0, 1), (1, 0)])
    pairs = [near, far, swap(near, 1), swap(far, 1)]
    late_x = swap(after(late_w, far_latents), 2)

    edge_flops = 2 * edge_count * features * (2 * features + lanes + node_count)
    node_flops = 2 * node_count * features * 3 * features
    full_edge = shape((edge_count, features), BF16)
    full_node = shape((node_count, features), BF16)
    own_edge = shape((edge_count, part), F32)
    own_node = shape((node_count, part), F32)
    second_shape = pltpu.VMEM((hidden, features), BF16)
    edge_shape = pltpu.VMEM((edge_first.shape[1], hidden), BF16)
    node_shape = pltpu.VMEM((node_first.shape[1], hidden), BF16)

    edge_own, edge_full, node_own, node_full, right, left, coarse = call(
        first_kernel,
        [own_edge, full_edge, own_node, full_node] + sent(features),
        [(SMEM, spot)]
        + [(HBM, w) for w in list(weights) + core_w + pairs + shards]
        + [(VMEM, a) for a in (edge_state, node_state, hot, incidence, wanted)],
        [
            edge_shape,
            second_shape,
            node_shape,
            second_shape,
            pltpu.VMEM((lanes, hidden), BF16),
            pltpu.VMEM((edge_count + table_rows, features), BF16),
            dma((28,)),
            dma((24,)),
        ],
        edge_flops + node_flops,
        "layer_0",
    )
    tables = [node_full] + neighbour_rows(right, left, coarse, halo)
    late_d = swap(after(late_x, tables[1]), 1)
    edge_own, node_own = call(
        functools.partial(late_kernel, len(tables)),
        [own_edge, own_node],
        [(SMEM, spot)]
        + [(HBM, w) for w in list(weights) + core_w + [late_x, late_d]]
        + [(VMEM, a) for a in (edge_full, edge_own, node_own)]
        + [(VMEM, t) for t in tables]
        + [(VMEM, hot), (VMEM, incidence)],
        [
            edge_shape,
            second_shape,
            node_shape,
            second_shape,
            pltpu.VMEM((lanes, hidden), BF16),
            pltpu.VMEM((table_rows, features), BF16),
            dma((14,)),
            dma((14,)),
        ],
        edge_flops + node_flops,
        "layer_1",
    )
    return (node_own, edge_own)


def solution(mesh):
    in_specs = (
        P(("groups", "graph"), "mp"),
        P(("groups", "graph"), "mp"),
        P(None, None, "mp"),
        P(None, "mp", None),
        P(None, None, "mp"),
        P(None, "mp", None),
        P("graph"),
        P("graph"),
        P("graph"),
    )
    out_specs = (P(("groups", "graph"), "mp"), P(("groups", "graph"), "mp"))
    return jax.shard_map(
        on_device, mesh=mesh, in_specs=in_specs, out_specs=out_specs, check_vma=False
    )
```

```python
import functools

import jax
import jax.numpy as jnp
from jax import lax
from jax.experimental import pallas as pl
from jax.experimental.pallas import tpu as pltpu
from jax.sharding import PartitionSpec as P

COARSE_DEV = 12
COARSE_PAD = 16
EPS = 1e-05
TILE = 256
F32 = jnp.float32
BF16 = jnp.bfloat16


def silu(x):
    half = 0.5 * x
    return half + half * jnp.tanh(half)


def normalize(msg):
    width = msg.shape[1]
    mean = jnp.sum(msg, axis=1, keepdims=True) * (1.0 / width)
    square = jnp.sum(msg * msg, axis=1, keepdims=True) * (1.0 / width)
    return (msg - mean) * lax.rsqrt(square - mean * mean + EPS)


def dot(a, b):
    return jnp.dot(a, b, preferred_element_type=F32)


def own_columns(full, spot_ref, part):
    mine = spot_ref[0]
    out = full[:, 0:part]
    for j in range(1, full.shape[1] // part):
        out = jnp.where(mine == j, full[:, j * part : (j + 1) * part], out)
    return out


class Copies:
    def __init__(self, sems):
        self.sems, self.started = sems, []

    def start(self, source, target):
        copy = pltpu.make_async_copy(source, target, self.sems.at[len(self.started)])
        copy.start()
        self.started.append(copy)

    def wait(self):
        for copy in self.started:
            copy.wait()


def load_shard(copies, layer, first, second, j, first_ref, second_ref):
    part = second.shape[1]
    copies.start(first.at[layer], first_ref.at[:, pl.ds(j * part, part)])
    copies.start(second.at[layer], second_ref.at[pl.ds(j * part, part)])


def load_packed(copies, packed, base, j, first_ref, second_ref):
    rows = first_ref.shape[0]
    hidden, features = second_ref.shape
    part = hidden // 4
    copies.start(packed.at[pl.ds(base, rows)], first_ref.at[:, pl.ds(j * part, part)])
    for q in range(features // part):
        copies.start(
            packed.at[pl.ds(base + rows + q * part, part)],
            second_ref.at[pl.ds(j * part, part), pl.ds(q * part, part)],
        )


def load_half(copies, packed, base, half, j, first_ref, second_ref):
    rows = first_ref.shape[0] // 2
    hidden, features = second_ref.shape
    part = hidden // 4
    deep = part // 2
    at = pl.multiple_of(half * rows, rows)
    copies.start(packed.at[pl.ds(base, rows)], first_ref.at[pl.ds(at, rows), pl.ds(j * part, part)])
    at = pl.multiple_of(j * part + half * deep, deep)
    for q in range(features // part):
        copies.start(
            packed.at[pl.ds(base + rows + q * deep, deep)],
            second_ref.at[pl.ds(at, deep), pl.ds(q * part, part)],
        )
    return base + rows + features // part * deep


def ride_kernel(spot_ref, ef, es, nf, ns, ride_out, sems):
    y = spot_ref[1]
    part, features = es.shape[1:]
    copies = Copies(sems)
    at = 0
    for first, second in ((ef, es), (nf, ns)):
        rows = first.shape[1] // 2
        source = first.at[0, pl.ds(pl.multiple_of(y * rows, rows), rows)]
        copies.start(source, ride_out.at[pl.ds(at, rows)])
        at += rows
        deep = part // 2
        for q in range(features // part):
            source = second.at[0, pl.ds(pl.multiple_of(y * deep, deep), deep), pl.ds(q * part, part)]
            copies.start(source, ride_out.at[pl.ds(at, deep)])
            at += deep
    copies.wait()


def prepare_kernel(index_ref, receiver_ref, ef, es, nf, ns, hot_out, incidence_out, late_out, sems):
    part, features = es.shape[1:]
    copies = Copies(sems)
    at = 0
    for first, second in ((ef, es), (nf, ns)):
        rows = first.shape[1]
        copies.start(first.at[1], late_out.at[pl.ds(at, rows)])
        at += rows
        for q in range(features // part):
            copies.start(second.at[1, :, pl.ds(q * part, part)], late_out.at[pl.ds(at, part)])
            at += part
    for at in range(0, hot_out.shape[0], TILE):
        rows = slice(at, at + TILE)
        index = index_ref[rows, :]
        lanes = lax.broadcasted_iota(jnp.int32, (TILE, hot_out.shape[1]), 1)
        hot = (lanes == index[:, 0:1]) | (lanes == index[:, 1:2])
        hot_out[rows, :] = jnp.where(hot, 1.0, 0.0).astype(BF16)
        node_ids = lax.broadcasted_iota(jnp.int32, (incidence_out.shape[0], TILE), 0)
        hit = node_ids == receiver_ref[:, rows]
        incidence_out[:, rows] = jnp.where(hit, 1.0, 0.0).astype(BF16)
    copies.wait()


def pick_rows(wanted_ref, node_bf, outs):
    wanted = wanted_ref[...]
    lanes = lax.broadcasted_iota(jnp.int32, (wanted.shape[0], node_bf.shape[0]), 1)
    picked = dot(jnp.where(lanes == wanted, 1.0, 0.0).astype(BF16), node_bf).astype(BF16)
    start = 0
    for out in outs:
        out[...] = picked[start : start + out.shape[0]]
        start += out.shape[0]


def start_kernel(node_ref, wanted_ref, node_out, right, left, coarse):
    node_bf = node_ref[...].astype(BF16)
    node_out[...] = node_bf
    pick_rows(wanted_ref, node_bf, (right, left, coarse))


def latent_kernel(edge_ref, *refs):
    rows, out = refs[:-1], refs[-1]
    at = edge_ref.shape[0]
    out[0:at, :] = edge_ref[...].astype(BF16)
    for piece in rows:
        out[at : at + piece.shape[0], :] = piece[...]
        at += piece.shape[0]


def edge_rows(spot_ref, edge_ref, table, nodes, own_ref, hot_ref, incidence_ref, first_ref, second_ref, product_ref, own_out, full_out):
    features = second_ref.shape[1]
    node_count = nodes.shape[0]
    table_rows = table.shape[0]
    lanes_all = product_ref.shape[0]
    used = table_rows + node_count
    part = own_ref.shape[1]
    product_ref[0:table_rows, :] = dot(table, first_ref[features : 2 * features, :]).astype(BF16)
    product_ref[table_rows:used, :] = dot(
        nodes, first_ref[2 * features : 3 * features, :]
    ).astype(BF16)
    if used < lanes_all:
        product_ref[used:, :] = jnp.zeros((lanes_all - used, features), BF16)
    incoming = jnp.zeros((node_count, features), F32)
    for at in range(0, own_ref.shape[0], TILE):
        rows = slice(at, at + TILE)
        edge_bf = edge_ref[rows, :]
        pre = dot(edge_bf, first_ref[0:features, :]) + dot(hot_ref[rows, :], product_ref[...])
        norm = normalize(dot(silu(pre).astype(BF16), second_ref[...]))
        edge_new = (edge_bf.astype(F32) + norm).astype(BF16)
        if full_out is not None:
            full_out[rows, :] = edge_new
        own_out[rows, :] = own_ref[rows, :] + own_columns(norm, spot_ref, part)
        incoming = incoming + dot(incidence_ref[:, rows], edge_new)
    return incoming.astype(BF16)


def node_rows(spot_ref, node_bf, incoming, own_ref, first_ref, second_ref, own_out):
    features = second_ref.shape[1]
    pre = dot(node_bf, first_ref[0:features, :]) + dot(incoming, first_ref[features:, :])
    norm = normalize(dot(silu(pre).astype(BF16), second_ref[...]))
    own_out[...] = own_ref[...] + own_columns(norm, spot_ref, own_ref.shape[1])
    return (node_bf.astype(F32) + norm).astype(BF16)


def first_kernel(spot_ref, *refs):
    refs = list(refs)
    own_w = [refs.pop(0) for _ in range(4)]
    core_w = [refs.pop(0) for _ in range(4)]
    halves = [[refs.pop(0) for _ in range(2)] for _ in range(2)]
    shards = [refs.pop(0) for _ in range(4)]
    edge_own, node_own, hot_ref, incidence_ref, wanted_ref = [refs.pop(0) for _ in range(5)]
    edge_out, full_out, node_out, node_full = [refs.pop(0) for _ in range(4)]
    sends = [refs.pop(0) for _ in range(3)]
    edge_w, edge_w2, node_w, node_w2, product_ref, x_ref, edge_sems, node_sems = refs
    part = edge_own.shape[1]
    edge_count = edge_own.shape[0]
    node_count = node_own.shape[0]
    edge_copies, node_copies = Copies(edge_sems), Copies(node_sems)
    for j, shard in enumerate(shards):
        column = pl.multiple_of((spot_ref[0] ^ j) * part, part)
        edge_copies.start(shard, x_ref.at[:, pl.ds(column, part)])
    y = spot_ref[1]
    starts = [0, 0]
    for base, copies, (first, second), at in (
        (0, edge_copies, (edge_w, edge_w2), 0),
        (1, node_copies, (node_w, node_w2), 2),
    ):
        load_shard(copies, 0, own_w[at], own_w[at + 1], 0, first, second)
        load_shard(copies, 0, core_w[at], core_w[at + 1], 1, first, second)
        for j, pair in enumerate(halves):
            for k, piece in enumerate(pair):
                half = y if k == 0 else 1 - y
                end = load_half(copies, piece, starts[base], half, 2 + j, first, second)
        starts[1] = end
    edge_copies.wait()
    nodes = x_ref[edge_count : edge_count + node_count, :]
    incoming = edge_rows(
        spot_ref, x_ref, x_ref[edge_count:, :], nodes, edge_own, hot_ref, incidence_ref,
        edge_w, edge_w2, product_ref, edge_out, full_out,
    )
    node_copies.wait()
    node_new = node_rows(spot_ref, nodes, incoming, node_own, node_w, node_w2, node_out)
    node_full[...] = node_new
    pick_rows(wanted_ref, node_new, sends)


def late_kernel(pieces, spot_ref, *refs):
    refs = list(refs)
    own_w = [refs.pop(0) for _ in range(4)]
    core_w = [refs.pop(0) for _ in range(4)]
    packed = [refs.pop(0) for _ in range(2)]
    edge_ref, edge_own, node_own = [refs.pop(0) for _ in range(3)]
    tables = [refs.pop(0) for _ in range(pieces)]
    hot_ref, incidence_ref, edge_out, node_out = [refs.pop(0) for _ in range(4)]
    edge_w, edge_w2, node_w, node_w2, product_ref, table_ref, edge_sems, node_sems = refs
    edge_copies, node_copies = Copies(edge_sems), Copies(node_sems)
    base = 0
    for copies, first, second, at in (
        (edge_copies, edge_w, edge_w2, 0),
        (node_copies, node_w, node_w2, 2),
    ):
        load_shard(copies, 1, own_w[at], own_w[at + 1], 0, first, second)
        load_shard(copies, 1, core_w[at], core_w[at + 1], 1, first, second)
        for j, pack in enumerate(packed):
            load_packed(copies, pack, base, 2 + j, first, second)
        base = edge_w.shape[0] + edge_w2.shape[1]
    start = 0
    for table in tables:
        table_ref[start : start + table.shape[0], :] = table[...]
        start += table.shape[0]
    edge_copies.wait()
    nodes = tables[0][...]
    incoming = edge_rows(
        spot_ref, edge_ref, table_ref[...], nodes, edge_own, hot_ref, incidence_ref,
        edge_w, edge_w2, product_ref, edge_out, None,
    )
    node_copies.wait()
    node_rows(spot_ref, nodes, incoming, node_own, node_w, node_w2, node_out)


SMEM, VMEM, ANY = pltpu.SMEM, pltpu.VMEM, pl.ANY


def call(kernel, out_shape, args, scratch, flops, name, vmem_mib=24):
    arrays = [a for _, a in args]
    moved = sum(a.size * a.dtype.itemsize for a in arrays + list(out_shape))
    return pl.pallas_call(
        kernel,
        out_shape=out_shape,
        in_specs=[pl.BlockSpec(memory_space=s) for s, _ in args],
        out_specs=[pl.BlockSpec(memory_space=VMEM)] * len(out_shape),
        scratch_shapes=scratch,
        compiler_params=pltpu.CompilerParams(vmem_limit_bytes=vmem_mib * 1024 * 1024),
        cost_estimate=pl.CostEstimate(flops=flops, bytes_accessed=moved, transcendentals=0),
        name=name,
    )(*arrays)


def swap(x, mask):
    size = lax.axis_size("mp")
    return lax.ppermute(x, "mp", [(i, i ^ mask) for i in range(size)])


def shift(x, by):
    size = lax.axis_size("graph")
    return lax.ppermute(x, "graph", [(i, (i + by) % size) for i in range(size)])


def after(x, *others):
    return lax.optimization_barrier((x, *others))[0]


def neighbour_rows(right, left, coarse, halo):
    if lax.axis_size("graph") == 4:
        return [shift(right, 1), shift(left, -1), shift(coarse, 2)]
    everyone = lax.all_gather(coarse, "graph", axis=0, tiled=True)
    return [shift(right[:halo], 1), shift(left[:halo], -1), everyone]


def table_index(senders, node_count, halo):
    size = lax.axis_size("graph")
    coarse_start = node_count + 2 * halo
    number = jnp.maximum(senders - coarse_start, 0)
    block, row = number // COARSE_DEV, number % COARSE_DEV
    if size != 4:
        return jnp.where(senders < coarse_start, senders, coarse_start + block * COARSE_PAD + row)
    wide = halo + COARSE_PAD
    away = (block - lax.axis_index("graph")) % size
    starts = (node_count - COARSE_DEV, node_count + wide + halo, node_count + 2 * wide, node_count + halo)
    base = jnp.where(
        away < 2,
        jnp.where(away == 0, starts[0], starts[1]),
        jnp.where(away == 2, starts[2], starts[3]),
    )
    fine = jnp.where(senders < node_count + halo, senders, senders + COARSE_PAD)
    return jnp.where(senders < coarse_start, fine, base + row)


def on_device(
    node_state,
    edge_state,
    edge_first,
    edge_second,
    node_first,
    node_second,
    senders,
    receivers,
    boundary_rows,
):
    node_count, part = node_state.shape
    edge_count = edge_state.shape[0]
    features = edge_second.shape[2]
    hidden = 4 * part
    halo = boundary_rows.shape[0] // 2
    blocks = lax.axis_size("graph")
    shape = jax.ShapeDtypeStruct
    dma = pltpu.SemaphoreType.DMA
    block = lax.axis_index("graph")
    group = lax.axis_index("groups")
    spot = jnp.stack([lax.axis_index("mp"), group, group * blocks + block]).astype(jnp.int32)

    wide = halo + COARSE_PAD

    def sent(width):
        return [shape((n, width), BF16) for n in (wide, wide, COARSE_PAD)]

    weights = (edge_first, edge_second, node_first, node_second)
    edge_pack = edge_first.shape[1] + features
    node_pack = node_first.shape[1] + features
    (ride,) = call(
        ride_kernel,
        [shape(((edge_pack + node_pack) // 2, part), BF16)],
        [(SMEM, spot)] + [(ANY, w) for w in weights],
        [dma((10,))],
        0,
        "layer_0_half",
        60,
    )
    near = swap(ride, 2)
    boundary_rows = after(boundary_rows, ride)
    own_coarse = jnp.arange(node_count - COARSE_DEV, node_count, dtype=jnp.int32)
    padding = jnp.full((COARSE_PAD - COARSE_DEV,), -1, jnp.int32)
    coarse_list = jnp.concatenate([own_coarse, padding])
    wanted = jnp.concatenate(
        [boundary_rows[halo:], coarse_list, boundary_rows[:halo], coarse_list, coarse_list]
    )[:, None]
    node_bf, right, left, coarse = call(
        start_kernel,
        [shape((node_count, part), BF16)] + sent(part),
        [(VMEM, after(node_state, ride)), (VMEM, wanted)],
        [],
        2 * wanted.shape[0] * node_count * part,
        "boundary_rows",
    )
    halo_rows = neighbour_rows(right, left, coarse, halo)
    table_rows = node_count + sum(r.shape[0] for r in halo_rows)
    lanes = -(-(table_rows + node_count) // 128) * 128
    senders, receivers = lax.optimization_barrier((senders, receivers, right))[:2]
    index = jnp.stack([table_index(senders, node_count, halo), receivers + table_rows], axis=1)
    hot, incidence, late_w = call(
        prepare_kernel,
        [
            shape((edge_count, lanes), BF16),
            shape((node_count, edge_count), BF16),
            shape((edge_pack + node_pack, part), BF16),
        ],
        [(VMEM, index), (VMEM, receivers[None, :])] + [(ANY, w) for w in weights],
        [dma((10,))],
        0,
        "one_hot",
    )
    core_w = [swap(after(w, right), 1) for w in weights]
    (latents,) = call(
        latent_kernel,
        [shape((edge_count + table_rows, part), BF16)],
        [(VMEM, after(edge_state, late_w)), (VMEM, node_bf)] + [(VMEM, r) for r in halo_rows],
        [],
        0,
        "latents",
    )
    far_latents = swap(after(latents, near, *core_w), 2)
    shards = [latents, swap(latents, 1), far_latents, swap(far_latents, 1)]
    far = lax.ppermute(near, "groups", [(0, 1), (1, 0)])
    pairs = [near, far, swap(near, 1), swap(far, 1)]
    late_x = swap(after(late_w, far_latents), 2)

    edge_flops = 2 * edge_count * features * (2 * features + lanes + node_count)
    node_flops = 2 * node_count * features * 3 * features
    full_edge = shape((edge_count, features), BF16)
    full_node = shape((node_count, features), BF16)
    own_edge = shape((edge_count, part), F32)
    own_node = shape((node_count, part), F32)
    second_shape = pltpu.VMEM((hidden, features), BF16)
    edge_shape = pltpu.VMEM((edge_first.shape[1], hidden), BF16)
    node_shape = pltpu.VMEM((node_first.shape[1], hidden), BF16)

    edge_own, edge_full, node_own, node_full, right, left, coarse = call(
        first_kernel,
        [own_edge, full_edge, own_node, full_node] + sent(features),
        [(SMEM, spot)]
        + [(ANY, w) for w in list(weights) + core_w + pairs + shards]
        + [(VMEM, a) for a in (edge_state, node_state, hot, incidence, wanted)],
        [
            edge_shape,
            second_shape,
            node_shape,
            second_shape,
            pltpu.VMEM((lanes, hidden), BF16),
            pltpu.VMEM((edge_count + table_rows, features), BF16),
            dma((28,)),
            dma((24,)),
        ],
        edge_flops + node_flops,
        "layer_0",
    )
    tables = [node_full] + neighbour_rows(right, left, coarse, halo)
    late_d = swap(after(late_x, tables[1]), 1)
    edge_own, node_own = call(
        functools.partial(late_kernel, len(tables)),
        [own_edge, own_node],
        [(SMEM, spot)]
        + [(ANY, w) for w in list(weights) + core_w + [late_x, late_d]]
        + [(VMEM, a) for a in (edge_full, edge_own, node_own)]
        + [(VMEM, t) for t in tables]
        + [(VMEM, hot), (VMEM, incidence)],
        [
            edge_shape,
            second_shape,
            node_shape,
            second_shape,
            pltpu.VMEM((lanes, hidden), BF16),
            pltpu.VMEM((table_rows, features), BF16),
            dma((14,)),
            dma((14,)),
        ],
        edge_flops + node_flops,
        "layer_1",
    )
    return (node_own, edge_own)


def solution(mesh):
    in_specs = (
        P(("groups", "graph"), "mp"),
        P(("groups", "graph"), "mp"),
        P(None, None, "mp"),
        P(None, "mp", None),
        P(None, None, "mp"),
        P(None, "mp", None),
        P("graph"),
        P("graph"),
        P("graph"),
    )
    out_specs = (P(("groups", "graph"), "mp"), P(("groups", "graph"), "mp"))
    return jax.shard_map(
        on_device, mesh=mesh, in_specs=in_specs, out_specs=out_specs, check_vma=False
    )
```

```python
import functools

import jax
import jax.numpy as jnp
from jax import lax
from jax.experimental import pallas as pl
from jax.experimental.pallas import tpu as pltpu
from jax.sharding import PartitionSpec as P

COARSE_DEV = 12
COARSE_PAD = 16
EPS = 1e-05
TILE = 256
F32 = jnp.float32
BF16 = jnp.bfloat16


def silu(x):
    half = 0.5 * x
    return half + half * jnp.tanh(half)


def normalize(msg):
    width = msg.shape[1]
    mean = jnp.sum(msg, axis=1, keepdims=True) * (1.0 / width)
    square = jnp.sum(msg * msg, axis=1, keepdims=True) * (1.0 / width)
    return (msg - mean) * lax.rsqrt(square - mean * mean + EPS)


def dot(a, b):
    return jnp.dot(a, b, preferred_element_type=F32)


def own_columns(full, spot_ref, part):
    mine = spot_ref[0]
    out = full[:, 0:part]
    for j in range(1, full.shape[1] // part):
        out = jnp.where(mine == j, full[:, j * part : (j + 1) * part], out)
    return out


class Copies:
    def __init__(self, sems):
        self.sems, self.started = sems, []

    def start(self, source, target):
        copy = pltpu.make_async_copy(source, target, self.sems.at[len(self.started)])
        copy.start()
        self.started.append(copy)

    def wait(self):
        for copy in self.started:
            copy.wait()


def load_shard(copies, layer, first, second, j, first_ref, second_ref):
    part = second.shape[1]
    copies.start(first.at[layer], first_ref.at[:, pl.ds(j * part, part)])
    copies.start(second.at[layer], second_ref.at[pl.ds(j * part, part)])


def load_packed(copies, packed, base, j, first_ref, second_ref):
    rows = first_ref.shape[0]
    hidden, features = second_ref.shape
    part = hidden // 4
    copies.start(packed.at[pl.ds(base, rows)], first_ref.at[:, pl.ds(j * part, part)])
    for q in range(features // part):
        copies.start(
            packed.at[pl.ds(base + rows + q * part, part)],
            second_ref.at[pl.ds(j * part, part), pl.ds(q * part, part)],
        )


def load_half(copies, packed, base, half, j, first_ref, second_ref):
    rows = first_ref.shape[0] // 2
    hidden, features = second_ref.shape
    part = hidden // 4
    deep = part // 2
    at = pl.multiple_of(half * rows, rows)
    copies.start(packed.at[pl.ds(base, rows)], first_ref.at[pl.ds(at, rows), pl.ds(j * part, part)])
    at = pl.multiple_of(j * part + half * deep, deep)
    for q in range(features // part):
        copies.start(
            packed.at[pl.ds(base + rows + q * deep, deep)],
            second_ref.at[pl.ds(at, deep), pl.ds(q * part, part)],
        )
    return base + rows + features // part * deep


def ride_kernel(spot_ref, ef, es, nf, ns, ride_out, sems):
    y = spot_ref[1]
    part, features = es.shape[1:]
    copies = Copies(sems)
    at = 0
    for first, second in ((ef, es), (nf, ns)):
        rows = first.shape[1] // 2
        source = first.at[0, pl.ds(pl.multiple_of(y * rows, rows), rows)]
        copies.start(source, ride_out.at[pl.ds(at, rows)])
        at += rows
        deep = part // 2
        for q in range(features // part):
            source = second.at[0, pl.ds(pl.multiple_of(y * deep, deep), deep), pl.ds(q * part, part)]
            copies.start(source, ride_out.at[pl.ds(at, deep)])
            at += deep
    copies.wait()


def prepare_kernel(index_ref, receiver_ref, ef, es, nf, ns, hot_out, incidence_out, late_out, sems):
    part, features = es.shape[1:]
    copies = Copies(sems)
    at = 0
    for first, second in ((ef, es), (nf, ns)):
        rows = first.shape[1]
        copies.start(first.at[1], late_out.at[pl.ds(at, rows)])
        at += rows
        for q in range(features // part):
            copies.start(second.at[1, :, pl.ds(q * part, part)], late_out.at[pl.ds(at, part)])
            at += part
    for at in range(0, hot_out.shape[0], TILE):
        rows = slice(at, at + TILE)
        index = index_ref[rows, :]
        lanes = lax.broadcasted_iota(jnp.int32, (TILE, hot_out.shape[1]), 1)
        hot = (lanes == index[:, 0:1]) | (lanes == index[:, 1:2])
        hot_out[rows, :] = jnp.where(hot, 1.0, 0.0).astype(BF16)
        node_ids = lax.broadcasted_iota(jnp.int32, (incidence_out.shape[0], TILE), 0)
        hit = node_ids == receiver_ref[:, rows]
        incidence_out[:, rows] = jnp.where(hit, 1.0, 0.0).astype(BF16)
    copies.wait()


def pick_rows(wanted_ref, node_bf, outs):
    wanted = wanted_ref[...]
    lanes = lax.broadcasted_iota(jnp.int32, (wanted.shape[0], node_bf.shape[0]), 1)
    picked = dot(jnp.where(lanes == wanted, 1.0, 0.0).astype(BF16), node_bf).astype(BF16)
    start = 0
    for out in outs:
        out[...] = picked[start : start + out.shape[0]]
        start += out.shape[0]


def start_kernel(node_ref, wanted_ref, right, left, coarse):
    pick_rows(wanted_ref, node_ref[...].astype(BF16), (right, left, coarse))


def latent_kernel(edge_ref, node_ref, out):
    at = edge_ref.shape[0]
    out[0:at, :] = edge_ref[...].astype(BF16)
    out[at:, :] = node_ref[...].astype(BF16)


def edge_rows(spot_ref, edge_ref, table, nodes, own_ref, hot_ref, incidence_ref, first_ref, second_ref, product_ref, own_out, full_out):
    features = second_ref.shape[1]
    node_count = nodes.shape[0]
    table_rows = table.shape[0]
    lanes_all = product_ref.shape[0]
    used = table_rows + node_count
    part = own_ref.shape[1]
    product_ref[0:table_rows, :] = dot(table, first_ref[features : 2 * features, :]).astype(BF16)
    product_ref[table_rows:used, :] = dot(
        nodes, first_ref[2 * features : 3 * features, :]
    ).astype(BF16)
    if used < lanes_all:
        product_ref[used:, :] = jnp.zeros((lanes_all - used, features), BF16)
    incoming = jnp.zeros((node_count, features), F32)
    for at in range(0, own_ref.shape[0], TILE):
        rows = slice(at, at + TILE)
        edge_bf = edge_ref[rows, :]
        pre = dot(edge_bf, first_ref[0:features, :]) + dot(hot_ref[rows, :], product_ref[...])
        norm = normalize(dot(silu(pre).astype(BF16), second_ref[...]))
        edge_new = (edge_bf.astype(F32) + norm).astype(BF16)
        if full_out is not None:
            full_out[rows, :] = edge_new
        own_out[rows, :] = own_ref[rows, :] + own_columns(norm, spot_ref, part)
        incoming = incoming + dot(incidence_ref[:, rows], edge_new)
    return incoming.astype(BF16)


def node_rows(spot_ref, node_bf, incoming, own_ref, first_ref, second_ref, own_out):
    features = second_ref.shape[1]
    pre = dot(node_bf, first_ref[0:features, :]) + dot(incoming, first_ref[features:, :])
    norm = normalize(dot(silu(pre).astype(BF16), second_ref[...]))
    own_out[...] = own_ref[...] + own_columns(norm, spot_ref, own_ref.shape[1])
    return (node_bf.astype(F32) + norm).astype(BF16)


def first_kernel(spot_ref, *refs):
    refs = list(refs)
    own_w = [refs.pop(0) for _ in range(4)]
    core_w = [refs.pop(0) for _ in range(4)]
    halves = [[refs.pop(0) for _ in range(2)] for _ in range(2)]
    shards = [refs.pop(0) for _ in range(4)]
    rims = [refs.pop(0) for _ in range(4)]
    edge_own, node_own, hot_ref, incidence_ref, wanted_ref = [refs.pop(0) for _ in range(5)]
    edge_out, full_out, node_out, node_full = [refs.pop(0) for _ in range(4)]
    sends = [refs.pop(0) for _ in range(3)]
    edge_w, edge_w2, node_w, node_w2, product_ref, x_ref, edge_sems, node_sems = refs
    part = edge_own.shape[1]
    edge_count = edge_own.shape[0]
    node_count = node_own.shape[0]
    edge_copies, node_copies = Copies(edge_sems), Copies(node_sems)
    for pieces, at in ((shards, 0), (rims, edge_count + node_count)):
        rows = pl.ds(at, pieces[0].shape[0])
        for j, shard in enumerate(pieces):
            column = pl.multiple_of((spot_ref[0] ^ j) * part, part)
            edge_copies.start(shard, x_ref.at[rows, pl.ds(column, part)])
    y = spot_ref[1]
    starts = [0, 0]
    for base, copies, (first, second), at in (
        (0, edge_copies, (edge_w, edge_w2), 0),
        (1, node_copies, (node_w, node_w2), 2),
    ):
        load_shard(copies, 0, own_w[at], own_w[at + 1], 0, first, second)
        load_shard(copies, 0, core_w[at], core_w[at + 1], 1, first, second)
        for j, pair in enumerate(halves):
            for k, piece in enumerate(pair):
                half = y if k == 0 else 1 - y
                end = load_half(copies, piece, starts[base], half, 2 + j, first, second)
        starts[1] = end
    edge_copies.wait()
    nodes = x_ref[edge_count : edge_count + node_count, :]
    incoming = edge_rows(
        spot_ref, x_ref, x_ref[edge_count:, :], nodes, edge_own, hot_ref, incidence_ref,
        edge_w, edge_w2, product_ref, edge_out, full_out,
    )
    node_copies.wait()
    node_new = node_rows(spot_ref, nodes, incoming, node_own, node_w, node_w2, node_out)
    node_full[...] = node_new
    pick_rows(wanted_ref, node_new, sends)


def late_kernel(pieces, spot_ref, *refs):
    refs = list(refs)
    own_w = [refs.pop(0) for _ in range(4)]
    core_w = [refs.pop(0) for _ in range(4)]
    packed = [refs.pop(0) for _ in range(2)]
    edge_ref, edge_own, node_own = [refs.pop(0) for _ in range(3)]
    tables = [refs.pop(0) for _ in range(pieces)]
    hot_ref, incidence_ref, edge_out, node_out = [refs.pop(0) for _ in range(4)]
    edge_w, edge_w2, node_w, node_w2, product_ref, table_ref, edge_sems, node_sems = refs
    edge_copies, node_copies = Copies(edge_sems), Copies(node_sems)
    base = 0
    for copies, first, second, at in (
        (edge_copies, edge_w, edge_w2, 0),
        (node_copies, node_w, node_w2, 2),
    ):
        load_shard(copies, 1, own_w[at], own_w[at + 1], 0, first, second)
        load_shard(copies, 1, core_w[at], core_w[at + 1], 1, first, second)
        for j, pack in enumerate(packed):
            load_packed(copies, pack, base, 2 + j, first, second)
        base = edge_w.shape[0] + edge_w2.shape[1]
    start = 0
    for table in tables:
        table_ref[start : start + table.shape[0], :] = table[...]
        start += table.shape[0]
    edge_copies.wait()
    nodes = tables[0][...]
    incoming = edge_rows(
        spot_ref, edge_ref, table_ref[...], nodes, edge_own, hot_ref, incidence_ref,
        edge_w, edge_w2, product_ref, edge_out, None,
    )
    node_copies.wait()
    node_rows(spot_ref, nodes, incoming, node_own, node_w, node_w2, node_out)


SMEM, VMEM, ANY = pltpu.SMEM, pltpu.VMEM, pl.ANY


def call(kernel, out_shape, args, scratch, flops, name, vmem_mib=24):
    arrays = [a for _, a in args]
    moved = sum(a.size * a.dtype.itemsize for a in arrays + list(out_shape))
    return pl.pallas_call(
        kernel,
        out_shape=out_shape,
        in_specs=[pl.BlockSpec(memory_space=s) for s, _ in args],
        out_specs=[pl.BlockSpec(memory_space=VMEM)] * len(out_shape),
        scratch_shapes=scratch,
        compiler_params=pltpu.CompilerParams(vmem_limit_bytes=vmem_mib * 1024 * 1024),
        cost_estimate=pl.CostEstimate(flops=flops, bytes_accessed=moved, transcendentals=0),
        name=name,
    )(*arrays)


def swap(x, mask):
    size = lax.axis_size("mp")
    return lax.ppermute(x, "mp", [(i, i ^ mask) for i in range(size)])


def shift(x, by):
    size = lax.axis_size("graph")
    return lax.ppermute(x, "graph", [(i, (i + by) % size) for i in range(size)])


def after(x, *others):
    return lax.optimization_barrier((x, *others))[0]


def neighbour_rows(right, left, coarse, halo):
    if lax.axis_size("graph") == 4:
        return [shift(right, 1), shift(left, -1), shift(coarse, 2)]
    everyone = lax.all_gather(coarse, "graph", axis=0, tiled=True)
    return [shift(right[:halo], 1), shift(left[:halo], -1), everyone]


def table_index(senders, node_count, halo):
    size = lax.axis_size("graph")
    coarse_start = node_count + 2 * halo
    number = jnp.maximum(senders - coarse_start, 0)
    block, row = number // COARSE_DEV, number % COARSE_DEV
    if size != 4:
        return jnp.where(senders < coarse_start, senders, coarse_start + block * COARSE_PAD + row)
    wide = halo + COARSE_PAD
    away = (block - lax.axis_index("graph")) % size
    starts = (node_count - COARSE_DEV, node_count + wide + halo, node_count + 2 * wide, node_count + halo)
    base = jnp.where(
        away < 2,
        jnp.where(away == 0, starts[0], starts[1]),
        jnp.where(away == 2, starts[2], starts[3]),
    )
    fine = jnp.where(senders < node_count + halo, senders, senders + COARSE_PAD)
    return jnp.where(senders < coarse_start, fine, base + row)


def on_device(
    node_state,
    edge_state,
    edge_first,
    edge_second,
    node_first,
    node_second,
    senders,
    receivers,
    boundary_rows,
):
    node_count, part = node_state.shape
    edge_count = edge_state.shape[0]
    features = edge_second.shape[2]
    hidden = 4 * part
    halo = boundary_rows.shape[0] // 2
    blocks = lax.axis_size("graph")
    shape = jax.ShapeDtypeStruct
    dma = pltpu.SemaphoreType.DMA
    block = lax.axis_index("graph")
    group = lax.axis_index("groups")
    spot = jnp.stack([lax.axis_index("mp"), group, group * blocks + block]).astype(jnp.int32)

    wide = halo + COARSE_PAD

    def sent(width):
        return [shape((n, width), BF16) for n in (wide, wide, COARSE_PAD)]

    weights = (edge_first, edge_second, node_first, node_second)
    edge_pack = edge_first.shape[1] + features
    node_pack = node_first.shape[1] + features
    (ride,) = call(
        ride_kernel,
        [shape(((edge_pack + node_pack) // 2, part), BF16)],
        [(SMEM, spot)] + [(ANY, w) for w in weights],
        [dma((10,))],
        0,
        "layer_0_half",
        60,
    )
    near = swap(ride, 2)
    own_coarse = jnp.arange(node_count - COARSE_DEV, node_count, dtype=jnp.int32)
    padding = jnp.full((COARSE_PAD - COARSE_DEV,), -1, jnp.int32)
    coarse_list = jnp.concatenate([own_coarse, padding])
    boundary_rows, senders, receivers = lax.optimization_barrier(
        (boundary_rows, senders, receivers, ride)
    )[:3]
    wanted = jnp.concatenate(
        [boundary_rows[halo:], coarse_list, boundary_rows[:halo], coarse_list, coarse_list]
    )[:, None]
    far_rows = 2 * wide + COARSE_PAD if blocks == 4 else 2 * halo + blocks * COARSE_PAD
    table_rows = node_count + far_rows
    lanes = -(-(table_rows + node_count) // 128) * 128
    index = jnp.stack([table_index(senders, node_count, halo), receivers + table_rows], axis=1)
    hot, incidence, late_w = call(
        prepare_kernel,
        [
            shape((edge_count, lanes), BF16),
            shape((node_count, edge_count), BF16),
            shape((edge_pack + node_pack, part), BF16),
        ],
        [(VMEM, index), (VMEM, receivers[None, :])] + [(ANY, w) for w in weights],
        [dma((10,))],
        0,
        "one_hot",
    )
    core_w = [swap(after(w, ride), 1) for w in weights]
    (latents,) = call(
        latent_kernel,
        [shape((edge_count + node_count, part), BF16)],
        [(VMEM, after(edge_state, late_w)), (VMEM, node_state)],
        [],
        0,
        "latents",
    )
    right, left, coarse = call(
        start_kernel,
        sent(part),
        [(VMEM, node_state), (VMEM, after(wanted, latents))],
        [],
        2 * wanted.shape[0] * node_count * part,
        "boundary_rows",
    )
    latents_sent, right, left, coarse = lax.optimization_barrier(
        (latents, right, left, coarse, near, *core_w)
    )[:4]
    far_latents = swap(latents_sent, 2)
    shards = [latents, swap(latents, 1), far_latents, swap(far_latents, 1)]
    rim = jnp.concatenate(neighbour_rows(right, left, coarse, halo), axis=0)
    far_rim = swap(rim, 2)
    rims = [rim, swap(rim, 1), far_rim, swap(far_rim, 1)]
    far = lax.ppermute(near, "groups", [(0, 1), (1, 0)])
    pairs = [near, far, swap(near, 1), swap(far, 1)]
    late_x = swap(after(late_w, far_latents, far_rim), 2)

    edge_flops = 2 * edge_count * features * (2 * features + lanes + node_count)
    node_flops = 2 * node_count * features * 3 * features
    full_edge = shape((edge_count, features), BF16)
    full_node = shape((node_count, features), BF16)
    own_edge = shape((edge_count, part), F32)
    own_node = shape((node_count, part), F32)
    second_shape = pltpu.VMEM((hidden, features), BF16)
    edge_shape = pltpu.VMEM((edge_first.shape[1], hidden), BF16)
    node_shape = pltpu.VMEM((node_first.shape[1], hidden), BF16)

    edge_own, edge_full, node_own, node_full, right, left, coarse = call(
        first_kernel,
        [own_edge, full_edge, own_node, full_node] + sent(features),
        [(SMEM, spot)]
        + [(ANY, w) for w in list(weights) + core_w + pairs + shards + rims]
        + [(VMEM, a) for a in (edge_state, node_state, hot, incidence, wanted)],
        [
            edge_shape,
            second_shape,
            node_shape,
            second_shape,
            pltpu.VMEM((lanes, hidden), BF16),
            pltpu.VMEM((edge_count + table_rows, features), BF16),
            dma((32,)),
            dma((24,)),
        ],
        edge_flops + node_flops,
        "layer_0",
    )
    tables = [node_full] + neighbour_rows(right, left, coarse, halo)
    late_d = swap(after(late_x, *tables[1:]), 1)
    edge_own, node_own = call(
        functools.partial(late_kernel, len(tables)),
        [own_edge, own_node],
        [(SMEM, spot)]
        + [(ANY, w) for w in list(weights) + core_w + [late_x, late_d]]
        + [(VMEM, a) for a in (edge_full, edge_own, node_own)]
        + [(VMEM, t) for t in tables]
        + [(VMEM, hot), (VMEM, incidence)],
        [
            edge_shape,
            second_shape,
            node_shape,
            second_shape,
            pltpu.VMEM((lanes, hidden), BF16),
            pltpu.VMEM((table_rows, features), BF16),
            dma((14,)),
            dma((14,)),
        ],
        edge_flops + node_flops,
        "layer_1",
    )
    return (node_own, edge_own)


def solution(mesh):
    in_specs = (
        P(("groups", "graph"), "mp"),
        P(("groups", "graph"), "mp"),
        P(None, None, "mp"),
        P(None, "mp", None),
        P(None, None, "mp"),
        P(None, "mp", None),
        P("graph"),
        P("graph"),
        P("graph"),
    )
    out_specs = (P(("groups", "graph"), "mp"), P(("groups", "graph"), "mp"))
    return jax.shard_map(
        on_device, mesh=mesh, in_specs=in_specs, out_specs=out_specs, check_vma=False
    )
```

```python
import functools

import jax
import jax.numpy as jnp
from jax import lax
from jax.experimental import pallas as pl
from jax.experimental.pallas import tpu as pltpu
from jax.sharding import PartitionSpec as P

COARSE_DEV = 12
COARSE_PAD = 16
EPS = 1e-05
TILE = 256
F32 = jnp.float32
BF16 = jnp.bfloat16


def silu(x):
    half = 0.5 * x
    return half + half * jnp.tanh(half)


def normalize(msg):
    width = msg.shape[1]
    mean = jnp.sum(msg, axis=1, keepdims=True) * (1.0 / width)
    square = jnp.sum(msg * msg, axis=1, keepdims=True) * (1.0 / width)
    return (msg - mean) * lax.rsqrt(square - mean * mean + EPS)


def dot(a, b):
    return jnp.dot(a, b, preferred_element_type=F32)


def own_columns(full, spot_ref, part):
    mine = spot_ref[0]
    out = full[:, 0:part]
    for j in range(1, full.shape[1] // part):
        out = jnp.where(mine == j, full[:, j * part : (j + 1) * part], out)
    return out


class Copies:
    def __init__(self, sems):
        self.sems, self.started = sems, []

    def start(self, source, target):
        copy = pltpu.make_async_copy(source, target, self.sems.at[len(self.started)])
        copy.start()
        self.started.append(copy)

    def wait(self):
        for copy in self.started:
            copy.wait()


def load_shard(copies, layer, first, second, j, first_ref, second_ref):
    part = second.shape[1]
    copies.start(first.at[layer], first_ref.at[:, pl.ds(j * part, part)])
    copies.start(second.at[layer], second_ref.at[pl.ds(j * part, part)])


def load_packed(copies, packed, base, j, first_ref, second_ref):
    rows = first_ref.shape[0]
    hidden, features = second_ref.shape
    part = hidden // 4
    copies.start(packed.at[pl.ds(base, rows)], first_ref.at[:, pl.ds(j * part, part)])
    for q in range(features // part):
        copies.start(
            packed.at[pl.ds(base + rows + q * part, part)],
            second_ref.at[pl.ds(j * part, part), pl.ds(q * part, part)],
        )


def load_half(copies, packed, base, half, j, first_ref, second_ref):
    rows = first_ref.shape[0] // 2
    hidden, features = second_ref.shape
    part = hidden // 4
    deep = part // 2
    at = pl.multiple_of(half * rows, rows)
    copies.start(packed.at[pl.ds(base, rows)], first_ref.at[pl.ds(at, rows), pl.ds(j * part, part)])
    at = pl.multiple_of(j * part + half * deep, deep)
    for q in range(features // part):
        copies.start(
            packed.at[pl.ds(base + rows + q * deep, deep)],
            second_ref.at[pl.ds(at, deep), pl.ds(q * part, part)],
        )
    return base + rows + features // part * deep


def ride_kernel(spot_ref, ef, es, nf, ns, ride_out, sems):
    y = spot_ref[1]
    part, features = es.shape[1:]
    copies = Copies(sems)
    at = 0
    for first, second in ((ef, es), (nf, ns)):
        rows = first.shape[1] // 2
        source = first.at[0, pl.ds(pl.multiple_of(y * rows, rows), rows)]
        copies.start(source, ride_out.at[pl.ds(at, rows)])
        at += rows
        deep = part // 2
        for q in range(features // part):
            source = second.at[0, pl.ds(pl.multiple_of(y * deep, deep), deep), pl.ds(q * part, part)]
            copies.start(source, ride_out.at[pl.ds(at, deep)])
            at += deep
    copies.wait()


def prepare_kernel(index_ref, receiver_ref, ef, es, nf, ns, hot_out, incidence_out, late_out, sems):
    part, features = es.shape[1:]
    copies = Copies(sems)
    at = 0
    for first, second in ((ef, es), (nf, ns)):
        rows = first.shape[1]
        copies.start(first.at[1], late_out.at[pl.ds(at, rows)])
        at += rows
        for q in range(features // part):
            copies.start(second.at[1, :, pl.ds(q * part, part)], late_out.at[pl.ds(at, part)])
            at += part
    for at in range(0, hot_out.shape[0], TILE):
        rows = slice(at, at + TILE)
        index = index_ref[rows, :]
        lanes = lax.broadcasted_iota(jnp.int32, (TILE, hot_out.shape[1]), 1)
        hot = (lanes == index[:, 0:1]) | (lanes == index[:, 1:2])
        hot_out[rows, :] = jnp.where(hot, 1.0, 0.0).astype(BF16)
        node_ids = lax.broadcasted_iota(jnp.int32, (incidence_out.shape[0], TILE), 0)
        hit = node_ids == receiver_ref[:, rows]
        incidence_out[:, rows] = jnp.where(hit, 1.0, 0.0).astype(BF16)
    copies.wait()


def pick_rows(wanted_ref, node_bf, outs):
    wanted = wanted_ref[...]
    lanes = lax.broadcasted_iota(jnp.int32, (wanted.shape[0], node_bf.shape[0]), 1)
    picked = dot(jnp.where(lanes == wanted, 1.0, 0.0).astype(BF16), node_bf).astype(BF16)
    start = 0
    for out in outs:
        out[...] = picked[start : start + out.shape[0]]
        start += out.shape[0]


def start_kernel(node_ref, wanted_ref, right, left, coarse):
    pick_rows(wanted_ref, node_ref[...].astype(BF16), (right, left, coarse))


def latent_kernel(edge_ref, node_ref, out):
    at = edge_ref.shape[0]
    out[0:at, :] = edge_ref[...].astype(BF16)
    out[at:, :] = node_ref[...].astype(BF16)


def edge_rows(spot_ref, edge_ref, table, nodes, own_ref, hot_ref, incidence_ref, first_ref, second_ref, product_ref, own_out, full_out):
    features = second_ref.shape[1]
    node_count = nodes.shape[0]
    table_rows = table.shape[0]
    lanes_all = product_ref.shape[0]
    used = table_rows + node_count
    part = own_ref.shape[1]
    product_ref[0:table_rows, :] = dot(table, first_ref[features : 2 * features, :]).astype(BF16)
    product_ref[table_rows:used, :] = dot(
        nodes, first_ref[2 * features : 3 * features, :]
    ).astype(BF16)
    if used < lanes_all:
        product_ref[used:, :] = jnp.zeros((lanes_all - used, features), BF16)
    incoming = jnp.zeros((node_count, features), F32)
    for at in range(0, own_ref.shape[0], TILE):
        rows = slice(at, at + TILE)
        edge_bf = edge_ref[rows, :]
        pre = dot(edge_bf, first_ref[0:features, :]) + dot(hot_ref[rows, :], product_ref[...])
        norm = normalize(dot(silu(pre).astype(BF16), second_ref[...]))
        edge_new = (edge_bf.astype(F32) + norm).astype(BF16)
        if full_out is not None:
            full_out[rows, :] = edge_new
        own_out[rows, :] = own_ref[rows, :] + own_columns(norm, spot_ref, part)
        incoming = incoming + dot(incidence_ref[:, rows], edge_new)
    return incoming.astype(BF16)


def node_rows(spot_ref, node_bf, incoming, own_ref, first_ref, second_ref, own_out):
    features = second_ref.shape[1]
    pre = dot(node_bf, first_ref[0:features, :]) + dot(incoming, first_ref[features:, :])
    norm = normalize(dot(silu(pre).astype(BF16), second_ref[...]))
    own_out[...] = own_ref[...] + own_columns(norm, spot_ref, own_ref.shape[1])
    return (node_bf.astype(F32) + norm).astype(BF16)


def first_kernel(spot_ref, *refs):
    refs = list(refs)
    own_w = [refs.pop(0) for _ in range(4)]
    core_w = [refs.pop(0) for _ in range(4)]
    halves = [[refs.pop(0) for _ in range(2)] for _ in range(2)]
    shards = [refs.pop(0) for _ in range(4)]
    rims = [refs.pop(0) for _ in range(4)]
    edge_own, node_own, hot_ref, incidence_ref, wanted_ref = [refs.pop(0) for _ in range(5)]
    edge_out, full_out, node_out, node_full = [refs.pop(0) for _ in range(4)]
    sends = [refs.pop(0) for _ in range(3)]
    edge_w, edge_w2, node_w, node_w2, product_ref, x_ref, edge_sems, node_sems = refs
    part = edge_own.shape[1]
    edge_count = edge_own.shape[0]
    node_count = node_own.shape[0]
    edge_copies, node_copies = Copies(edge_sems), Copies(node_sems)
    for pieces, at in ((shards, 0), (rims, edge_count + node_count)):
        rows = pl.ds(at, pieces[0].shape[0])
        for j, shard in enumerate(pieces):
            column = pl.multiple_of((spot_ref[0] ^ j) * part, part)
            edge_copies.start(shard, x_ref.at[rows, pl.ds(column, part)])
    y = spot_ref[1]
    starts = [0, 0]
    for base, copies, (first, second), at in (
        (0, edge_copies, (edge_w, edge_w2), 0),
        (1, node_copies, (node_w, node_w2), 2),
    ):
        load_shard(copies, 0, own_w[at], own_w[at + 1], 0, first, second)
        load_shard(copies, 0, core_w[at], core_w[at + 1], 1, first, second)
        for j, pair in enumerate(halves):
            for k, piece in enumerate(pair):
                half = y if k == 0 else 1 - y
                end = load_half(copies, piece, starts[base], half, 2 + j, first, second)
        starts[1] = end
    edge_copies.wait()
    nodes = x_ref[edge_count : edge_count + node_count, :]
    incoming = edge_rows(
        spot_ref, x_ref, x_ref[edge_count:, :], nodes, edge_own, hot_ref, incidence_ref,
        edge_w, edge_w2, product_ref, edge_out, full_out,
    )
    node_copies.wait()
    node_new = node_rows(spot_ref, nodes, incoming, node_own, node_w, node_w2, node_out)
    node_full[...] = node_new
    pick_rows(wanted_ref, node_new, sends)


def late_kernel(pieces, spot_ref, *refs):
    refs = list(refs)
    own_w = [refs.pop(0) for _ in range(4)]
    core_w = [refs.pop(0) for _ in range(4)]
    packed = [refs.pop(0) for _ in range(2)]
    edge_ref, edge_own, node_own = [refs.pop(0) for _ in range(3)]
    tables = [refs.pop(0) for _ in range(pieces)]
    hot_ref, incidence_ref, edge_out, node_out = [refs.pop(0) for _ in range(4)]
    edge_w, edge_w2, node_w, node_w2, product_ref, table_ref, edge_sems, node_sems = refs
    edge_copies, node_copies = Copies(edge_sems), Copies(node_sems)
    base = 0
    for copies, first, second, at in (
        (edge_copies, edge_w, edge_w2, 0),
        (node_copies, node_w, node_w2, 2),
    ):
        load_shard(copies, 1, own_w[at], own_w[at + 1], 0, first, second)
        load_shard(copies, 1, core_w[at], core_w[at + 1], 1, first, second)
        for j, pack in enumerate(packed):
            load_packed(copies, pack, base, 2 + j, first, second)
        base = edge_w.shape[0] + edge_w2.shape[1]
    start = 0
    for table in tables:
        table_ref[start : start + table.shape[0], :] = table[...]
        start += table.shape[0]
    edge_copies.wait()
    nodes = tables[0][...]
    incoming = edge_rows(
        spot_ref, edge_ref, table_ref[...], nodes, edge_own, hot_ref, incidence_ref,
        edge_w, edge_w2, product_ref, edge_out, None,
    )
    node_copies.wait()
    node_rows(spot_ref, nodes, incoming, node_own, node_w, node_w2, node_out)


SMEM, VMEM, ANY = pltpu.SMEM, pltpu.VMEM, pl.ANY


def call(kernel, out_shape, args, scratch, flops, name, vmem_mib=8):
    arrays = [a for _, a in args]
    moved = sum(a.size * a.dtype.itemsize for a in arrays + list(out_shape))
    return pl.pallas_call(
        kernel,
        out_shape=out_shape,
        in_specs=[pl.BlockSpec(memory_space=s) for s, _ in args],
        out_specs=[pl.BlockSpec(memory_space=VMEM)] * len(out_shape),
        scratch_shapes=scratch,
        compiler_params=pltpu.CompilerParams(vmem_limit_bytes=vmem_mib * 1024 * 1024),
        cost_estimate=pl.CostEstimate(flops=flops, bytes_accessed=moved, transcendentals=0),
        name=name,
    )(*arrays)


def swap(x, mask):
    size = lax.axis_size("mp")
    return lax.ppermute(x, "mp", [(i, i ^ mask) for i in range(size)])


def shift(x, by):
    size = lax.axis_size("graph")
    return lax.ppermute(x, "graph", [(i, (i + by) % size) for i in range(size)])


def after(x, *others):
    return lax.optimization_barrier((x, *others))[0]


def neighbour_rows(right, left, coarse, halo):
    if lax.axis_size("graph") == 4:
        return [shift(right, 1), shift(left, -1), shift(coarse, 2)]
    everyone = lax.all_gather(coarse, "graph", axis=0, tiled=True)
    return [shift(right[:halo], 1), shift(left[:halo], -1), everyone]


def table_index(senders, node_count, halo):
    size = lax.axis_size("graph")
    coarse_start = node_count + 2 * halo
    number = jnp.maximum(senders - coarse_start, 0)
    block, row = number // COARSE_DEV, number % COARSE_DEV
    if size != 4:
        return jnp.where(senders < coarse_start, senders, coarse_start + block * COARSE_PAD + row)
    wide = halo + COARSE_PAD
    away = (block - lax.axis_index("graph")) % size
    starts = (node_count - COARSE_DEV, node_count + wide + halo, node_count + 2 * wide, node_count + halo)
    base = jnp.where(
        away < 2,
        jnp.where(away == 0, starts[0], starts[1]),
        jnp.where(away == 2, starts[2], starts[3]),
    )
    fine = jnp.where(senders < node_count + halo, senders, senders + COARSE_PAD)
    return jnp.where(senders < coarse_start, fine, base + row)


def on_device(
    node_state,
    edge_state,
    edge_first,
    edge_second,
    node_first,
    node_second,
    senders,
    receivers,
    boundary_rows,
):
    node_count, part = node_state.shape
    edge_count = edge_state.shape[0]
    features = edge_second.shape[2]
    hidden = 4 * part
    halo = boundary_rows.shape[0] // 2
    blocks = lax.axis_size("graph")
    shape = jax.ShapeDtypeStruct
    dma = pltpu.SemaphoreType.DMA
    block = lax.axis_index("graph")
    group = lax.axis_index("groups")
    spot = jnp.stack([lax.axis_index("mp"), group, group * blocks + block]).astype(jnp.int32)

    wide = halo + COARSE_PAD

    def sent(width):
        return [shape((n, width), BF16) for n in (wide, wide, COARSE_PAD)]

    weights = (edge_first, edge_second, node_first, node_second)
    edge_pack = edge_first.shape[1] + features
    node_pack = node_first.shape[1] + features
    (ride,) = call(
        ride_kernel,
        [shape(((edge_pack + node_pack) // 2, part), BF16)],
        [(SMEM, spot)] + [(ANY, w) for w in weights],
        [dma((10,))],
        0,
        "layer_0_half",
        60,
    )
    near = swap(ride, 2)
    own_coarse = jnp.arange(node_count - COARSE_DEV, node_count, dtype=jnp.int32)
    padding = jnp.full((COARSE_PAD - COARSE_DEV,), -1, jnp.int32)
    coarse_list = jnp.concatenate([own_coarse, padding])
    boundary_rows, senders, receivers = lax.optimization_barrier(
        (boundary_rows, senders, receivers, ride)
    )[:3]
    wanted = jnp.concatenate(
        [boundary_rows[halo:], coarse_list, boundary_rows[:halo], coarse_list, coarse_list]
    )[:, None]
    far_rows = 2 * wide + COARSE_PAD if blocks == 4 else 2 * halo + blocks * COARSE_PAD
    table_rows = node_count + far_rows
    lanes = -(-(table_rows + node_count) // 128) * 128
    index = jnp.stack([table_index(senders, node_count, halo), receivers + table_rows], axis=1)
    hot, incidence, late_w = call(
        prepare_kernel,
        [
            shape((edge_count, lanes), BF16),
            shape((node_count, edge_count), BF16),
            shape((edge_pack + node_pack, part), BF16),
        ],
        [(VMEM, index), (VMEM, receivers[None, :])] + [(ANY, w) for w in weights],
        [dma((10,))],
        0,
        "one_hot",
    )
    core_w = [swap(after(w, ride), 1) for w in weights]
    (latents,) = call(
        latent_kernel,
        [shape((edge_count + node_count, part), BF16)],
        [(VMEM, after(edge_state, late_w)), (VMEM, node_state)],
        [],
        0,
        "latents",
    )
    right, left, coarse = call(
        start_kernel,
        sent(part),
        [(VMEM, node_state), (VMEM, after(wanted, latents))],
        [],
        2 * wanted.shape[0] * node_count * part,
        "boundary_rows",
    )
    far_latents = swap(after(latents, near), 2)
    shards = [latents, swap(latents, 1), far_latents, swap(far_latents, 1)]
    rim = jnp.concatenate(neighbour_rows(right, left, coarse, halo), axis=0)
    far_rim = swap(rim, 2)
    rims = [rim, swap(rim, 1), far_rim, swap(far_rim, 1)]
    far = lax.ppermute(near, "groups", [(0, 1), (1, 0)])
    pairs = [near, far, swap(near, 1), swap(far, 1)]
    late_x = swap(after(late_w, far_latents), 2)

    edge_flops = 2 * edge_count * features * (2 * features + lanes + node_count)
    node_flops = 2 * node_count * features * 3 * features
    full_edge = shape((edge_count, features), BF16)
    full_node = shape((node_count, features), BF16)
    own_edge = shape((edge_count, part), F32)
    own_node = shape((node_count, part), F32)
    second_shape = pltpu.VMEM((hidden, features), BF16)
    edge_shape = pltpu.VMEM((edge_first.shape[1], hidden), BF16)
    node_shape = pltpu.VMEM((node_first.shape[1], hidden), BF16)

    edge_own, edge_full, node_own, node_full, right, left, coarse = call(
        first_kernel,
        [own_edge, full_edge, own_node, full_node] + sent(features),
        [(SMEM, spot)]
        + [(ANY, w) for w in list(weights) + core_w + pairs + shards + rims]
        + [(VMEM, a) for a in (edge_state, node_state, hot, incidence, wanted)],
        [
            edge_shape,
            second_shape,
            node_shape,
            second_shape,
            pltpu.VMEM((lanes, hidden), BF16),
            pltpu.VMEM((edge_count + table_rows, features), BF16),
            dma((32,)),
            dma((24,)),
        ],
        edge_flops + node_flops,
        "layer_0",
        16,
    )
    tables = [node_full] + neighbour_rows(right, left, coarse, halo)
    late_d = swap(after(late_x, *tables[1:]), 1)
    edge_own, node_own = call(
        functools.partial(late_kernel, len(tables)),
        [own_edge, own_node],
        [(SMEM, spot)]
        + [(ANY, w) for w in list(weights) + core_w + [late_x, late_d]]
        + [(VMEM, a) for a in (edge_full, edge_own, node_own)]
        + [(VMEM, t) for t in tables]
        + [(VMEM, hot), (VMEM, incidence)],
        [
            edge_shape,
            second_shape,
            node_shape,
            second_shape,
            pltpu.VMEM((lanes, hidden), BF16),
            pltpu.VMEM((table_rows, features), BF16),
            dma((14,)),
            dma((14,)),
        ],
        edge_flops + node_flops,
        "layer_1",
        16,
    )
    return (node_own, edge_own)


def solution(mesh):
    in_specs = (
        P(("groups", "graph"), "mp"),
        P(("groups", "graph"), "mp"),
        P(None, None, "mp"),
        P(None, "mp", None),
        P(None, None, "mp"),
        P(None, "mp", None),
        P("graph"),
        P("graph"),
        P("graph"),
    )
    out_specs = (P(("groups", "graph"), "mp"), P(("groups", "graph"), "mp"))
    return jax.shard_map(
        on_device, mesh=mesh, in_specs=in_specs, out_specs=out_specs, check_vma=False
    )
```

```python
import functools

import jax
import jax.numpy as jnp
from jax import lax
from jax.experimental import pallas as pl
from jax.experimental.pallas import tpu as pltpu
from jax.sharding import PartitionSpec as P

COARSE_DEV = 12
COARSE_PAD = 16
EPS = 1e-05
TILE = 256
F32 = jnp.float32
BF16 = jnp.bfloat16


def silu(x):
    half = 0.5 * x
    return half + half * jnp.tanh(half)


def normalize(msg):
    width = msg.shape[1]
    mean = jnp.sum(msg, axis=1, keepdims=True) * (1.0 / width)
    square = jnp.sum(msg * msg, axis=1, keepdims=True) * (1.0 / width)
    return (msg - mean) * lax.rsqrt(square - mean * mean + EPS)


def dot(a, b):
    return jnp.dot(a, b, preferred_element_type=F32)


def own_columns(full, part):
    mine = lax.axis_index("mp")
    out = full[:, 0:part]
    for j in range(1, full.shape[1] // part):
        out = jnp.where(mine == j, full[:, j * part : (j + 1) * part], out)
    return out


class Copies:
    def __init__(self, sems):
        self.sems, self.started = sems, []

    def start(self, source, target):
        copy = pltpu.make_async_copy(source, target, self.sems.at[len(self.started)])
        copy.start()
        self.started.append(copy)

    def wait(self):
        for copy in self.started:
            copy.wait()


def load_shard(copies, layer, first, second, j, first_ref, second_ref):
    part = second.shape[1]
    copies.start(first.at[layer], first_ref.at[:, pl.ds(j * part, part)])
    copies.start(second.at[layer], second_ref.at[pl.ds(j * part, part)])


def load_packed(copies, packed, base, j, first_ref, second_ref):
    rows = first_ref.shape[0]
    hidden, features = second_ref.shape
    part = hidden // 4
    copies.start(packed.at[pl.ds(base, rows)], first_ref.at[:, pl.ds(j * part, part)])
    for q in range(features // part):
        copies.start(
            packed.at[pl.ds(base + rows + q * part, part)],
            second_ref.at[pl.ds(j * part, part), pl.ds(q * part, part)],
        )


def load_half(copies, packed, base, half, j, first_ref, second_ref):
    rows = first_ref.shape[0] // 2
    hidden, features = second_ref.shape
    part = hidden // 4
    deep = part // 2
    at = pl.multiple_of(half * rows, rows)
    copies.start(packed.at[pl.ds(base, rows)], first_ref.at[pl.ds(at, rows), pl.ds(j * part, part)])
    at = pl.multiple_of(j * part + half * deep, deep)
    for q in range(features // part):
        copies.start(
            packed.at[pl.ds(base + rows + q * deep, deep)],
            second_ref.at[pl.ds(at, deep), pl.ds(q * part, part)],
        )
    return base + rows + features // part * deep


def ride_kernel(ef, es, nf, ns, ride_out, sems):
    y = lax.axis_index("groups")
    part, features = es.shape[1:]
    copies = Copies(sems)
    at = 0
    for first, second in ((ef, es), (nf, ns)):
        rows = first.shape[1] // 2
        source = first.at[0, pl.ds(pl.multiple_of(y * rows, rows), rows)]
        copies.start(source, ride_out.at[pl.ds(at, rows)])
        at += rows
        deep = part // 2
        for q in range(features // part):
            source = second.at[0, pl.ds(pl.multiple_of(y * deep, deep), deep), pl.ds(q * part, part)]
            copies.start(source, ride_out.at[pl.ds(at, deep)])
            at += deep
    copies.wait()


def one_hot(hit):
    return jnp.where(hit, 1.0, 0.0).astype(BF16)


def column(row):
    return jnp.broadcast_to(row, (8, row.shape[1])).T[:, 0:1]


def prepare_kernel(blocks, halo, table_rows, list_ref, ef, es, nf, ns, hot_out, incidence_out, pick_out, late_out, sems):
    part, features = es.shape[1:]
    edge_count, lanes_all = hot_out.shape
    node_count = incidence_out.shape[0]
    copies = Copies(sems)
    at = 0
    for first, second in ((ef, es), (nf, ns)):
        rows = first.shape[1]
        copies.start(first.at[1], late_out.at[pl.ds(at, rows)])
        at += rows
        for q in range(features // part):
            copies.start(second.at[1, :, pl.ds(q * part, part)], late_out.at[pl.ds(at, part)])
            at += part
    for at in range(0, edge_count, TILE):
        senders = table_index(list_ref[:, at : at + TILE], blocks, node_count, halo)
        receivers = list_ref[:, edge_count + at : edge_count + at + TILE]
        lanes = lax.broadcasted_iota(jnp.int32, (TILE, lanes_all), 1)
        hit = (lanes == column(senders)) | (lanes == column(receivers) + table_rows)
        hot_out[at : at + TILE, :] = one_hot(hit)
        node_ids = lax.broadcasted_iota(jnp.int32, (node_count, TILE), 0)
        incidence_out[:, at : at + TILE] = one_hot(node_ids == receivers)
    wanted = column(list_ref[:, 2 * edge_count : 2 * edge_count + 2 * halo])
    lanes = lax.broadcasted_iota(jnp.int32, (halo, node_count), 1)
    number = lax.broadcasted_iota(jnp.int32, (COARSE_PAD, node_count), 0)
    ids = lax.broadcasted_iota(jnp.int32, (COARSE_PAD, node_count), 1)
    coarse = one_hot((ids == number + (node_count - COARSE_DEV)) & (number < COARSE_DEV))
    wide = halo + COARSE_PAD
    pick_out[0:halo, :] = one_hot(lanes == wanted[halo:])
    pick_out[wide : wide + halo, :] = one_hot(lanes == wanted[:halo])
    for at in (halo, wide + halo, 2 * wide):
        pick_out[at : at + COARSE_PAD, :] = coarse
    copies.wait()


def pick_rows(pick_ref, node_bf, outs):
    picked = dot(pick_ref[...], node_bf).astype(BF16)
    start = 0
    for out in outs:
        out[...] = picked[start : start + out.shape[0]]
        start += out.shape[0]


def join_kernel(*refs):
    at = 0
    for piece in refs[:-1]:
        refs[-1][at : at + piece.shape[0], :] = piece[...]
        at += piece.shape[0]


def start_kernel(node_ref, pick_ref, right, left, coarse):
    pick_rows(pick_ref, node_ref[...].astype(BF16), (right, left, coarse))


def latent_kernel(edge_ref, node_ref, out):
    at = edge_ref.shape[0]
    out[0:at, :] = edge_ref[...].astype(BF16)
    out[at:, :] = node_ref[...].astype(BF16)


def edge_rows(edge_ref, table, nodes, own_ref, hot_ref, incidence_ref, first_ref, second_ref, product_ref, own_out, full_out):
    features = second_ref.shape[1]
    node_count = nodes.shape[0]
    table_rows = table.shape[0]
    lanes_all = product_ref.shape[0]
    used = table_rows + node_count
    part = own_ref.shape[1]
    product_ref[0:table_rows, :] = dot(table, first_ref[features : 2 * features, :]).astype(BF16)
    product_ref[table_rows:used, :] = dot(
        nodes, first_ref[2 * features : 3 * features, :]
    ).astype(BF16)
    if used < lanes_all:
        product_ref[used:, :] = jnp.zeros((lanes_all - used, features), BF16)
    incoming = jnp.zeros((node_count, features), F32)
    for at in range(0, own_ref.shape[0], TILE):
        rows = slice(at, at + TILE)
        edge_bf = edge_ref[rows, :]
        pre = dot(edge_bf, first_ref[0:features, :]) + dot(hot_ref[rows, :], product_ref[...])
        norm = normalize(dot(silu(pre).astype(BF16), second_ref[...]))
        edge_new = (edge_bf.astype(F32) + norm).astype(BF16)
        if full_out is not None:
            full_out[rows, :] = edge_new
        own_out[rows, :] = own_ref[rows, :] + own_columns(norm, part)
        incoming = incoming + dot(incidence_ref[:, rows], edge_new)
    return incoming.astype(BF16)


def node_rows(node_bf, incoming, own_ref, first_ref, second_ref, own_out):
    features = second_ref.shape[1]
    pre = dot(node_bf, first_ref[0:features, :]) + dot(incoming, first_ref[features:, :])
    norm = normalize(dot(silu(pre).astype(BF16), second_ref[...]))
    own_out[...] = own_ref[...] + own_columns(norm, own_ref.shape[1])
    return (node_bf.astype(F32) + norm).astype(BF16)


def first_kernel(*refs):
    refs = list(refs)
    own_w = [refs.pop(0) for _ in range(4)]
    core_w = [refs.pop(0) for _ in range(4)]
    halves = [[refs.pop(0) for _ in range(2)] for _ in range(2)]
    shards = [refs.pop(0) for _ in range(4)]
    rims = [refs.pop(0) for _ in range(4)]
    edge_own, node_own, hot_ref, incidence_ref, pick_ref = [refs.pop(0) for _ in range(5)]
    edge_out, full_out, node_out, node_full = [refs.pop(0) for _ in range(4)]
    sends = [refs.pop(0) for _ in range(3)]
    edge_w, edge_w2, node_w, node_w2, product_ref, x_ref, edge_sems, node_sems = refs
    part = edge_own.shape[1]
    edge_count = edge_own.shape[0]
    node_count = node_own.shape[0]
    edge_copies, node_copies = Copies(edge_sems), Copies(node_sems)
    for pieces, at in ((shards, 0), (rims, edge_count + node_count)):
        rows = pl.ds(at, pieces[0].shape[0])
        for j, shard in enumerate(pieces):
            column = pl.multiple_of((lax.axis_index("mp") ^ j) * part, part)
            edge_copies.start(shard, x_ref.at[rows, pl.ds(column, part)])
    y = lax.axis_index("groups")
    starts = [0, 0]
    for base, copies, (first, second), at in (
        (0, edge_copies, (edge_w, edge_w2), 0),
        (1, node_copies, (node_w, node_w2), 2),
    ):
        load_shard(copies, 0, own_w[at], own_w[at + 1], 0, first, second)
        load_shard(copies, 0, core_w[at], core_w[at + 1], 1, first, second)
        for j, pair in enumerate(halves):
            for k, piece in enumerate(pair):
                half = y if k == 0 else 1 - y
                end = load_half(copies, piece, starts[base], half, 2 + j, first, second)
        starts[1] = end
    edge_copies.wait()
    nodes = x_ref[edge_count : edge_count + node_count, :]
    incoming = edge_rows(
        x_ref, x_ref[edge_count:, :], nodes, edge_own, hot_ref, incidence_ref,
        edge_w, edge_w2, product_ref, edge_out, full_out,
    )
    node_copies.wait()
    node_new = node_rows(nodes, incoming, node_own, node_w, node_w2, node_out)
    node_full[...] = node_new
    pick_rows(pick_ref, node_new, sends)


def late_kernel(pieces, *refs):
    refs = list(refs)
    own_w = [refs.pop(0) for _ in range(4)]
    core_w = [refs.pop(0) for _ in range(4)]
    packed = [refs.pop(0) for _ in range(2)]
    edge_ref, edge_own, node_own = [refs.pop(0) for _ in range(3)]
    tables = [refs.pop(0) for _ in range(pieces)]
    hot_ref, incidence_ref, edge_out, node_out = [refs.pop(0) for _ in range(4)]
    edge_w, edge_w2, node_w, node_w2, product_ref, table_ref, edge_sems, node_sems = refs
    edge_copies, node_copies = Copies(edge_sems), Copies(node_sems)
    base = 0
    for copies, first, second, at in (
        (edge_copies, edge_w, edge_w2, 0),
        (node_copies, node_w, node_w2, 2),
    ):
        load_shard(copies, 1, own_w[at], own_w[at + 1], 0, first, second)
        load_shard(copies, 1, core_w[at], core_w[at + 1], 1, first, second)
        for j, pack in enumerate(packed):
            load_packed(copies, pack, base, 2 + j, first, second)
        base = edge_w.shape[0] + edge_w2.shape[1]
    start = 0
    for table in tables:
        table_ref[start : start + table.shape[0], :] = table[...]
        start += table.shape[0]
    edge_copies.wait()
    nodes = tables[0][...]
    incoming = edge_rows(
        edge_ref, table_ref[...], nodes, edge_own, hot_ref, incidence_ref,
        edge_w, edge_w2, product_ref, edge_out, None,
    )
    node_copies.wait()
    node_rows(nodes, incoming, node_own, node_w, node_w2, node_out)


SMEM, VMEM, ANY = pltpu.SMEM, pltpu.VMEM, pl.ANY


def call(kernel, out_shape, args, scratch, flops, name, vmem_mib=8):
    arrays = [a for _, a in args]
    moved = sum(a.size * a.dtype.itemsize for a in arrays + list(out_shape))
    return pl.pallas_call(
        kernel,
        out_shape=out_shape,
        in_specs=[pl.BlockSpec(memory_space=s) for s, _ in args],
        out_specs=[pl.BlockSpec(memory_space=VMEM)] * len(out_shape),
        scratch_shapes=scratch,
        compiler_params=pltpu.CompilerParams(vmem_limit_bytes=vmem_mib * 1024 * 1024),
        cost_estimate=pl.CostEstimate(flops=flops, bytes_accessed=moved, transcendentals=0),
        name=name,
    )(*arrays)


def swap(x, mask):
    size = lax.axis_size("mp")
    return lax.ppermute(x, "mp", [(i, i ^ mask) for i in range(size)])


def shift(x, by):
    size = lax.axis_size("graph")
    return lax.ppermute(x, "graph", [(i, (i + by) % size) for i in range(size)])


def after(x, *others):
    return lax.optimization_barrier((x, *others))[0]


def neighbour_rows(right, left, coarse, halo):
    if lax.axis_size("graph") == 4:
        return [shift(right, 1), shift(left, -1), shift(coarse, 2)]
    everyone = lax.all_gather(coarse, "graph", axis=0, tiled=True)
    return [shift(right[:halo], 1), shift(left[:halo], -1), everyone]


def table_index(senders, size, node_count, halo):
    coarse_start = node_count + 2 * halo
    number = jnp.maximum(senders - coarse_start, 0)
    block = (number * 43691) >> 19
    row = number - block * COARSE_DEV
    if size != 4:
        return jnp.where(senders < coarse_start, senders, coarse_start + block * COARSE_PAD + row)
    wide = halo + COARSE_PAD
    away = (block - lax.axis_index("graph")) & 3
    starts = (node_count - COARSE_DEV, node_count + wide + halo, node_count + 2 * wide, node_count + halo)
    base = jnp.where(
        away < 2,
        jnp.where(away == 0, starts[0], starts[1]),
        jnp.where(away == 2, starts[2], starts[3]),
    )
    fine = jnp.where(senders < node_count + halo, senders, senders + COARSE_PAD)
    return jnp.where(senders < coarse_start, fine, base + row)


def on_device(
    node_state,
    edge_state,
    edge_first,
    edge_second,
    node_first,
    node_second,
    senders,
    receivers,
    boundary_rows,
):
    node_count, part = node_state.shape
    edge_count = edge_state.shape[0]
    features = edge_second.shape[2]
    hidden = 4 * part
    halo = boundary_rows.shape[0] // 2
    blocks = lax.axis_size("graph")
    shape = jax.ShapeDtypeStruct
    dma = pltpu.SemaphoreType.DMA

    wide = halo + COARSE_PAD

    def sent(width):
        return [shape((n, width), BF16) for n in (wide, wide, COARSE_PAD)]

    weights = (edge_first, edge_second, node_first, node_second)
    edge_pack = edge_first.shape[1] + features
    node_pack = node_first.shape[1] + features
    (ride,) = call(
        ride_kernel,
        [shape(((edge_pack + node_pack) // 2, part), BF16)],
        [(ANY, w) for w in weights],
        [dma((10,))],
        0,
        "layer_0_half",
        60,
    )
    near = swap(ride, 2)
    far_rows = 2 * wide + COARSE_PAD if blocks == 4 else 2 * halo + blocks * COARSE_PAD
    table_rows = node_count + far_rows
    lanes = -(-(table_rows + node_count) // 128) * 128
    lists = jnp.concatenate([senders, receivers, boundary_rows])[None, :]
    hot, incidence, pick, late_w = call(
        functools.partial(prepare_kernel, blocks, halo, table_rows),
        [
            shape((edge_count, lanes), BF16),
            shape((node_count, edge_count), BF16),
            shape((2 * wide + COARSE_PAD, node_count), BF16),
            shape((edge_pack + node_pack, part), BF16),
        ],
        [(VMEM, after(lists, ride))] + [(ANY, w) for w in weights],
        [dma((10,))],
        0,
        "one_hot",
    )
    core_w = [swap(after(w, ride), 1) for w in weights]
    (latents,) = call(
        latent_kernel,
        [shape((edge_count + node_count, part), BF16)],
        [(VMEM, after(edge_state, late_w)), (VMEM, node_state)],
        [],
        0,
        "latents",
    )
    right, left, coarse = call(
        start_kernel,
        sent(part),
        [(VMEM, node_state), (VMEM, after(pick, latents))],
        [],
        2 * pick.size * part,
        "boundary_rows",
    )
    (rim,) = call(
        join_kernel,
        [shape((far_rows, part), BF16)],
        [(VMEM, r) for r in neighbour_rows(right, left, coarse, halo)],
        [],
        0,
        "halo_rows",
    )
    far_latents = swap(after(latents, near, rim), 2)
    far = lax.ppermute(near, "groups", [(0, 1), (1, 0)])
    far_rim = swap(rim, 2)
    shards = [latents, swap(latents, 1), far_latents, swap(after(far_latents, far, far_rim), 1)]
    rims = [rim, swap(rim, 1), far_rim, swap(far_rim, 1)]
    pairs = [near, far, swap(near, 1), swap(far, 1)]
    late_x = swap(after(late_w, far_latents), 2)

    edge_flops = 2 * edge_count * features * (2 * features + lanes + node_count)
    node_flops = 2 * node_count * features * 3 * features
    full_edge = shape((edge_count, features), BF16)
    full_node = shape((node_count, features), BF16)
    own_edge = shape((edge_count, part), F32)
    own_node = shape((node_count, part), F32)
    second_shape = pltpu.VMEM((hidden, features), BF16)
    edge_shape = pltpu.VMEM((edge_first.shape[1], hidden), BF16)
    node_shape = pltpu.VMEM((node_first.shape[1], hidden), BF16)

    edge_own, edge_full, node_own, node_full, right, left, coarse = call(
        first_kernel,
        [own_edge, full_edge, own_node, full_node] + sent(features),
        [(ANY, w) for w in list(weights) + core_w + pairs + shards + rims]
        + [(VMEM, a) for a in (edge_state, node_state, hot, incidence, pick)],
        [
            edge_shape,
            second_shape,
            node_shape,
            second_shape,
            pltpu.VMEM((lanes, hidden), BF16),
            pltpu.VMEM((edge_count + table_rows, features), BF16),
            dma((32,)),
            dma((24,)),
        ],
        edge_flops + node_flops,
        "layer_0",
        16,
    )
    tables = [node_full] + neighbour_rows(right, left, coarse, halo)
    late_d = swap(after(late_x, *tables[1:]), 1)
    edge_own, node_own = call(
        functools.partial(late_kernel, len(tables)),
        [own_edge, own_node],
        [(ANY, w) for w in list(weights) + core_w + [late_x, late_d]]
        + [(VMEM, a) for a in (edge_full, edge_own, node_own)]
        + [(VMEM, t) for t in tables]
        + [(VMEM, hot), (VMEM, incidence)],
        [
            edge_shape,
            second_shape,
            node_shape,
            second_shape,
            pltpu.VMEM((lanes, hidden), BF16),
            pltpu.VMEM((table_rows, features), BF16),
            dma((14,)),
            dma((14,)),
        ],
        edge_flops + node_flops,
        "layer_1",
        16,
    )
    return (node_own, edge_own)


def solution(mesh):
    in_specs = (
        P(("groups", "graph"), "mp"),
        P(("groups", "graph"), "mp"),
        P(None, None, "mp"),
        P(None, "mp", None),
        P(None, None, "mp"),
        P(None, "mp", None),
        P("graph"),
        P("graph"),
        P("graph"),
    )
    out_specs = (P(("groups", "graph"), "mp"), P(("groups", "graph"), "mp"))
    return jax.shard_map(
        on_device, mesh=mesh, in_specs=in_specs, out_specs=out_specs, check_vma=False
    )
```

```python
import functools

import jax
import jax.numpy as jnp
from jax import lax
from jax.experimental import pallas as pl
from jax.experimental.pallas import tpu as pltpu
from jax.sharding import PartitionSpec as P

COARSE_DEV = 12
COARSE_PAD = 16
EPS = 1e-05
TILE = 256
F32 = jnp.float32
BF16 = jnp.bfloat16


def silu(x):
    half = 0.5 * x
    return half + half * jnp.tanh(half)


def normalize(msg):
    width = msg.shape[1]
    mean = jnp.sum(msg, axis=1, keepdims=True) * (1.0 / width)
    square = jnp.sum(msg * msg, axis=1, keepdims=True) * (1.0 / width)
    return (msg - mean) * lax.rsqrt(square - mean * mean + EPS)


def dot(a, b):
    return jnp.dot(a, b, preferred_element_type=F32)


def own_columns(full, part):
    mine = lax.axis_index("mp")
    out = full[:, 0:part]
    for j in range(1, full.shape[1] // part):
        out = jnp.where(mine == j, full[:, j * part : (j + 1) * part], out)
    return out


class Copies:
    def __init__(self, sems):
        self.sems, self.started = sems, []

    def start(self, source, target):
        copy = pltpu.make_async_copy(source, target, self.sems.at[len(self.started)])
        copy.start()
        self.started.append(copy)

    def wait(self):
        for copy in self.started:
            copy.wait()


class Moves:
    def start(self, source, target):
        target[...] = source[...]

    def wait(self):
        pass


def load_shard(copies, layer, first, second, j, first_ref, second_ref):
    part = second.shape[1]
    copies.start(first.at[layer], first_ref.at[:, pl.ds(j * part, part)])
    copies.start(second.at[layer], second_ref.at[pl.ds(j * part, part)])


def load_packed(copies, packed, base, j, first_ref, second_ref):
    rows = first_ref.shape[0]
    hidden, features = second_ref.shape
    part = hidden // 4
    copies.start(packed.at[pl.ds(base, rows)], first_ref.at[:, pl.ds(j * part, part)])
    for q in range(features // part):
        copies.start(
            packed.at[pl.ds(base + rows + q * part, part)],
            second_ref.at[pl.ds(j * part, part), pl.ds(q * part, part)],
        )


def load_half(copies, packed, base, half, j, first_ref, second_ref):
    rows = first_ref.shape[0] // 2
    hidden, features = second_ref.shape
    part = hidden // 4
    deep = part // 2
    at = pl.multiple_of(half * rows, rows)
    copies.start(packed.at[pl.ds(base, rows)], first_ref.at[pl.ds(at, rows), pl.ds(j * part, part)])
    at = pl.multiple_of(j * part + half * deep, deep)
    for q in range(features // part):
        copies.start(
            packed.at[pl.ds(base + rows + q * deep, deep)],
            second_ref.at[pl.ds(at, deep), pl.ds(q * part, part)],
        )
    return base + rows + features // part * deep


def ride_kernel(ef, es, nf, ns, ride_out, sems):
    y = lax.axis_index("groups")
    part, features = es.shape[1:]
    copies = Copies(sems)
    at = 0
    for first, second in ((ef, es), (nf, ns)):
        rows = first.shape[1] // 2
        source = first.at[0, pl.ds(pl.multiple_of(y * rows, rows), rows)]
        copies.start(source, ride_out.at[pl.ds(at, rows)])
        at += rows
        deep = part // 2
        for q in range(features // part):
            source = second.at[0, pl.ds(pl.multiple_of(y * deep, deep), deep), pl.ds(q * part, part)]
            copies.start(source, ride_out.at[pl.ds(at, deep)])
            at += deep
    copies.wait()


def one_hot(hit):
    return jnp.where(hit, 1.0, 0.0).astype(BF16)


def column(row):
    return jnp.broadcast_to(row, (8, row.shape[1])).T[:, 0:1]


def prepare_kernel(blocks, halo, table_rows, list_ref, ef, es, nf, ns, hot_out, incidence_out, pick_out, late_out, sems):
    part, features = es.shape[1:]
    edge_count, lanes_all = hot_out.shape
    node_count = incidence_out.shape[0]
    copies = Copies(sems)
    at = 0
    for first, second in ((ef, es), (nf, ns)):
        rows = first.shape[1]
        copies.start(first.at[1], late_out.at[pl.ds(at, rows)])
        at += rows
        for q in range(features // part):
            copies.start(second.at[1, :, pl.ds(q * part, part)], late_out.at[pl.ds(at, part)])
            at += part
    for at in range(0, edge_count, TILE):
        senders = table_index(list_ref[:, at : at + TILE], blocks, node_count, halo)
        receivers = list_ref[:, edge_count + at : edge_count + at + TILE]
        lanes = lax.broadcasted_iota(jnp.int32, (TILE, lanes_all), 1)
        hit = (lanes == column(senders)) | (lanes == column(receivers) + table_rows)
        hot_out[at : at + TILE, :] = one_hot(hit)
        node_ids = lax.broadcasted_iota(jnp.int32, (node_count, TILE), 0)
        incidence_out[:, at : at + TILE] = one_hot(node_ids == receivers)
    wanted = column(list_ref[:, 2 * edge_count : 2 * edge_count + 2 * halo])
    lanes = lax.broadcasted_iota(jnp.int32, (halo, node_count), 1)
    number = lax.broadcasted_iota(jnp.int32, (COARSE_PAD, node_count), 0)
    ids = lax.broadcasted_iota(jnp.int32, (COARSE_PAD, node_count), 1)
    coarse = one_hot((ids == number + (node_count - COARSE_DEV)) & (number < COARSE_DEV))
    wide = halo + COARSE_PAD
    pick_out[0:halo, :] = one_hot(lanes == wanted[halo:])
    pick_out[wide : wide + halo, :] = one_hot(lanes == wanted[:halo])
    for at in (halo, wide + halo, 2 * wide):
        pick_out[at : at + COARSE_PAD, :] = coarse
    copies.wait()


def pick_rows(pick_ref, node_bf, outs):
    picked = dot(pick_ref[...], node_bf).astype(BF16)
    start = 0
    for out in outs:
        out[...] = picked[start : start + out.shape[0]]
        start += out.shape[0]


def start_kernel(node_ref, pick_ref, right, left, coarse):
    pick_rows(pick_ref, node_ref[...].astype(BF16), (right, left, coarse))


def latent_kernel(*refs):
    out = refs[-1]
    at = 0
    for piece in refs[:-1]:
        out[at : at + piece.shape[0], :] = piece[...].astype(BF16)
        at += piece.shape[0]


def edge_rows(edge_ref, table, nodes, own_ref, hot_ref, incidence_ref, first_ref, second_ref, product_ref, own_out, full_out):
    features = second_ref.shape[1]
    node_count = nodes.shape[0]
    table_rows = table.shape[0]
    lanes_all = product_ref.shape[0]
    used = table_rows + node_count
    part = own_ref.shape[1]
    product_ref[0:table_rows, :] = dot(table, first_ref[features : 2 * features, :]).astype(BF16)
    product_ref[table_rows:used, :] = dot(
        nodes, first_ref[2 * features : 3 * features, :]
    ).astype(BF16)
    if used < lanes_all:
        product_ref[used:, :] = jnp.zeros((lanes_all - used, features), BF16)
    incoming = jnp.zeros((node_count, features), F32)
    for at in range(0, own_ref.shape[0], TILE):
        rows = slice(at, at + TILE)
        edge_bf = edge_ref[rows, :]
        pre = dot(edge_bf, first_ref[0:features, :]) + dot(hot_ref[rows, :], product_ref[...])
        norm = normalize(dot(silu(pre).astype(BF16), second_ref[...]))
        edge_new = (edge_bf.astype(F32) + norm).astype(BF16)
        if full_out is not None:
            full_out[rows, :] = edge_new
        own_out[rows, :] = own_ref[rows, :] + own_columns(norm, part)
        incoming = incoming + dot(incidence_ref[:, rows], edge_new)
    return incoming.astype(BF16)


def node_rows(node_bf, incoming, own_ref, first_ref, second_ref, own_out):
    features = second_ref.shape[1]
    pre = dot(node_bf, first_ref[0:features, :]) + dot(incoming, first_ref[features:, :])
    norm = normalize(dot(silu(pre).astype(BF16), second_ref[...]))
    own_out[...] = own_ref[...] + own_columns(norm, own_ref.shape[1])
    return (node_bf.astype(F32) + norm).astype(BF16)


def first_kernel(*refs):
    refs = list(refs)
    own_w = [refs.pop(0) for _ in range(4)]
    core_w = [refs.pop(0) for _ in range(4)]
    halves = [[refs.pop(0) for _ in range(2)] for _ in range(2)]
    shards = [refs.pop(0) for _ in range(4)]
    edge_own, node_own, hot_ref, incidence_ref, pick_ref = [refs.pop(0) for _ in range(5)]
    edge_out, full_out, node_out, node_full = [refs.pop(0) for _ in range(4)]
    sends = [refs.pop(0) for _ in range(3)]
    edge_w, edge_w2, node_w, node_w2, product_ref, x_ref = refs
    part = edge_own.shape[1]
    edge_count = edge_own.shape[0]
    node_count = node_own.shape[0]
    edge_copies, node_copies = Moves(), Moves()
    for j, shard in enumerate(shards):
        column = pl.multiple_of((lax.axis_index("mp") ^ j) * part, part)
        edge_copies.start(shard, x_ref.at[:, pl.ds(column, part)])
    y = lax.axis_index("groups")
    starts = [0, 0]
    for base, copies, (first, second), at in (
        (0, edge_copies, (edge_w, edge_w2), 0),
        (1, node_copies, (node_w, node_w2), 2),
    ):
        load_shard(copies, 0, own_w[at], own_w[at + 1], 0, first, second)
        load_shard(copies, 0, core_w[at], core_w[at + 1], 1, first, second)
        for j, pair in enumerate(halves):
            for k, piece in enumerate(pair):
                half = y if k == 0 else 1 - y
                end = load_half(copies, piece, starts[base], half, 2 + j, first, second)
        starts[1] = end
    edge_copies.wait()
    nodes = x_ref[edge_count : edge_count + node_count, :]
    incoming = edge_rows(
        x_ref, x_ref[edge_count:, :], nodes, edge_own, hot_ref, incidence_ref,
        edge_w, edge_w2, product_ref, edge_out, full_out,
    )
    node_copies.wait()
    node_new = node_rows(nodes, incoming, node_own, node_w, node_w2, node_out)
    node_full[...] = node_new
    pick_rows(pick_ref, node_new, sends)


def late_kernel(pieces, *refs):
    refs = list(refs)
    own_w = [refs.pop(0) for _ in range(4)]
    core_w = [refs.pop(0) for _ in range(4)]
    packed = [refs.pop(0) for _ in range(2)]
    edge_ref, edge_own, node_own = [refs.pop(0) for _ in range(3)]
    tables = [refs.pop(0) for _ in range(pieces)]
    hot_ref, incidence_ref, edge_out, node_out = [refs.pop(0) for _ in range(4)]
    edge_w, edge_w2, node_w, node_w2, product_ref, table_ref = refs
    edge_copies, node_copies = Moves(), Moves()
    base = 0
    for copies, first, second, at in (
        (edge_copies, edge_w, edge_w2, 0),
        (node_copies, node_w, node_w2, 2),
    ):
        load_shard(copies, 1, own_w[at], own_w[at + 1], 0, first, second)
        load_shard(copies, 1, core_w[at], core_w[at + 1], 1, first, second)
        for j, pack in enumerate(packed):
            load_packed(copies, pack, base, 2 + j, first, second)
        base = edge_w.shape[0] + edge_w2.shape[1]
    start = 0
    for table in tables:
        table_ref[start : start + table.shape[0], :] = table[...]
        start += table.shape[0]
    edge_copies.wait()
    nodes = tables[0][...]
    incoming = edge_rows(
        edge_ref, table_ref[...], nodes, edge_own, hot_ref, incidence_ref,
        edge_w, edge_w2, product_ref, edge_out, None,
    )
    node_copies.wait()
    node_rows(nodes, incoming, node_own, node_w, node_w2, node_out)


SMEM, VMEM, ANY = pltpu.SMEM, pltpu.VMEM, pl.ANY


def call(kernel, out_shape, args, scratch, flops, name, vmem_mib=8):
    arrays = [a for _, a in args]
    moved = sum(a.size * a.dtype.itemsize for a in arrays + list(out_shape))
    return pl.pallas_call(
        kernel,
        out_shape=out_shape,
        in_specs=[pl.BlockSpec(memory_space=s) for s, _ in args],
        out_specs=[pl.BlockSpec(memory_space=VMEM)] * len(out_shape),
        scratch_shapes=scratch,
        compiler_params=pltpu.CompilerParams(vmem_limit_bytes=vmem_mib * 1024 * 1024),
        cost_estimate=pl.CostEstimate(flops=flops, bytes_accessed=moved, transcendentals=0),
        name=name,
    )(*arrays)


def swap(x, mask):
    size = lax.axis_size("mp")
    return lax.ppermute(x, "mp", [(i, i ^ mask) for i in range(size)])


def shift(x, by):
    size = lax.axis_size("graph")
    return lax.ppermute(x, "graph", [(i, (i + by) % size) for i in range(size)])


def after(x, *others):
    return lax.optimization_barrier((x, *others))[0]


def neighbour_rows(right, left, coarse, halo):
    if lax.axis_size("graph") == 4:
        return [shift(right, 1), shift(left, -1), shift(coarse, 2)]
    everyone = lax.all_gather(coarse, "graph", axis=0, tiled=True)
    return [shift(right[:halo], 1), shift(left[:halo], -1), everyone]


def table_index(senders, size, node_count, halo):
    coarse_start = node_count + 2 * halo
    number = jnp.maximum(senders - coarse_start, 0)
    block = (number * 43691) >> 19
    row = number - block * COARSE_DEV
    if size != 4:
        return jnp.where(senders < coarse_start, senders, coarse_start + block * COARSE_PAD + row)
    wide = halo + COARSE_PAD
    away = (block - lax.axis_index("graph")) & 3
    starts = (node_count - COARSE_DEV, node_count + wide + halo, node_count + 2 * wide, node_count + halo)
    base = jnp.where(
        away < 2,
        jnp.where(away == 0, starts[0], starts[1]),
        jnp.where(away == 2, starts[2], starts[3]),
    )
    fine = jnp.where(senders < node_count + halo, senders, senders + COARSE_PAD)
    return jnp.where(senders < coarse_start, fine, base + row)


def on_device(
    node_state,
    edge_state,
    edge_first,
    edge_second,
    node_first,
    node_second,
    senders,
    receivers,
    boundary_rows,
):
    node_count, part = node_state.shape
    edge_count = edge_state.shape[0]
    features = edge_second.shape[2]
    hidden = 4 * part
    halo = boundary_rows.shape[0] // 2
    blocks = lax.axis_size("graph")
    shape = jax.ShapeDtypeStruct
    dma = pltpu.SemaphoreType.DMA

    wide = halo + COARSE_PAD

    def sent(width):
        return [shape((n, width), BF16) for n in (wide, wide, COARSE_PAD)]

    weights = (edge_first, edge_second, node_first, node_second)
    edge_pack = edge_first.shape[1] + features
    node_pack = node_first.shape[1] + features
    (ride,) = call(
        ride_kernel,
        [shape(((edge_pack + node_pack) // 2, part), BF16)],
        [(ANY, w) for w in weights],
        [dma((10,))],
        0,
        "layer_0_half",
        60,
    )
    near = swap(ride, 2)
    far_rows = 2 * wide + COARSE_PAD if blocks == 4 else 2 * halo + blocks * COARSE_PAD
    table_rows = node_count + far_rows
    lanes = -(-(table_rows + node_count) // 128) * 128
    lists = jnp.concatenate([senders, receivers, boundary_rows])[None, :]
    hot, incidence, pick, late_w = call(
        functools.partial(prepare_kernel, blocks, halo, table_rows),
        [
            shape((edge_count, lanes), BF16),
            shape((node_count, edge_count), BF16),
            shape((2 * wide + COARSE_PAD, node_count), BF16),
            shape((edge_pack + node_pack, part), BF16),
        ],
        [(VMEM, after(lists, ride))] + [(ANY, w) for w in weights],
        [dma((10,))],
        0,
        "one_hot",
    )
    core_w = [swap(after(w, ride), 1) for w in weights]
    right, left, coarse = call(
        start_kernel,
        sent(part),
        [(VMEM, node_state), (VMEM, pick)],
        [],
        2 * pick.size * part,
        "boundary_rows",
    )
    rows = neighbour_rows(right, left, coarse, halo)
    (latents,) = call(
        latent_kernel,
        [shape((edge_count + table_rows, part), BF16)],
        [(VMEM, after(edge_state, late_w)), (VMEM, node_state)] + [(VMEM, r) for r in rows],
        [],
        0,
        "latents",
    )
    far_latents = swap(after(latents, near, *core_w), 2)
    far = lax.ppermute(near, "groups", [(0, 1), (1, 0)])
    shards = [latents, swap(latents, 1), far_latents, swap(after(far_latents, far), 1)]
    pairs = [near, far, swap(near, 1), swap(far, 1)]
    late_x = swap(after(late_w, far_latents, far), 2)

    edge_flops = 2 * edge_count * features * (2 * features + lanes + node_count)
    node_flops = 2 * node_count * features * 3 * features
    full_edge = shape((edge_count, features), BF16)
    full_node = shape((node_count, features), BF16)
    own_edge = shape((edge_count, part), F32)
    own_node = shape((node_count, part), F32)
    second_shape = pltpu.VMEM((hidden, features), BF16)
    edge_shape = pltpu.VMEM((edge_first.shape[1], hidden), BF16)
    node_shape = pltpu.VMEM((node_first.shape[1], hidden), BF16)

    edge_own, edge_full, node_own, node_full, right, left, coarse = call(
        first_kernel,
        [own_edge, full_edge, own_node, full_node] + sent(features),
        [(VMEM, w) for w in list(weights) + core_w + pairs + shards]
        + [(VMEM, a) for a in (edge_state, node_state, hot, incidence, pick)],
        [
            edge_shape,
            second_shape,
            node_shape,
            second_shape,
            pltpu.VMEM((lanes, hidden), BF16),
            pltpu.VMEM((edge_count + table_rows, features), BF16),
        ],
        edge_flops + node_flops,
        "layer_0",
        16,
    )
    tables = [node_full] + neighbour_rows(right, left, coarse, halo)
    late_d = swap(after(late_x, *tables[1:]), 1)
    edge_own, node_own = call(
        functools.partial(late_kernel, len(tables)),
        [own_edge, own_node],
        [(VMEM, w) for w in list(weights) + core_w + [late_x, late_d]]
        + [(VMEM, a) for a in (edge_full, edge_own, node_own)]
        + [(VMEM, t) for t in tables]
        + [(VMEM, hot), (VMEM, incidence)],
        [
            edge_shape,
            second_shape,
            node_shape,
            second_shape,
            pltpu.VMEM((lanes, hidden), BF16),
            pltpu.VMEM((table_rows, features), BF16),
        ],
        edge_flops + node_flops,
        "layer_1",
        16,
    )
    return (node_own, edge_own)


def solution(mesh):
    in_specs = (
        P(("groups", "graph"), "mp"),
        P(("groups", "graph"), "mp"),
        P(None, None, "mp"),
        P(None, "mp", None),
        P(None, None, "mp"),
        P(None, "mp", None),
        P("graph"),
        P("graph"),
        P("graph"),
    )
    out_specs = (P(("groups", "graph"), "mp"), P(("groups", "graph"), "mp"))
    return jax.shard_map(
        on_device, mesh=mesh, in_specs=in_specs, out_specs=out_specs, check_vma=False
    )
```

```python
import functools

import jax
import jax.numpy as jnp
from jax import lax
from jax.experimental import pallas as pl
from jax.experimental.pallas import tpu as pltpu
from jax.sharding import PartitionSpec as P

COARSE_DEV = 12
COARSE_PAD = 16
EPS = 1e-05
TILE = 256
F32 = jnp.float32
BF16 = jnp.bfloat16


def silu(x):
    half = 0.5 * x
    return half + half * jnp.tanh(half)


def normalize(msg):
    width = msg.shape[1]
    mean = jnp.sum(msg, axis=1, keepdims=True) * (1.0 / width)
    square = jnp.sum(msg * msg, axis=1, keepdims=True) * (1.0 / width)
    return (msg - mean) * lax.rsqrt(square - mean * mean + EPS)


def dot(a, b):
    return jnp.dot(a, b, preferred_element_type=F32)


def own_columns(full, part):
    mine = lax.axis_index("mp")
    out = full[:, 0:part]
    for j in range(1, full.shape[1] // part):
        out = jnp.where(mine == j, full[:, j * part : (j + 1) * part], out)
    return out


class Copies:
    def __init__(self, sems):
        self.sems, self.started = sems, []

    def start(self, source, target):
        copy = pltpu.make_async_copy(source, target, self.sems.at[len(self.started)])
        copy.start()
        self.started.append(copy)

    def wait(self):
        for copy in self.started:
            copy.wait()


class Moves:
    def start(self, source, target):
        target[...] = source[...]

    def wait(self):
        pass


def load_shard(copies, layer, first, second, j, first_ref, second_ref):
    part = second.shape[1]
    copies.start(first.at[layer], first_ref.at[:, pl.ds(j * part, part)])
    copies.start(second.at[layer], second_ref.at[pl.ds(j * part, part)])


def load_packed(copies, packed, j, first_ref, second_ref):
    rows = first_ref.shape[0]
    hidden, features = second_ref.shape
    part = hidden // 4
    copies.start(packed.at[pl.ds(0, rows)], first_ref.at[:, pl.ds(j * part, part)])
    for q in range(features // part):
        copies.start(
            packed.at[pl.ds(rows + q * part, part)],
            second_ref.at[pl.ds(j * part, part), pl.ds(q * part, part)],
        )


def load_half(copies, packed, half, j, first_ref, second_ref):
    rows = first_ref.shape[0] // 2
    hidden, features = second_ref.shape
    part = hidden // 4
    deep = part // 2
    at = pl.multiple_of(half * rows, rows)
    copies.start(packed.at[pl.ds(0, rows)], first_ref.at[pl.ds(at, rows), pl.ds(j * part, part)])
    at = pl.multiple_of(j * part + half * deep, deep)
    for q in range(features // part):
        copies.start(
            packed.at[pl.ds(rows + q * deep, deep)],
            second_ref.at[pl.ds(at, deep), pl.ds(q * part, part)],
        )


def ride_kernel(ef, es, nf, ns, edge_out, node_out, sems):
    y = lax.axis_index("groups")
    part, features = es.shape[1:]
    copies = Copies(sems)
    for first, second, out in ((ef, es, edge_out), (nf, ns, node_out)):
        rows = first.shape[1] // 2
        source = first.at[0, pl.ds(pl.multiple_of(y * rows, rows), rows)]
        copies.start(source, out.at[pl.ds(0, rows)])
        deep = part // 2
        for q in range(features // part):
            source = second.at[0, pl.ds(pl.multiple_of(y * deep, deep), deep), pl.ds(q * part, part)]
            copies.start(source, out.at[pl.ds(rows + q * deep, deep)])
    copies.wait()


def one_hot(hit):
    return jnp.where(hit, 1.0, 0.0).astype(BF16)


def column(row):
    return jnp.broadcast_to(row, (8, row.shape[1])).T[:, 0:1]


def prepare_kernel(blocks, halo, table_rows, list_ref, ef, es, nf, ns, hot_out, incidence_out, pick_out, edge_late, node_late, sems):
    part, features = es.shape[1:]
    edge_count, lanes_all = hot_out.shape
    node_count = incidence_out.shape[0]
    copies = Copies(sems)
    for first, second, out in ((ef, es, edge_late), (nf, ns, node_late)):
        rows = first.shape[1]
        copies.start(first.at[1], out.at[pl.ds(0, rows)])
        for q in range(features // part):
            copies.start(second.at[1, :, pl.ds(q * part, part)], out.at[pl.ds(rows + q * part, part)])
    for at in range(0, edge_count, TILE):
        senders = table_index(list_ref[:, at : at + TILE], blocks, node_count, halo)
        receivers = list_ref[:, edge_count + at : edge_count + at + TILE]
        lanes = lax.broadcasted_iota(jnp.int32, (TILE, lanes_all), 1)
        hit = (lanes == column(senders)) | (lanes == column(receivers) + table_rows)
        hot_out[at : at + TILE, :] = one_hot(hit)
        node_ids = lax.broadcasted_iota(jnp.int32, (node_count, TILE), 0)
        incidence_out[:, at : at + TILE] = one_hot(node_ids == receivers)
    wanted = column(list_ref[:, 2 * edge_count : 2 * edge_count + 2 * halo])
    lanes = lax.broadcasted_iota(jnp.int32, (halo, node_count), 1)
    number = lax.broadcasted_iota(jnp.int32, (COARSE_PAD, node_count), 0)
    ids = lax.broadcasted_iota(jnp.int32, (COARSE_PAD, node_count), 1)
    coarse = one_hot((ids == number + (node_count - COARSE_DEV)) & (number < COARSE_DEV))
    wide = halo + COARSE_PAD
    pick_out[0:halo, :] = one_hot(lanes == wanted[halo:])
    pick_out[wide : wide + halo, :] = one_hot(lanes == wanted[:halo])
    for at in (halo, wide + halo, 2 * wide):
        pick_out[at : at + COARSE_PAD, :] = coarse
    copies.wait()


def pick_rows(pick_ref, node_bf, outs):
    picked = dot(pick_ref[...], node_bf).astype(BF16)
    start = 0
    for out in outs:
        out[...] = picked[start : start + out.shape[0]]
        start += out.shape[0]


def join_kernel(*refs):
    at = 0
    for piece in refs[:-1]:
        refs[-1][at : at + piece.shape[0], :] = piece[...]
        at += piece.shape[0]


def start_kernel(node_ref, pick_ref, right, left, coarse):
    pick_rows(pick_ref, node_ref[...].astype(BF16), (right, left, coarse))


def latent_kernel(*refs):
    out = refs[-1]
    at = 0
    for piece in refs[:-1]:
        out[at : at + piece.shape[0], :] = piece[...].astype(BF16)
        at += piece.shape[0]


def edge_rows(edge_ref, table, nodes, own_ref, hot_ref, incidence_ref, first_ref, second_ref, product_ref, own_out, full_out):
    features = second_ref.shape[1]
    node_count = nodes.shape[0]
    table_rows = table.shape[0]
    lanes_all = product_ref.shape[0]
    used = table_rows + node_count
    part = own_ref.shape[1]
    product_ref[0:table_rows, :] = dot(table, first_ref[features : 2 * features, :]).astype(BF16)
    product_ref[table_rows:used, :] = dot(
        nodes, first_ref[2 * features : 3 * features, :]
    ).astype(BF16)
    if used < lanes_all:
        product_ref[used:, :] = jnp.zeros((lanes_all - used, features), BF16)
    incoming = jnp.zeros((node_count, features), F32)
    for at in range(0, own_ref.shape[0], TILE):
        rows = slice(at, at + TILE)
        edge_bf = edge_ref[rows, :]
        pre = dot(edge_bf, first_ref[0:features, :]) + dot(hot_ref[rows, :], product_ref[...])
        norm = normalize(dot(silu(pre).astype(BF16), second_ref[...]))
        edge_new = (edge_bf.astype(F32) + norm).astype(BF16)
        if full_out is not None:
            full_out[rows, :] = edge_new
        own_out[rows, :] = own_ref[rows, :] + own_columns(norm, part)
        incoming = incoming + dot(incidence_ref[:, rows], edge_new)
    return incoming.astype(BF16)


def node_rows(node_bf, incoming, own_ref, first_ref, second_ref, own_out):
    features = second_ref.shape[1]
    pre = dot(node_bf, first_ref[0:features, :]) + dot(incoming, first_ref[features:, :])
    norm = normalize(dot(silu(pre).astype(BF16), second_ref[...]))
    own_out[...] = own_ref[...] + own_columns(norm, own_ref.shape[1])
    return (node_bf.astype(F32) + norm).astype(BF16)


def first_kernel(*refs):
    refs = list(refs)
    own_w = [refs.pop(0) for _ in range(4)]
    core_w = [refs.pop(0) for _ in range(4)]
    halves = [[[refs.pop(0) for _ in range(2)] for _ in range(2)] for _ in range(2)]
    shards = [refs.pop(0) for _ in range(4)]
    rims = [refs.pop(0) for _ in range(4)]
    edge_own, node_own, hot_ref, incidence_ref, pick_ref = [refs.pop(0) for _ in range(5)]
    edge_out, full_out, node_out, node_full = [refs.pop(0) for _ in range(4)]
    sends = [refs.pop(0) for _ in range(3)]
    edge_w, edge_w2, node_w, node_w2, product_ref, x_ref = refs
    part = edge_own.shape[1]
    edge_count = edge_own.shape[0]
    node_count = node_own.shape[0]
    moves = Moves()
    for pieces, at in ((shards, 0), (rims, edge_count + node_count)):
        rows = pl.ds(at, pieces[0].shape[0])
        for j, shard in enumerate(pieces):
            column = pl.multiple_of((lax.axis_index("mp") ^ j) * part, part)
            moves.start(shard, x_ref.at[rows, pl.ds(column, part)])
    y = lax.axis_index("groups")
    for at, first, second in ((0, edge_w, edge_w2), (1, node_w, node_w2)):
        load_shard(moves, 0, own_w[2 * at], own_w[2 * at + 1], 0, first, second)
        load_shard(moves, 0, core_w[2 * at], core_w[2 * at + 1], 1, first, second)
        for j, pair in enumerate(halves[at]):
            for piece, half in zip(pair, (y, 1 - y)):
                load_half(moves, piece, half, 2 + j, first, second)
    nodes = x_ref[edge_count : edge_count + node_count, :]
    incoming = edge_rows(
        x_ref, x_ref[edge_count:, :], nodes, edge_own, hot_ref, incidence_ref,
        edge_w, edge_w2, product_ref, edge_out, full_out,
    )
    node_new = node_rows(nodes, incoming, node_own, node_w, node_w2, node_out)
    node_full[...] = node_new
    pick_rows(pick_ref, node_new, sends)


def late_weights(weights, first, second):
    moves = Moves()
    load_shard(moves, 1, weights[0], weights[1], 0, first, second)
    load_shard(moves, 1, weights[2], weights[3], 1, first, second)
    load_packed(moves, weights[4], 2, first, second)
    load_packed(moves, weights[5], 3, first, second)


def late_edge_kernel(pieces, *refs):
    refs = list(refs)
    weights = [refs.pop(0) for _ in range(6)]
    edge_ref, edge_own = [refs.pop(0) for _ in range(2)]
    tables = [refs.pop(0) for _ in range(pieces)]
    hot_ref, incidence_ref, edge_out, incoming_out = [refs.pop(0) for _ in range(4)]
    edge_w, edge_w2, product_ref, table_ref = refs
    late_weights(weights, edge_w, edge_w2)
    start = 0
    for table in tables:
        table_ref[start : start + table.shape[0], :] = table[...]
        start += table.shape[0]
    incoming_out[...] = edge_rows(
        edge_ref, table_ref[...], tables[0][...], edge_own, hot_ref, incidence_ref,
        edge_w, edge_w2, product_ref, edge_out, None,
    )


def late_node_kernel(*refs):
    weights = refs[:6]
    node_ref, node_own, incoming_ref, node_out, node_w, node_w2 = refs[6:]
    late_weights(weights, node_w, node_w2)
    node_rows(node_ref[...], incoming_ref[...], node_own, node_w, node_w2, node_out)


SMEM, VMEM, ANY = pltpu.SMEM, pltpu.VMEM, pl.ANY


def call(kernel, out_shape, args, scratch, flops, name, vmem_mib=8):
    arrays = [a for _, a in args]
    moved = sum(a.size * a.dtype.itemsize for a in arrays + list(out_shape))
    return pl.pallas_call(
        kernel,
        out_shape=out_shape,
        in_specs=[pl.BlockSpec(memory_space=s) for s, _ in args],
        out_specs=[pl.BlockSpec(memory_space=VMEM)] * len(out_shape),
        scratch_shapes=scratch,
        compiler_params=pltpu.CompilerParams(vmem_limit_bytes=vmem_mib * 1024 * 1024),
        cost_estimate=pl.CostEstimate(flops=flops, bytes_accessed=moved, transcendentals=0),
        name=name,
    )(*arrays)


def swap(x, mask):
    size = lax.axis_size("mp")
    return lax.ppermute(x, "mp", [(i, i ^ mask) for i in range(size)])


def shift(x, by):
    size = lax.axis_size("graph")
    return lax.ppermute(x, "graph", [(i, (i + by) % size) for i in range(size)])


def after(x, *others):
    return lax.optimization_barrier((x, *others))[0]


def neighbour_rows(right, left, coarse, halo):
    if lax.axis_size("graph") == 4:
        return [shift(right, 1), shift(left, -1), shift(coarse, 2)]
    everyone = lax.all_gather(coarse, "graph", axis=0, tiled=True)
    return [shift(right[:halo], 1), shift(left[:halo], -1), everyone]


def table_index(senders, size, node_count, halo):
    coarse_start = node_count + 2 * halo
    number = jnp.maximum(senders - coarse_start, 0)
    block = (number * 43691) >> 19
    row = number - block * COARSE_DEV
    if size != 4:
        return jnp.where(senders < coarse_start, senders, coarse_start + block * COARSE_PAD + row)
    wide = halo + COARSE_PAD
    away = (block - lax.axis_index("graph")) & 3
    starts = (node_count - COARSE_DEV, node_count + wide + halo, node_count + 2 * wide, node_count + halo)
    base = jnp.where(
        away < 2,
        jnp.where(away == 0, starts[0], starts[1]),
        jnp.where(away == 2, starts[2], starts[3]),
    )
    fine = jnp.where(senders < node_count + halo, senders, senders + COARSE_PAD)
    return jnp.where(senders < coarse_start, fine, base + row)


def on_device(
    node_state,
    edge_state,
    edge_first,
    edge_second,
    node_first,
    node_second,
    senders,
    receivers,
    boundary_rows,
):
    node_count, part = node_state.shape
    edge_count = edge_state.shape[0]
    features = edge_second.shape[2]
    hidden = 4 * part
    halo = boundary_rows.shape[0] // 2
    blocks = lax.axis_size("graph")
    shape = jax.ShapeDtypeStruct
    dma = pltpu.SemaphoreType.DMA

    wide = halo + COARSE_PAD

    def sent(width):
        return [shape((n, width), BF16) for n in (wide, wide, COARSE_PAD)]

    weights = (edge_first, edge_second, node_first, node_second)
    edge_pack = edge_first.shape[1] + features
    node_pack = node_first.shape[1] + features
    edge_ride, node_ride = call(
        ride_kernel,
        [shape((n // 2, part), BF16) for n in (edge_pack, node_pack)],
        [(ANY, w) for w in weights],
        [dma((10,))],
        0,
        "layer_0_half",
        60,
    )
    edge_near, node_near = swap(edge_ride, 2), swap(node_ride, 2)
    (latents,) = call(
        latent_kernel,
        [shape((edge_count + node_count, part), BF16)],
        [(VMEM, after(edge_state, edge_ride)), (VMEM, node_state)],
        [],
        0,
        "latents",
    )
    far_latents = swap(latents, 2)
    far_rows = 2 * wide + COARSE_PAD if blocks == 4 else 2 * halo + blocks * COARSE_PAD
    table_rows = node_count + far_rows
    lanes = -(-(table_rows + node_count) // 128) * 128
    lists = jnp.concatenate([senders, receivers, boundary_rows])[None, :]
    hot, incidence, pick, edge_late, node_late = call(
        functools.partial(prepare_kernel, blocks, halo, table_rows),
        [
            shape((edge_count, lanes), BF16),
            shape((node_count, edge_count), BF16),
            shape((2 * wide + COARSE_PAD, node_count), BF16),
            shape((edge_pack, part), BF16),
            shape((node_pack, part), BF16),
        ],
        [(VMEM, after(lists, latents))] + [(ANY, w) for w in weights],
        [dma((10,))],
        0,
        "one_hot",
    )
    core_w = [swap(after(w, edge_ride), 1) for w in weights]
    right, left, coarse = call(
        start_kernel,
        sent(part),
        [(VMEM, node_state), (VMEM, pick)],
        [],
        2 * pick.size * part,
        "boundary_rows",
    )
    (rim,) = call(
        join_kernel,
        [shape((far_rows, part), BF16)],
        [(VMEM, r) for r in neighbour_rows(right, left, coarse, halo)],
        [],
        0,
        "halo_rows",
    )
    edge_far = lax.ppermute(edge_near, "groups", [(0, 1), (1, 0)])
    node_far = lax.ppermute(node_near, "groups", [(0, 1), (1, 0)])
    far_rim = swap(after(rim, *core_w), 2)
    edge_late_x, node_late_x = lax.optimization_barrier((edge_late, node_late, far_rim, edge_far))[:2]
    edge_late_x, node_late_x = swap(edge_late_x, 2), swap(node_late_x, 2)
    shards = [latents, swap(latents, 1), far_latents, swap(after(far_latents, node_far), 1)]
    rims = [rim, swap(rim, 1), far_rim, swap(far_rim, 1)]
    pairs = []
    for near, far in ((edge_near, edge_far), (node_near, node_far)):
        pairs += [near, far, swap(near, 1), swap(far, 1)]

    edge_flops = 2 * edge_count * features * (2 * features + lanes + node_count)
    node_flops = 2 * node_count * features * 3 * features
    full_edge = shape((edge_count, features), BF16)
    full_node = shape((node_count, features), BF16)
    own_edge = shape((edge_count, part), F32)
    own_node = shape((node_count, part), F32)
    second_shape = pltpu.VMEM((hidden, features), BF16)
    edge_shape = pltpu.VMEM((edge_first.shape[1], hidden), BF16)
    node_shape = pltpu.VMEM((node_first.shape[1], hidden), BF16)

    edge_own, edge_full, node_own, node_full, right, left, coarse = call(
        first_kernel,
        [own_edge, full_edge, own_node, full_node] + sent(features),
        [(VMEM, w) for w in list(weights) + core_w + pairs + shards + rims]
        + [(VMEM, a) for a in (edge_state, node_state, hot, incidence, pick)],
        [
            edge_shape,
            second_shape,
            node_shape,
            second_shape,
            pltpu.VMEM((lanes, hidden), BF16),
            pltpu.VMEM((edge_count + table_rows, features), BF16),
        ],
        edge_flops + node_flops,
        "layer_0",
        16,
    )
    tables = [node_full] + neighbour_rows(right, left, coarse, halo)
    edge_late_d = swap(after(edge_late_x, right), 1)
    edge_own, incoming = call(
        functools.partial(late_edge_kernel, len(tables)),
        [own_edge, full_node],
        [(VMEM, w) for w in (*weights[:2], *core_w[:2], edge_late_x, edge_late_d)]
        + [(VMEM, a) for a in (edge_full, edge_own)]
        + [(VMEM, t) for t in tables]
        + [(VMEM, hot), (VMEM, incidence)],
        [
            edge_shape,
            second_shape,
            pltpu.VMEM((lanes, hidden), BF16),
            pltpu.VMEM((table_rows, features), BF16),
        ],
        edge_flops,
        "layer_1_edges",
        16,
    )
    node_late_d = swap(after(node_late_x, *tables[1:]), 1)
    (node_own,) = call(
        late_node_kernel,
        [own_node],
        [(VMEM, w) for w in (*weights[2:], *core_w[2:], node_late_x, node_late_d)]
        + [(VMEM, a) for a in (node_full, node_own, incoming)],
        [node_shape, second_shape],
        node_flops,
        "layer_1_nodes",
        16,
    )
    return (node_own, edge_own)


def solution(mesh):
    in_specs = (
        P(("groups", "graph"), "mp"),
        P(("groups", "graph"), "mp"),
        P(None, None, "mp"),
        P(None, "mp", None),
        P(None, None, "mp"),
        P(None, "mp", None),
        P("graph"),
        P("graph"),
        P("graph"),
    )
    out_specs = (P(("groups", "graph"), "mp"), P(("groups", "graph"), "mp"))
    return jax.shard_map(
        on_device, mesh=mesh, in_specs=in_specs, out_specs=out_specs, check_vma=False
    )
```

```python
import functools

import jax
import jax.numpy as jnp
from jax import lax
from jax.experimental import pallas as pl
from jax.experimental.pallas import tpu as pltpu
from jax.sharding import PartitionSpec as P

COARSE_DEV = 12
COARSE_PAD = 16
EPS = 1e-05
TILE = 256
F32 = jnp.float32
BF16 = jnp.bfloat16


def silu(x):
    half = 0.5 * x
    return half + half * jnp.tanh(half)


def normalize(msg):
    width = msg.shape[1]
    mean = jnp.sum(msg, axis=1, keepdims=True) * (1.0 / width)
    square = jnp.sum(msg * msg, axis=1, keepdims=True) * (1.0 / width)
    return (msg - mean) * lax.rsqrt(square - mean * mean + EPS)


def dot(a, b):
    return jnp.dot(a, b, preferred_element_type=F32)


def own_columns(full, part):
    mine = lax.axis_index("mp")
    out = full[:, 0:part]
    for j in range(1, full.shape[1] // part):
        out = jnp.where(mine == j, full[:, j * part : (j + 1) * part], out)
    return out


class Copies:
    def __init__(self, sems):
        self.sems, self.started = sems, []

    def start(self, source, target):
        copy = pltpu.make_async_copy(source, target, self.sems.at[len(self.started)])
        copy.start()
        self.started.append(copy)

    def wait(self):
        for copy in self.started:
            copy.wait()


class Moves:
    def start(self, source, target):
        target[...] = source[...]

    def wait(self):
        pass


def load_shard(copies, layer, first, second, j, first_ref, second_ref):
    part = second.shape[1]
    copies.start(first.at[layer], first_ref.at[:, pl.ds(j * part, part)])
    copies.start(second.at[layer], second_ref.at[pl.ds(j * part, part)])


def load_packed(copies, packed, base, j, first_ref, second_ref):
    rows = first_ref.shape[0]
    hidden, features = second_ref.shape
    part = hidden // 4
    copies.start(packed.at[pl.ds(base, rows)], first_ref.at[:, pl.ds(j * part, part)])
    for q in range(features // part):
        copies.start(
            packed.at[pl.ds(base + rows + q * part, part)],
            second_ref.at[pl.ds(j * part, part), pl.ds(q * part, part)],
        )


def load_half(copies, packed, base, half, j, first_ref, second_ref):
    rows = first_ref.shape[0] // 2
    hidden, features = second_ref.shape
    part = hidden // 4
    deep = part // 2
    at = pl.multiple_of(half * rows, rows)
    copies.start(packed.at[pl.ds(base, rows)], first_ref.at[pl.ds(at, rows), pl.ds(j * part, part)])
    at = pl.multiple_of(j * part + half * deep, deep)
    for q in range(features // part):
        copies.start(
            packed.at[pl.ds(base + rows + q * deep, deep)],
            second_ref.at[pl.ds(at, deep), pl.ds(q * part, part)],
        )
    return base + rows + features // part * deep


def ride_kernel(ef, es, nf, ns, ride_out, sems):
    y = lax.axis_index("groups")
    part, features = es.shape[1:]
    copies = Copies(sems)
    at = 0
    for first, second in ((ef, es), (nf, ns)):
        rows = first.shape[1] // 2
        source = first.at[0, pl.ds(pl.multiple_of(y * rows, rows), rows)]
        copies.start(source, ride_out.at[pl.ds(at, rows)])
        at += rows
        deep = part // 2
        for q in range(features // part):
            source = second.at[0, pl.ds(pl.multiple_of(y * deep, deep), deep), pl.ds(q * part, part)]
            copies.start(source, ride_out.at[pl.ds(at, deep)])
            at += deep
    copies.wait()


def one_hot(hit):
    return jnp.where(hit, 1.0, 0.0).astype(BF16)


def column(row):
    return jnp.broadcast_to(row, (8, row.shape[1])).T[:, 0:1]


def make_pick(boundary, pick_out):
    halo = boundary.shape[1] // 2
    node_count = pick_out.shape[1]
    wanted = column(boundary)
    lanes = lax.broadcasted_iota(jnp.int32, (halo, node_count), 1)
    number = lax.broadcasted_iota(jnp.int32, (COARSE_PAD, node_count), 0)
    ids = lax.broadcasted_iota(jnp.int32, (COARSE_PAD, node_count), 1)
    coarse = one_hot((ids == number + (node_count - COARSE_DEV)) & (number < COARSE_DEV))
    wide = halo + COARSE_PAD
    pick_out[0:halo, :] = one_hot(lanes == wanted[halo:])
    pick_out[wide : wide + halo, :] = one_hot(lanes == wanted[:halo])
    for at in (halo, wide + halo, 2 * wide):
        pick_out[at : at + COARSE_PAD, :] = coarse


def prepare_kernel(blocks, halo, table_rows, list_ref, ef, es, nf, ns, hot_out, incidence_out, pick_out, pack_0, pack_1, edge_late, node_late, sems):
    part, features = es.shape[1:]
    edge_count, lanes_all = hot_out.shape
    node_count = incidence_out.shape[0]
    copies = Copies(sems)

    def pack(first, second, layer, out, at):
        rows = first.shape[1]
        copies.start(first.at[layer], out.at[pl.ds(at, rows)])
        at += rows
        for q in range(features // part):
            copies.start(second.at[layer, :, pl.ds(q * part, part)], out.at[pl.ds(at, part)])
            at += part
        return at

    for layer, out in ((0, pack_0), (1, pack_1)):
        pack(nf, ns, layer, out, pack(ef, es, layer, out, 0))
    pack(ef, es, 1, edge_late, 0)
    pack(nf, ns, 1, node_late, 0)
    for at in range(0, edge_count, TILE):
        senders = table_index(list_ref[:, at : at + TILE], blocks, node_count, halo)
        receivers = list_ref[:, edge_count + at : edge_count + at + TILE]
        lanes = lax.broadcasted_iota(jnp.int32, (TILE, lanes_all), 1)
        hit = (lanes == column(senders)) | (lanes == column(receivers) + table_rows)
        hot_out[at : at + TILE, :] = one_hot(hit)
        node_ids = lax.broadcasted_iota(jnp.int32, (node_count, TILE), 0)
        incidence_out[:, at : at + TILE] = one_hot(node_ids == receivers)
    make_pick(list_ref[:, 2 * edge_count : 2 * edge_count + 2 * halo], pick_out)
    copies.wait()


def pick_rows(pick_ref, node_bf, outs):
    picked = dot(pick_ref[...], node_bf).astype(BF16)
    start = 0
    for out in outs:
        out[...] = picked[start : start + out.shape[0]]
        start += out.shape[0]


def start_kernel(node_ref, boundary_ref, right, left, coarse, pick_ref):
    make_pick(boundary_ref[...], pick_ref)
    pick_rows(pick_ref, node_ref[...].astype(BF16), (right, left, coarse))


def latent_kernel(*refs):
    out = refs[-1]
    at = 0
    for piece in refs[:-1]:
        out[at : at + piece.shape[0], :] = piece[...].astype(BF16)
        at += piece.shape[0]


def edge_rows(edge_ref, table, nodes, own_ref, hot_ref, incidence_ref, first_ref, second_ref, product_ref, own_out, full_out):
    features = second_ref.shape[1]
    node_count = nodes.shape[0]
    table_rows = table.shape[0]
    lanes_all = product_ref.shape[0]
    used = table_rows + node_count
    part = own_ref.shape[1]
    product_ref[0:table_rows, :] = dot(table, first_ref[features : 2 * features, :]).astype(BF16)
    product_ref[table_rows:used, :] = dot(
        nodes, first_ref[2 * features : 3 * features, :]
    ).astype(BF16)
    if used < lanes_all:
        product_ref[used:, :] = jnp.zeros((lanes_all - used, features), BF16)
    incoming = jnp.zeros((node_count, features), F32)
    for at in range(0, own_ref.shape[0], TILE):
        rows = slice(at, at + TILE)
        edge_bf = edge_ref[rows, :]
        pre = dot(edge_bf, first_ref[0:features, :]) + dot(hot_ref[rows, :], product_ref[...])
        norm = normalize(dot(silu(pre).astype(BF16), second_ref[...]))
        edge_new = (edge_bf.astype(F32) + norm).astype(BF16)
        if full_out is not None:
            full_out[rows, :] = edge_new
        own_out[rows, :] = own_ref[rows, :] + own_columns(norm, part)
        incoming = incoming + dot(incidence_ref[:, rows], edge_new)
    return incoming.astype(BF16)


def node_rows(node_bf, incoming, own_ref, first_ref, second_ref, own_out):
    features = second_ref.shape[1]
    pre = dot(node_bf, first_ref[0:features, :]) + dot(incoming, first_ref[features:, :])
    norm = normalize(dot(silu(pre).astype(BF16), second_ref[...]))
    own_out[...] = own_ref[...] + own_columns(norm, own_ref.shape[1])
    return (node_bf.astype(F32) + norm).astype(BF16)


def first_kernel(*refs):
    refs = list(refs)
    packs = [refs.pop(0) for _ in range(2)]
    halves = [[refs.pop(0) for _ in range(2)] for _ in range(2)]
    shards = [refs.pop(0) for _ in range(4)]
    edge_own, node_own, hot_ref, incidence_ref, pick_ref = [refs.pop(0) for _ in range(5)]
    edge_out, full_out, node_out, node_full = [refs.pop(0) for _ in range(4)]
    sends = [refs.pop(0) for _ in range(3)]
    edge_w, edge_w2, node_w, node_w2, product_ref, x_ref = refs
    part = edge_own.shape[1]
    edge_count = edge_own.shape[0]
    node_count = node_own.shape[0]
    edge_copies, node_copies = Moves(), Moves()
    for j, shard in enumerate(shards):
        column = pl.multiple_of((lax.axis_index("mp") ^ j) * part, part)
        edge_copies.start(shard, x_ref.at[:, pl.ds(column, part)])
    y = lax.axis_index("groups")
    starts = [0, 0]
    for base, copies, (first, second) in (
        (0, edge_copies, (edge_w, edge_w2)),
        (1, node_copies, (node_w, node_w2)),
    ):
        for j, pack in enumerate(packs):
            load_packed(copies, pack, (0, edge_w.shape[0] + edge_w2.shape[1])[base], j, first, second)
        for j, pair in enumerate(halves):
            for k, piece in enumerate(pair):
                half = y if k == 0 else 1 - y
                end = load_half(copies, piece, starts[base], half, 2 + j, first, second)
        starts[1] = end
    edge_copies.wait()
    nodes = x_ref[edge_count : edge_count + node_count, :]
    incoming = edge_rows(
        x_ref, x_ref[edge_count:, :], nodes, edge_own, hot_ref, incidence_ref,
        edge_w, edge_w2, product_ref, edge_out, full_out,
    )
    node_copies.wait()
    node_new = node_rows(nodes, incoming, node_own, node_w, node_w2, node_out)
    node_full[...] = node_new
    pick_rows(pick_ref, node_new, sends)


def late_weights(weights, base, first, second):
    moves = Moves()
    load_packed(moves, weights[0], base, 0, first, second)
    load_packed(moves, weights[1], base, 1, first, second)
    load_packed(moves, weights[2], 0, 2, first, second)
    load_packed(moves, weights[3], 0, 3, first, second)


def late_edge_kernel(pieces, *refs):
    refs = list(refs)
    weights = [refs.pop(0) for _ in range(4)]
    edge_ref, edge_own = [refs.pop(0) for _ in range(2)]
    tables = [refs.pop(0) for _ in range(pieces)]
    hot_ref, incidence_ref, edge_out, incoming_out = [refs.pop(0) for _ in range(4)]
    edge_w, edge_w2, product_ref, table_ref = refs
    late_weights(weights, 0, edge_w, edge_w2)
    start = 0
    for table in tables:
        table_ref[start : start + table.shape[0], :] = table[...]
        start += table.shape[0]
    incoming_out[...] = edge_rows(
        edge_ref, table_ref[...], tables[0][...], edge_own, hot_ref, incidence_ref,
        edge_w, edge_w2, product_ref, edge_out, None,
    )


def late_node_kernel(base, *refs):
    weights = refs[:4]
    node_ref, node_own, incoming_ref, node_out, node_w, node_w2 = refs[4:]
    late_weights(weights, base, node_w, node_w2)
    node_rows(node_ref[...], incoming_ref[...], node_own, node_w, node_w2, node_out)


SMEM, VMEM, ANY = pltpu.SMEM, pltpu.VMEM, pl.ANY


def call(kernel, out_shape, args, scratch, flops, name, vmem_mib=8):
    arrays = [a for _, a in args]
    moved = sum(a.size * a.dtype.itemsize for a in arrays + list(out_shape))
    return pl.pallas_call(
        kernel,
        out_shape=out_shape,
        in_specs=[pl.BlockSpec(memory_space=s) for s, _ in args],
        out_specs=[pl.BlockSpec(memory_space=VMEM)] * len(out_shape),
        scratch_shapes=scratch,
        compiler_params=pltpu.CompilerParams(vmem_limit_bytes=vmem_mib * 1024 * 1024),
        cost_estimate=pl.CostEstimate(flops=flops, bytes_accessed=moved, transcendentals=0),
        name=name,
    )(*arrays)


def swap(x, mask):
    size = lax.axis_size("mp")
    return lax.ppermute(x, "mp", [(i, i ^ mask) for i in range(size)])


def shift(x, by):
    size = lax.axis_size("graph")
    return lax.ppermute(x, "graph", [(i, (i + by) % size) for i in range(size)])


def after(x, *others):
    return lax.optimization_barrier((x, *others))[0]


def neighbour_rows(right, left, coarse, halo):
    if lax.axis_size("graph") == 4:
        return [shift(right, 1), shift(left, -1), shift(coarse, 2)]
    everyone = lax.all_gather(coarse, "graph", axis=0, tiled=True)
    return [shift(right[:halo], 1), shift(left[:halo], -1), everyone]


def table_index(senders, size, node_count, halo):
    coarse_start = node_count + 2 * halo
    number = jnp.maximum(senders - coarse_start, 0)
    block = (number * 43691) >> 19
    row = number - block * COARSE_DEV
    if size != 4:
        return jnp.where(senders < coarse_start, senders, coarse_start + block * COARSE_PAD + row)
    wide = halo + COARSE_PAD
    away = (block - lax.axis_index("graph")) & 3
    starts = (node_count - COARSE_DEV, node_count + wide + halo, node_count + 2 * wide, node_count + halo)
    base = jnp.where(
        away < 2,
        jnp.where(away == 0, starts[0], starts[1]),
        jnp.where(away == 2, starts[2], starts[3]),
    )
    fine = jnp.where(senders < node_count + halo, senders, senders + COARSE_PAD)
    return jnp.where(senders < coarse_start, fine, base + row)


def on_device(
    node_state,
    edge_state,
    edge_first,
    edge_second,
    node_first,
    node_second,
    senders,
    receivers,
    boundary_rows,
):
    node_count, part = node_state.shape
    edge_count = edge_state.shape[0]
    features = edge_second.shape[2]
    hidden = 4 * part
    halo = boundary_rows.shape[0] // 2
    blocks = lax.axis_size("graph")
    shape = jax.ShapeDtypeStruct
    dma = pltpu.SemaphoreType.DMA

    wide = halo + COARSE_PAD

    def sent(width):
        return [shape((n, width), BF16) for n in (wide, wide, COARSE_PAD)]

    weights = (edge_first, edge_second, node_first, node_second)
    edge_pack = edge_first.shape[1] + features
    node_pack = node_first.shape[1] + features
    late_pack = edge_pack + node_pack
    (ride,) = call(
        ride_kernel,
        [shape(((edge_pack + node_pack) // 2, part), BF16)],
        [(ANY, w) for w in weights],
        [dma((10,))],
        0,
        "layer_0_half",
        60,
    )
    near = swap(ride, 2)
    far_rows = 2 * wide + COARSE_PAD if blocks == 4 else 2 * halo + blocks * COARSE_PAD
    table_rows = node_count + far_rows
    lanes = -(-(table_rows + node_count) // 128) * 128
    right, left, coarse = call(
        start_kernel,
        sent(part),
        [(VMEM, after(node_state, ride)), (VMEM, boundary_rows[None, :])],
        [pltpu.VMEM((2 * wide + COARSE_PAD, node_count), BF16)],
        0,
        "boundary_rows",
    )
    rows = neighbour_rows(right, left, coarse, halo)
    lists = jnp.concatenate([senders, receivers, boundary_rows])[None, :]
    hot, incidence, pick, pack_0, pack_1, edge_late, node_late = call(
        functools.partial(prepare_kernel, blocks, halo, table_rows),
        [
            shape((edge_count, lanes), BF16),
            shape((node_count, edge_count), BF16),
            shape((2 * wide + COARSE_PAD, node_count), BF16),
            shape((late_pack, part), BF16),
            shape((late_pack, part), BF16),
            shape((edge_pack, part), BF16),
            shape((node_pack, part), BF16),
        ],
        [(VMEM, after(lists, *rows))] + [(ANY, w) for w in weights],
        [dma((32,))],
        0,
        "one_hot",
    )
    core_0 = swap(pack_0, 1)
    (latents,) = call(
        latent_kernel,
        [shape((edge_count + table_rows, part), BF16)],
        [(VMEM, after(edge_state, pack_0)), (VMEM, node_state)] + [(VMEM, r) for r in rows],
        [],
        0,
        "latents",
    )
    near = after(near, latents)
    far_latents = swap(latents, 2)
    far = lax.ppermute(near, "groups", [(0, 1), (1, 0)])
    core_near, core_latents = swap(near, 1), swap(latents, 1)
    core_1 = swap(after(pack_1, far), 1)
    core_far = swap(after(far, core_latents, core_near), 1)
    edge_late_x = swap(after(edge_late, core_near), 2)
    node_late_x = swap(after(node_late, far_latents), 2)
    shards = [latents, core_latents, far_latents, swap(after(far_latents, far), 1)]
    pairs = [near, far, core_near, core_far]

    edge_flops = 2 * edge_count * features * (2 * features + lanes + node_count)
    node_flops = 2 * node_count * features * 3 * features
    full_edge = shape((edge_count, features), BF16)
    full_node = shape((node_count, features), BF16)
    own_edge = shape((edge_count, part), F32)
    own_node = shape((node_count, part), F32)
    second_shape = pltpu.VMEM((hidden, features), BF16)
    edge_shape = pltpu.VMEM((edge_first.shape[1], hidden), BF16)
    node_shape = pltpu.VMEM((node_first.shape[1], hidden), BF16)

    edge_own, edge_full, node_own, node_full, right, left, coarse = call(
        first_kernel,
        [own_edge, full_edge, own_node, full_node] + sent(features),
        [(VMEM, w) for w in [pack_0, core_0] + pairs + shards]
        + [(VMEM, a) for a in (edge_state, node_state, hot, incidence, pick)],
        [
            edge_shape,
            second_shape,
            node_shape,
            second_shape,
            pltpu.VMEM((lanes, hidden), BF16),
            pltpu.VMEM((edge_count + table_rows, features), BF16),
        ],
        edge_flops + node_flops,
        "layer_0",
        16,
    )
    tables = [node_full] + neighbour_rows(right, left, coarse, halo)
    edge_late_d = swap(after(edge_late_x, right, core_1), 1)
    edge_own, incoming = call(
        functools.partial(late_edge_kernel, len(tables)),
        [own_edge, full_node],
        [(VMEM, w) for w in (pack_1, core_1, edge_late_x, edge_late_d)]
        + [(VMEM, a) for a in (edge_full, edge_own)]
        + [(VMEM, t) for t in tables]
        + [(VMEM, hot), (VMEM, incidence)],
        [
            edge_shape,
            second_shape,
            pltpu.VMEM((lanes, hidden), BF16),
            pltpu.VMEM((table_rows, features), BF16),
        ],
        edge_flops,
        "layer_1_edges",
        16,
    )
    node_late_d = swap(after(node_late_x, *tables[1:]), 1)
    (node_own,) = call(
        functools.partial(late_node_kernel, edge_pack),
        [own_node],
        [(VMEM, w) for w in (pack_1, core_1, node_late_x, node_late_d)]
        + [(VMEM, a) for a in (node_full, node_own, incoming)],
        [node_shape, second_shape],
        node_flops,
        "layer_1_nodes",
        16,
    )
    return (node_own, edge_own)


def solution(mesh):
    in_specs = (
        P(("groups", "graph"), "mp"),
        P(("groups", "graph"), "mp"),
        P(None, None, "mp"),
        P(None, "mp", None),
        P(None, None, "mp"),
        P(None, "mp", None),
        P("graph"),
        P("graph"),
        P("graph"),
    )
    out_specs = (P(("groups", "graph"), "mp"), P(("groups", "graph"), "mp"))
    return jax.shard_map(
        on_device, mesh=mesh, in_specs=in_specs, out_specs=out_specs, check_vma=False
    )
```

```python
import functools

import jax
import jax.numpy as jnp
from jax import lax
from jax.experimental import pallas as pl
from jax.experimental.pallas import tpu as pltpu
from jax.sharding import PartitionSpec as P

COARSE_DEV = 12
COARSE_PAD = 16
EPS = 1e-05
TILE = 256
F32 = jnp.float32
BF16 = jnp.bfloat16


def silu(x):
    half = 0.5 * x
    return half + half * jnp.tanh(half)


def normalize(msg):
    width = msg.shape[1]
    mean = jnp.sum(msg, axis=1, keepdims=True) * (1.0 / width)
    square = jnp.sum(msg * msg, axis=1, keepdims=True) * (1.0 / width)
    return (msg - mean) * lax.rsqrt(square - mean * mean + EPS)


def dot(a, b):
    return jnp.dot(a, b, preferred_element_type=F32)


def own_columns(full, part):
    mine = lax.axis_index("mp")
    out = full[:, 0:part]
    for j in range(1, full.shape[1] // part):
        out = jnp.where(mine == j, full[:, j * part : (j + 1) * part], out)
    return out


class Copies:
    def __init__(self, sems):
        self.sems, self.started = sems, []

    def start(self, source, target):
        copy = pltpu.make_async_copy(source, target, self.sems.at[len(self.started)])
        copy.start()
        self.started.append(copy)

    def wait(self):
        for copy in self.started:
            copy.wait()


class Moves:
    def start(self, source, target):
        target[...] = source[...]

    def wait(self):
        pass


def load_shard(copies, layer, first, second, j, first_ref, second_ref):
    part = second.shape[1]
    copies.start(first.at[layer], first_ref.at[:, pl.ds(j * part, part)])
    copies.start(second.at[layer], second_ref.at[pl.ds(j * part, part)])


def load_packed(copies, packed, base, j, first_ref, second_ref):
    rows = first_ref.shape[0]
    hidden, features = second_ref.shape
    part = hidden // 4
    copies.start(packed.at[pl.ds(base, rows)], first_ref.at[:, pl.ds(j * part, part)])
    for q in range(features // part):
        copies.start(
            packed.at[pl.ds(base + rows + q * part, part)],
            second_ref.at[pl.ds(j * part, part), pl.ds(q * part, part)],
        )


def load_half(copies, packed, base, half, j, first_ref, second_ref):
    rows = first_ref.shape[0] // 2
    hidden, features = second_ref.shape
    part = hidden // 4
    deep = part // 2
    at = pl.multiple_of(half * rows, rows)
    copies.start(packed.at[pl.ds(base, rows)], first_ref.at[pl.ds(at, rows), pl.ds(j * part, part)])
    at = pl.multiple_of(j * part + half * deep, deep)
    for q in range(features // part):
        copies.start(
            packed.at[pl.ds(base + rows + q * deep, deep)],
            second_ref.at[pl.ds(at, deep), pl.ds(q * part, part)],
        )
    return base + rows + features // part * deep


def ride_kernel(ef, es, nf, ns, ride_out, sems):
    y = lax.axis_index("groups")
    part, features = es.shape[1:]
    copies = Copies(sems)
    at = 0
    for first, second in ((ef, es), (nf, ns)):
        rows = first.shape[1] // 2
        source = first.at[0, pl.ds(pl.multiple_of(y * rows, rows), rows)]
        copies.start(source, ride_out.at[pl.ds(at, rows)])
        at += rows
        deep = part // 2
        for q in range(features // part):
            source = second.at[0, pl.ds(pl.multiple_of(y * deep, deep), deep), pl.ds(q * part, part)]
            copies.start(source, ride_out.at[pl.ds(at, deep)])
            at += deep
    copies.wait()


def one_hot(hit):
    return jnp.where(hit, 1.0, 0.0).astype(BF16)


def column(row):
    return jnp.broadcast_to(row, (8, row.shape[1])).T[:, 0:1]


def make_pick(boundary, pick_out):
    halo = boundary.shape[1] // 2
    node_count = pick_out.shape[1]
    wanted = column(boundary)
    lanes = lax.broadcasted_iota(jnp.int32, (halo, node_count), 1)
    number = lax.broadcasted_iota(jnp.int32, (COARSE_PAD, node_count), 0)
    ids = lax.broadcasted_iota(jnp.int32, (COARSE_PAD, node_count), 1)
    coarse = one_hot((ids == number + (node_count - COARSE_DEV)) & (number < COARSE_DEV))
    wide = halo + COARSE_PAD
    pick_out[0:halo, :] = one_hot(lanes == wanted[halo:])
    pick_out[wide : wide + halo, :] = one_hot(lanes == wanted[:halo])
    for at in (halo, wide + halo, 2 * wide):
        pick_out[at : at + COARSE_PAD, :] = coarse


def prepare_kernel(blocks, halo, table_rows, list_ref, ef, es, nf, ns, hot_out, incidence_out, pick_out, pack_out, edge_late, node_late, sems):
    part, features = es.shape[1:]
    edge_count, lanes_all = hot_out.shape
    node_count = incidence_out.shape[0]
    copies = Copies(sems)

    def pack(first, second, layer, out, at):
        rows = first.shape[1]
        copies.start(first.at[layer], out.at[pl.ds(at, rows)])
        at += rows
        for q in range(features // part):
            copies.start(second.at[layer, :, pl.ds(q * part, part)], out.at[pl.ds(at, part)])
            at += part
        return at

    end = 0
    for layer in range(ef.shape[0]):
        end = pack(nf, ns, layer, pack_out, pack(ef, es, layer, pack_out, end))
    pack(ef, es, 1, edge_late, 0)
    pack(nf, ns, 1, node_late, 0)
    for at in range(0, edge_count, TILE):
        senders = table_index(list_ref[:, at : at + TILE], blocks, node_count, halo)
        receivers = list_ref[:, edge_count + at : edge_count + at + TILE]
        lanes = lax.broadcasted_iota(jnp.int32, (TILE, lanes_all), 1)
        hit = (lanes == column(senders)) | (lanes == column(receivers) + table_rows)
        hot_out[at : at + TILE, :] = one_hot(hit)
        node_ids = lax.broadcasted_iota(jnp.int32, (node_count, TILE), 0)
        incidence_out[:, at : at + TILE] = one_hot(node_ids == receivers)
    make_pick(list_ref[:, 2 * edge_count : 2 * edge_count + 2 * halo], pick_out)
    copies.wait()


def pick_rows(pick_ref, node_bf, outs):
    picked = dot(pick_ref[...], node_bf).astype(BF16)
    start = 0
    for out in outs:
        out[...] = picked[start : start + out.shape[0]]
        start += out.shape[0]


def start_kernel(node_ref, boundary_ref, right, left, coarse, pick_ref):
    make_pick(boundary_ref[...], pick_ref)
    pick_rows(pick_ref, node_ref[...].astype(BF16), (right, left, coarse))


def latent_kernel(*refs):
    out = refs[-1]
    at = 0
    for piece in refs[:-1]:
        out[at : at + piece.shape[0], :] = piece[...].astype(BF16)
        at += piece.shape[0]


def edge_rows(edge_ref, table, nodes, own_ref, hot_ref, incidence_ref, first_ref, second_ref, product_ref, own_out, full_out):
    features = second_ref.shape[1]
    node_count = nodes.shape[0]
    table_rows = table.shape[0]
    lanes_all = product_ref.shape[0]
    used = table_rows + node_count
    part = own_ref.shape[1]
    product_ref[0:table_rows, :] = dot(table, first_ref[features : 2 * features, :]).astype(BF16)
    product_ref[table_rows:used, :] = dot(
        nodes, first_ref[2 * features : 3 * features, :]
    ).astype(BF16)
    if used < lanes_all:
        product_ref[used:, :] = jnp.zeros((lanes_all - used, features), BF16)
    incoming = jnp.zeros((node_count, features), F32)
    for at in range(0, own_ref.shape[0], TILE):
        rows = slice(at, at + TILE)
        edge_bf = edge_ref[rows, :]
        pre = dot(edge_bf, first_ref[0:features, :]) + dot(hot_ref[rows, :], product_ref[...])
        norm = normalize(dot(silu(pre).astype(BF16), second_ref[...]))
        edge_new = (edge_bf.astype(F32) + norm).astype(BF16)
        if full_out is not None:
            full_out[rows, :] = edge_new
        own_out[rows, :] = own_ref[rows, :] + own_columns(norm, part)
        incoming = incoming + dot(incidence_ref[:, rows], edge_new)
    return incoming.astype(BF16)


def node_rows(node_bf, incoming, own_ref, first_ref, second_ref, own_out):
    features = second_ref.shape[1]
    pre = dot(node_bf, first_ref[0:features, :]) + dot(incoming, first_ref[features:, :])
    norm = normalize(dot(silu(pre).astype(BF16), second_ref[...]))
    own_out[...] = own_ref[...] + own_columns(norm, own_ref.shape[1])
    return (node_bf.astype(F32) + norm).astype(BF16)


def first_kernel(*refs):
    refs = list(refs)
    packs = [refs.pop(0) for _ in range(2)]
    halves = [[refs.pop(0) for _ in range(2)] for _ in range(2)]
    shards = [refs.pop(0) for _ in range(4)]
    edge_own, node_own, hot_ref, incidence_ref, pick_ref = [refs.pop(0) for _ in range(5)]
    edge_out, full_out, node_out, node_full = [refs.pop(0) for _ in range(4)]
    sends = [refs.pop(0) for _ in range(3)]
    edge_w, edge_w2, node_w, node_w2, product_ref, x_ref = refs
    part = edge_own.shape[1]
    edge_count = edge_own.shape[0]
    node_count = node_own.shape[0]
    edge_copies, node_copies = Moves(), Moves()
    for j, shard in enumerate(shards):
        column = pl.multiple_of((lax.axis_index("mp") ^ j) * part, part)
        edge_copies.start(shard, x_ref.at[:, pl.ds(column, part)])
    y = lax.axis_index("groups")
    starts = [0, 0]
    for base, copies, (first, second) in (
        (0, edge_copies, (edge_w, edge_w2)),
        (1, node_copies, (node_w, node_w2)),
    ):
        for j, pack in enumerate(packs):
            load_packed(copies, pack, (0, edge_w.shape[0] + edge_w2.shape[1])[base], j, first, second)
        for j, pair in enumerate(halves):
            for k, piece in enumerate(pair):
                half = y if k == 0 else 1 - y
                end = load_half(copies, piece, starts[base], half, 2 + j, first, second)
        starts[1] = end
    edge_copies.wait()
    nodes = x_ref[edge_count : edge_count + node_count, :]
    incoming = edge_rows(
        x_ref, x_ref[edge_count:, :], nodes, edge_own, hot_ref, incidence_ref,
        edge_w, edge_w2, product_ref, edge_out, full_out,
    )
    node_copies.wait()
    node_new = node_rows(nodes, incoming, node_own, node_w, node_w2, node_out)
    node_full[...] = node_new
    pick_rows(pick_ref, node_new, sends)


def late_weights(weights, base, first, second):
    moves = Moves()
    load_packed(moves, weights[0], base, 0, first, second)
    load_packed(moves, weights[1], base, 1, first, second)
    load_packed(moves, weights[2], 0, 2, first, second)
    load_packed(moves, weights[3], 0, 3, first, second)


def late_edge_kernel(pieces, base, *refs):
    refs = list(refs)
    weights = [refs.pop(0) for _ in range(4)]
    edge_ref, edge_own = [refs.pop(0) for _ in range(2)]
    tables = [refs.pop(0) for _ in range(pieces)]
    hot_ref, incidence_ref, edge_out, incoming_out = [refs.pop(0) for _ in range(4)]
    edge_w, edge_w2, product_ref, table_ref = refs
    late_weights(weights, base, edge_w, edge_w2)
    start = 0
    for table in tables:
        table_ref[start : start + table.shape[0], :] = table[...]
        start += table.shape[0]
    incoming_out[...] = edge_rows(
        edge_ref, table_ref[...], tables[0][...], edge_own, hot_ref, incidence_ref,
        edge_w, edge_w2, product_ref, edge_out, None,
    )


def late_node_kernel(base, *refs):
    weights = refs[:4]
    node_ref, node_own, incoming_ref, node_out, node_w, node_w2 = refs[4:]
    late_weights(weights, base, node_w, node_w2)
    node_rows(node_ref[...], incoming_ref[...], node_own, node_w, node_w2, node_out)


SMEM, VMEM, ANY = pltpu.SMEM, pltpu.VMEM, pl.ANY


def call(kernel, out_shape, args, scratch, flops, name, vmem_mib=8):
    arrays = [a for _, a in args]
    moved = sum(a.size * a.dtype.itemsize for a in arrays + list(out_shape))
    return pl.pallas_call(
        kernel,
        out_shape=out_shape,
        in_specs=[pl.BlockSpec(memory_space=s) for s, _ in args],
        out_specs=[pl.BlockSpec(memory_space=VMEM)] * len(out_shape),
        scratch_shapes=scratch,
        compiler_params=pltpu.CompilerParams(vmem_limit_bytes=vmem_mib * 1024 * 1024),
        cost_estimate=pl.CostEstimate(flops=0, bytes_accessed=0, transcendentals=0),
        name=name,
    )(*arrays)


def swap(x, mask):
    size = lax.axis_size("mp")
    return lax.ppermute(x, "mp", [(i, i ^ mask) for i in range(size)])


def shift(x, by):
    size = lax.axis_size("graph")
    return lax.ppermute(x, "graph", [(i, (i + by) % size) for i in range(size)])


def after(x, *others):
    return lax.optimization_barrier((x, *others))[0]


def neighbour_rows(right, left, coarse, halo):
    if lax.axis_size("graph") == 4:
        return [shift(right, 1), shift(left, -1), shift(coarse, 2)]
    everyone = lax.all_gather(coarse, "graph", axis=0, tiled=True)
    return [shift(right[:halo], 1), shift(left[:halo], -1), everyone]


def table_index(senders, size, node_count, halo):
    coarse_start = node_count + 2 * halo
    number = jnp.maximum(senders - coarse_start, 0)
    block = (number * 43691) >> 19
    row = number - block * COARSE_DEV
    if size != 4:
        return jnp.where(senders < coarse_start, senders, coarse_start + block * COARSE_PAD + row)
    wide = halo + COARSE_PAD
    away = (block - lax.axis_index("graph")) & 3
    starts = (node_count - COARSE_DEV, node_count + wide + halo, node_count + 2 * wide, node_count + halo)
    base = jnp.where(
        away < 2,
        jnp.where(away == 0, starts[0], starts[1]),
        jnp.where(away == 2, starts[2], starts[3]),
    )
    fine = jnp.where(senders < node_count + halo, senders, senders + COARSE_PAD)
    return jnp.where(senders < coarse_start, fine, base + row)


def on_device(
    node_state,
    edge_state,
    edge_first,
    edge_second,
    node_first,
    node_second,
    senders,
    receivers,
    boundary_rows,
):
    node_count, part = node_state.shape
    edge_count = edge_state.shape[0]
    features = edge_second.shape[2]
    hidden = 4 * part
    halo = boundary_rows.shape[0] // 2
    blocks = lax.axis_size("graph")
    shape = jax.ShapeDtypeStruct
    dma = pltpu.SemaphoreType.DMA

    wide = halo + COARSE_PAD

    def sent(width):
        return [shape((n, width), BF16) for n in (wide, wide, COARSE_PAD)]

    weights = (edge_first, edge_second, node_first, node_second)
    edge_pack = edge_first.shape[1] + features
    node_pack = node_first.shape[1] + features
    late_pack = edge_pack + node_pack
    (ride,) = call(
        ride_kernel,
        [shape(((edge_pack + node_pack) // 2, part), BF16)],
        [(ANY, w) for w in weights],
        [dma((10,))],
        0,
        "layer_0_half",
        60,
    )
    near = swap(ride, 2)
    far_rows = 2 * wide + COARSE_PAD if blocks == 4 else 2 * halo + blocks * COARSE_PAD
    table_rows = node_count + far_rows
    lanes = -(-(table_rows + node_count) // 128) * 128
    right, left, coarse = call(
        start_kernel,
        sent(part),
        [(VMEM, after(node_state, ride)), (VMEM, boundary_rows[None, :])],
        [pltpu.VMEM((2 * wide + COARSE_PAD, node_count), BF16)],
        0,
        "boundary_rows",
    )
    rows = neighbour_rows(right, left, coarse, halo)
    lists = jnp.concatenate([senders, receivers, boundary_rows])[None, :]
    hot, incidence, pick, packs, edge_late, node_late = call(
        functools.partial(prepare_kernel, blocks, halo, table_rows),
        [
            shape((edge_count, lanes), BF16),
            shape((node_count, edge_count), BF16),
            shape((2 * wide + COARSE_PAD, node_count), BF16),
            shape((2 * late_pack, part), BF16),
            shape((edge_pack, part), BF16),
            shape((node_pack, part), BF16),
        ],
        [(VMEM, after(lists, *rows))] + [(ANY, w) for w in weights],
        [dma((32,))],
        0,
        "one_hot",
    )
    (latents,) = call(
        latent_kernel,
        [shape((edge_count + table_rows, part), BF16)],
        [(VMEM, after(edge_state, packs)), (VMEM, node_state)] + [(VMEM, r) for r in rows],
        [],
        0,
        "latents",
    )
    near = near
    core_packs = swap(after(packs, near), 1)
    far_latents = swap(latents, 2)
    far = lax.ppermute(near, "groups", [(0, 1), (1, 0)])
    core_latents = swap(after(latents, near), 1)
    core_near = swap(near, 1)
    core_far = swap(far, 1)
    edge_late_x = swap(after(edge_late, near), 2)
    node_late_x = swap(after(node_late, far, far_latents), 2)
    shards = [latents, core_latents, far_latents, swap(after(far_latents, far, core_packs, core_near), 1)]
    pairs = [near, far, core_near, core_far]

    edge_flops = 2 * edge_count * features * (2 * features + lanes + node_count)
    node_flops = 2 * node_count * features * 3 * features
    full_edge = shape((edge_count, features), BF16)
    full_node = shape((node_count, features), BF16)
    own_edge = shape((edge_count, part), F32)
    own_node = shape((node_count, part), F32)
    second_shape = pltpu.VMEM((hidden, features), BF16)
    edge_shape = pltpu.VMEM((edge_first.shape[1], hidden), BF16)
    node_shape = pltpu.VMEM((node_first.shape[1], hidden), BF16)

    edge_own, edge_full, node_own, node_full, right, left, coarse = call(
        first_kernel,
        [own_edge, full_edge, own_node, full_node] + sent(features),
        [(VMEM, w) for w in [packs, core_packs] + pairs + shards]
        + [(VMEM, a) for a in (edge_state, node_state, hot, incidence, pick)],
        [
            edge_shape,
            second_shape,
            node_shape,
            second_shape,
            pltpu.VMEM((lanes, hidden), BF16),
            pltpu.VMEM((edge_count + table_rows, features), BF16),
        ],
        edge_flops + node_flops,
        "layer_0",
        16,
    )
    tables = [node_full] + neighbour_rows(right, left, coarse, halo)
    edge_late_d = swap(after(edge_late_x, *tables[1:]), 1)
    edge_own, incoming = call(
        functools.partial(late_edge_kernel, len(tables), late_pack),
        [own_edge, full_node],
        [(VMEM, w) for w in (packs, core_packs, edge_late_x, edge_late_d)]
        + [(VMEM, a) for a in (edge_full, edge_own)]
        + [(VMEM, t) for t in tables]
        + [(VMEM, hot), (VMEM, incidence)],
        [
            edge_shape,
            second_shape,
            pltpu.VMEM((lanes, hidden), BF16),
            pltpu.VMEM((table_rows, features), BF16),
        ],
        edge_flops,
        "layer_1_edges",
        16,
    )
    node_late_d = swap(after(node_late_x, right), 1)
    (node_own,) = call(
        functools.partial(late_node_kernel, late_pack + edge_pack),
        [own_node],
        [(VMEM, w) for w in (packs, core_packs, node_late_x, node_late_d)]
        + [(VMEM, a) for a in (node_full, node_own, incoming)],
        [node_shape, second_shape],
        node_flops,
        "layer_1_nodes",
        16,
    )
    return (node_own, edge_own)


def solution(mesh):
    in_specs = (
        P(("groups", "graph"), "mp"),
        P(("groups", "graph"), "mp"),
        P(None, None, "mp"),
        P(None, "mp", None),
        P(None, None, "mp"),
        P(None, "mp", None),
        P("graph"),
        P("graph"),
        P("graph"),
    )
    out_specs = (P(("groups", "graph"), "mp"), P(("groups", "graph"), "mp"))
    return jax.shard_map(
        on_device, mesh=mesh, in_specs=in_specs, out_specs=out_specs, check_vma=False
    )
```

```python
import functools

import jax
import jax.numpy as jnp
from jax import lax
from jax.experimental import pallas as pl
from jax.experimental.pallas import tpu as pltpu
from jax.sharding import PartitionSpec as P

COARSE_DEV = 12
COARSE_PAD = 16
EPS = 1e-05
TILE = 512
HOT_TILE = 256
F32 = jnp.float32
BF16 = jnp.bfloat16


def silu(x):
    half = 0.5 * x
    return half + half * jnp.tanh(half)


def normalize(msg):
    width = msg.shape[1]
    mean = jnp.sum(msg, axis=1, keepdims=True) * (1.0 / width)
    square = jnp.sum(msg * msg, axis=1, keepdims=True) * (1.0 / width)
    return (msg - mean) * lax.rsqrt(square - mean * mean + EPS)


def dot(a, b):
    return jnp.dot(a, b, preferred_element_type=F32)


def own_columns(full, part):
    mine = lax.axis_index("mp")
    out = full[:, 0:part]
    for j in range(1, full.shape[1] // part):
        out = jnp.where(mine == j, full[:, j * part : (j + 1) * part], out)
    return out


class Copies:
    def __init__(self, sems):
        self.sems, self.started = sems, []

    def start(self, source, target):
        copy = pltpu.make_async_copy(source, target, self.sems.at[len(self.started)])
        copy.start()
        self.started.append(copy)

    def wait(self):
        for copy in self.started:
            copy.wait()


class Moves:
    def start(self, source, target):
        target[...] = source[...]

    def wait(self):
        pass


def load_shard(copies, layer, first, second, j, first_ref, second_ref):
    part = second.shape[1]
    copies.start(first.at[layer], first_ref.at[:, pl.ds(j * part, part)])
    copies.start(second.at[layer], second_ref.at[pl.ds(j * part, part)])


def load_packed(copies, packed, base, j, first_ref, second_ref):
    rows = first_ref.shape[0]
    hidden, features = second_ref.shape
    part = hidden // 4
    copies.start(packed.at[pl.ds(base, rows)], first_ref.at[:, pl.ds(j * part, part)])
    for q in range(features // part):
        copies.start(
            packed.at[pl.ds(base + rows + q * part, part)],
            second_ref.at[pl.ds(j * part, part), pl.ds(q * part, part)],
        )


def load_half(copies, packed, base, half, j, first_ref, second_ref):
    rows = first_ref.shape[0] // 2
    hidden, features = second_ref.shape
    part = hidden // 4
    deep = part // 2
    at = pl.multiple_of(half * rows, rows)
    copies.start(packed.at[pl.ds(base, rows)], first_ref.at[pl.ds(at, rows), pl.ds(j * part, part)])
    at = pl.multiple_of(j * part + half * deep, deep)
    for q in range(features // part):
        copies.start(
            packed.at[pl.ds(base + rows + q * deep, deep)],
            second_ref.at[pl.ds(at, deep), pl.ds(q * part, part)],
        )
    return base + rows + features // part * deep


def ride_kernel(ef, es, nf, ns, ride_out, sems):
    y = lax.axis_index("groups")
    part, features = es.shape[1:]
    copies = Copies(sems)
    at = 0
    for first, second in ((ef, es), (nf, ns)):
        rows = first.shape[1] // 2
        source = first.at[0, pl.ds(pl.multiple_of(y * rows, rows), rows)]
        copies.start(source, ride_out.at[pl.ds(at, rows)])
        at += rows
        deep = part // 2
        for q in range(features // part):
            source = second.at[0, pl.ds(pl.multiple_of(y * deep, deep), deep), pl.ds(q * part, part)]
            copies.start(source, ride_out.at[pl.ds(at, deep)])
            at += deep
    copies.wait()


def one_hot(hit):
    return jnp.where(hit, 1.0, 0.0).astype(BF16)


def column(row):
    return jnp.broadcast_to(row, (8, row.shape[1])).T[:, 0:1]


def make_pick(boundary, pick_out):
    halo = boundary.shape[1] // 2
    node_count = pick_out.shape[1]
    wanted = column(boundary)
    lanes = lax.broadcasted_iota(jnp.int32, (halo, node_count), 1)
    number = lax.broadcasted_iota(jnp.int32, (COARSE_PAD, node_count), 0)
    ids = lax.broadcasted_iota(jnp.int32, (COARSE_PAD, node_count), 1)
    coarse = one_hot((ids == number + (node_count - COARSE_DEV)) & (number < COARSE_DEV))
    wide = halo + COARSE_PAD
    pick_out[0:halo, :] = one_hot(lanes == wanted[halo:])
    pick_out[wide : wide + halo, :] = one_hot(lanes == wanted[:halo])
    for at in (halo, wide + halo, 2 * wide):
        pick_out[at : at + COARSE_PAD, :] = coarse


def prepare_kernel(blocks, halo, table_rows, list_ref, ef, es, nf, ns, hot_out, incidence_out, pick_out, pack_out, edge_late, node_late, sems):
    part, features = es.shape[1:]
    edge_count, lanes_all = hot_out.shape
    node_count = incidence_out.shape[0]
    copies = Copies(sems)

    def pack(first, second, layer, out, at):
        rows = first.shape[1]
        copies.start(first.at[layer], out.at[pl.ds(at, rows)])
        at += rows
        for q in range(features // part):
            copies.start(second.at[layer, :, pl.ds(q * part, part)], out.at[pl.ds(at, part)])
            at += part
        return at

    end = 0
    for layer in range(ef.shape[0]):
        end = pack(nf, ns, layer, pack_out, pack(ef, es, layer, pack_out, end))
    pack(ef, es, 1, edge_late, 0)
    pack(nf, ns, 1, node_late, 0)
    for at in range(0, edge_count, HOT_TILE):
        senders = table_index(list_ref[:, at : at + HOT_TILE], blocks, node_count, halo)
        receivers = list_ref[:, edge_count + at : edge_count + at + HOT_TILE]
        lanes = lax.broadcasted_iota(jnp.int32, (HOT_TILE, lanes_all), 1)
        hit = (lanes == column(senders)) | (lanes == column(receivers) + table_rows)
        hot_out[at : at + HOT_TILE, :] = one_hot(hit)
        node_ids = lax.broadcasted_iota(jnp.int32, (node_count, HOT_TILE), 0)
        incidence_out[:, at : at + HOT_TILE] = one_hot(node_ids == receivers)
    make_pick(list_ref[:, 2 * edge_count : 2 * edge_count + 2 * halo], pick_out)
    copies.wait()


def pick_rows(pick_ref, node_bf, outs):
    picked = dot(pick_ref[...], node_bf).astype(BF16)
    start = 0
    for out in outs:
        out[...] = picked[start : start + out.shape[0]]
        start += out.shape[0]


def start_kernel(node_ref, boundary_ref, right, left, coarse, pick_ref):
    make_pick(boundary_ref[...], pick_ref)
    pick_rows(pick_ref, node_ref[...].astype(BF16), (right, left, coarse))


def latent_kernel(*refs):
    out = refs[-1]
    at = 0
    for piece in refs[:-1]:
        out[at : at + piece.shape[0], :] = piece[...].astype(BF16)
        at += piece.shape[0]


def edge_rows(edge_ref, table, nodes, own_ref, hot_ref, incidence_ref, first_ref, second_ref, product_ref, own_out, full_out):
    features = second_ref.shape[1]
    node_count = nodes.shape[0]
    table_rows = table.shape[0]
    lanes_all = product_ref.shape[0]
    used = table_rows + node_count
    part = own_ref.shape[1]
    product_ref[0:table_rows, :] = dot(table, first_ref[features : 2 * features, :]).astype(BF16)
    product_ref[table_rows:used, :] = dot(
        nodes, first_ref[2 * features : 3 * features, :]
    ).astype(BF16)
    if used < lanes_all:
        product_ref[used:, :] = jnp.zeros((lanes_all - used, features), BF16)
    incoming = jnp.zeros((node_count, features), F32)
    for at in range(0, own_ref.shape[0], TILE):
        rows = slice(at, at + TILE)
        edge_bf = edge_ref[rows, :]
        pre = dot(edge_bf, first_ref[0:features, :]) + dot(hot_ref[rows, :], product_ref[...])
        norm = normalize(dot(silu(pre).astype(BF16), second_ref[...]))
        edge_new = (edge_bf.astype(F32) + norm).astype(BF16)
        if full_out is not None:
            full_out[rows, :] = edge_new
        own_out[rows, :] = own_ref[rows, :] + own_columns(norm, part)
        incoming = incoming + dot(incidence_ref[:, rows], edge_new)
    return incoming.astype(BF16)


def node_rows(node_bf, incoming, own_ref, first_ref, second_ref, own_out):
    features = second_ref.shape[1]
    pre = dot(node_bf, first_ref[0:features, :]) + dot(incoming, first_ref[features:, :])
    norm = normalize(dot(silu(pre).astype(BF16), second_ref[...]))
    own_out[...] = own_ref[...] + own_columns(norm, own_ref.shape[1])
    return (node_bf.astype(F32) + norm).astype(BF16)


def first_kernel(*refs):
    refs = list(refs)
    packs = [refs.pop(0) for _ in range(2)]
    halves = [[refs.pop(0) for _ in range(2)] for _ in range(2)]
    shards = [refs.pop(0) for _ in range(4)]
    edge_own, node_own, hot_ref, incidence_ref, pick_ref = [refs.pop(0) for _ in range(5)]
    edge_out, full_out, node_out, node_full = [refs.pop(0) for _ in range(4)]
    sends = [refs.pop(0) for _ in range(3)]
    edge_w, edge_w2, node_w, node_w2, product_ref, x_ref = refs
    part = edge_own.shape[1]
    edge_count = edge_own.shape[0]
    node_count = node_own.shape[0]
    edge_copies, node_copies = Moves(), Moves()
    for j, shard in enumerate(shards):
        column = pl.multiple_of((lax.axis_index("mp") ^ j) * part, part)
        edge_copies.start(shard, x_ref.at[:, pl.ds(column, part)])
    y = lax.axis_index("groups")
    starts = [0, 0]
    for base, copies, (first, second) in (
        (0, edge_copies, (edge_w, edge_w2)),
        (1, node_copies, (node_w, node_w2)),
    ):
        for j, pack in enumerate(packs):
            load_packed(copies, pack, (0, edge_w.shape[0] + edge_w2.shape[1])[base], j, first, second)
        for j, pair in enumerate(halves):
            for k, piece in enumerate(pair):
                half = y if k == 0 else 1 - y
                end = load_half(copies, piece, starts[base], half, 2 + j, first, second)
        starts[1] = end
    edge_copies.wait()
    nodes = x_ref[edge_count : edge_count + node_count, :]
    incoming = edge_rows(
        x_ref, x_ref[edge_count:, :], nodes, edge_own, hot_ref, incidence_ref,
        edge_w, edge_w2, product_ref, edge_out, full_out,
    )
    node_copies.wait()
    node_new = node_rows(nodes, incoming, node_own, node_w, node_w2, node_out)
    node_full[...] = node_new
    pick_rows(pick_ref, node_new, sends)


def late_weights(weights, base, first, second):
    moves = Moves()
    load_packed(moves, weights[0], base, 0, first, second)
    load_packed(moves, weights[1], base, 1, first, second)
    load_packed(moves, weights[2], 0, 2, first, second)
    load_packed(moves, weights[3], 0, 3, first, second)


def late_edge_kernel(pieces, base, *refs):
    refs = list(refs)
    weights = [refs.pop(0) for _ in range(4)]
    edge_ref, edge_own = [refs.pop(0) for _ in range(2)]
    tables = [refs.pop(0) for _ in range(pieces)]
    hot_ref, incidence_ref, edge_out, incoming_out = [refs.pop(0) for _ in range(4)]
    edge_w, edge_w2, product_ref, table_ref = refs
    late_weights(weights, base, edge_w, edge_w2)
    start = 0
    for table in tables:
        table_ref[start : start + table.shape[0], :] = table[...]
        start += table.shape[0]
    incoming_out[...] = edge_rows(
        edge_ref, table_ref[...], tables[0][...], edge_own, hot_ref, incidence_ref,
        edge_w, edge_w2, product_ref, edge_out, None,
    )


def late_node_kernel(base, *refs):
    weights = refs[:4]
    node_ref, node_own, incoming_ref, node_out, node_w, node_w2 = refs[4:]
    late_weights(weights, base, node_w, node_w2)
    node_rows(node_ref[...], incoming_ref[...], node_own, node_w, node_w2, node_out)


SMEM, VMEM, ANY = pltpu.SMEM, pltpu.VMEM, pl.ANY


def call(kernel, out_shape, args, scratch, flops, name, vmem_mib=8):
    arrays = [a for _, a in args]
    moved = sum(a.size * a.dtype.itemsize for a in arrays + list(out_shape))
    moved = sum(a.size * a.dtype.itemsize for a in arrays + list(out_shape))
    return pl.pallas_call(
        kernel,
        out_shape=out_shape,
        in_specs=[pl.BlockSpec(memory_space=s) for s, _ in args],
        out_specs=[pl.BlockSpec(memory_space=VMEM)] * len(out_shape),
        scratch_shapes=scratch,
        compiler_params=pltpu.CompilerParams(vmem_limit_bytes=vmem_mib * 1024 * 1024),
        cost_estimate=pl.CostEstimate(flops=0, bytes_accessed=0, transcendentals=0),
        name=name,
    )(*arrays)


def swap(x, mask):
    size = lax.axis_size("mp")
    return lax.ppermute(x, "mp", [(i, i ^ mask) for i in range(size)])


def shift(x, by):
    size = lax.axis_size("graph")
    return lax.ppermute(x, "graph", [(i, (i + by) % size) for i in range(size)])


def after(x, *others):
    return lax.optimization_barrier((x, *others))[0]


def neighbour_rows(right, left, coarse, halo):
    if lax.axis_size("graph") == 4:
        return [shift(right, 1), shift(left, -1), shift(coarse, 2)]
    everyone = lax.all_gather(coarse, "graph", axis=0, tiled=True)
    return [shift(right[:halo], 1), shift(left[:halo], -1), everyone]


def table_index(senders, size, node_count, halo):
    coarse_start = node_count + 2 * halo
    number = jnp.maximum(senders - coarse_start, 0)
    block = (number * 43691) >> 19
    row = number - block * COARSE_DEV
    if size != 4:
        return jnp.where(senders < coarse_start, senders, coarse_start + block * COARSE_PAD + row)
    wide = halo + COARSE_PAD
    away = (block - lax.axis_index("graph")) & 3
    starts = (node_count - COARSE_DEV, node_count + wide + halo, node_count + 2 * wide, node_count + halo)
    base = jnp.where(
        away < 2,
        jnp.where(away == 0, starts[0], starts[1]),
        jnp.where(away == 2, starts[2], starts[3]),
    )
    fine = jnp.where(senders < node_count + halo, senders, senders + COARSE_PAD)
    return jnp.where(senders < coarse_start, fine, base + row)


def on_device(
    node_state,
    edge_state,
    edge_first,
    edge_second,
    node_first,
    node_second,
    senders,
    receivers,
    boundary_rows,
):
    node_count, part = node_state.shape
    edge_count = edge_state.shape[0]
    features = edge_second.shape[2]
    hidden = 4 * part
    halo = boundary_rows.shape[0] // 2
    blocks = lax.axis_size("graph")
    shape = jax.ShapeDtypeStruct
    dma = pltpu.SemaphoreType.DMA

    wide = halo + COARSE_PAD

    def sent(width):
        return [shape((n, width), BF16) for n in (wide, wide, COARSE_PAD)]

    weights = (edge_first, edge_second, node_first, node_second)
    edge_pack = edge_first.shape[1] + features
    node_pack = node_first.shape[1] + features
    late_pack = edge_pack + node_pack
    (ride,) = call(
        ride_kernel,
        [shape(((edge_pack + node_pack) // 2, part), BF16)],
        [(ANY, w) for w in weights],
        [dma((10,))],
        0,
        "layer_0_half",
        60,
    )
    near = swap(ride, 2)
    far_rows = 2 * wide + COARSE_PAD if blocks == 4 else 2 * halo + blocks * COARSE_PAD
    table_rows = node_count + far_rows
    lanes = -(-(table_rows + node_count) // 128) * 128
    right, left, coarse = call(
        start_kernel,
        sent(part),
        [(VMEM, after(node_state, ride)), (VMEM, boundary_rows[None, :])],
        [pltpu.VMEM((2 * wide + COARSE_PAD, node_count), BF16)],
        0,
        "boundary_rows",
    )
    rows = neighbour_rows(right, left, coarse, halo)
    (latents,) = call(
        latent_kernel,
        [shape((edge_count + table_rows, part), BF16)],
        [(VMEM, edge_state), (VMEM, node_state)] + [(VMEM, r) for r in rows],
        [],
        0,
        "latents",
    )
    near = after(near, *rows)
    far_latents = swap(latents, 2)
    far = lax.ppermute(near, "groups", [(0, 1), (1, 0)])
    core_latents = swap(latents, 1)
    lists = jnp.concatenate([senders, receivers, boundary_rows])[None, :]
    hot, incidence, pick, packs, edge_late, node_late = call(
        functools.partial(prepare_kernel, blocks, halo, table_rows),
        [
            shape((edge_count, lanes), BF16),
            shape((node_count, edge_count), BF16),
            shape((2 * wide + COARSE_PAD, node_count), BF16),
            shape((2 * late_pack, part), BF16),
            shape((edge_pack, part), BF16),
            shape((node_pack, part), BF16),
        ],
        [(VMEM, after(lists, *rows))] + [(ANY, w) for w in weights],
        [dma((32,))],
        0,
        "one_hot",
    )
    core_packs = swap(after(packs, near), 1)
    core_near = swap(after(near, core_latents), 1)
    core_far = swap(after(far, core_packs), 1)
    edge_late_x = swap(after(edge_late, core_latents), 2)
    node_late_x = swap(after(node_late, far_latents), 2)
    shards = [latents, core_latents, far_latents, swap(after(far_latents, far, core_packs, core_near), 1)]
    pairs = [near, far, core_near, core_far]

    edge_flops = 2 * edge_count * features * (2 * features + lanes + node_count)
    node_flops = 2 * node_count * features * 3 * features
    full_edge = shape((edge_count, features), BF16)
    full_node = shape((node_count, features), BF16)
    own_edge = shape((edge_count, part), F32)
    own_node = shape((node_count, part), F32)
    second_shape = pltpu.VMEM((hidden, features), BF16)
    edge_shape = pltpu.VMEM((edge_first.shape[1], hidden), BF16)
    node_shape = pltpu.VMEM((node_first.shape[1], hidden), BF16)

    edge_own, edge_full, node_own, node_full, right, left, coarse = call(
        first_kernel,
        [own_edge, full_edge, own_node, full_node] + sent(features),
        [(VMEM, w) for w in [packs, core_packs] + pairs + shards]
        + [(VMEM, a) for a in (edge_state, node_state, hot, incidence, pick)],
        [
            edge_shape,
            second_shape,
            node_shape,
            second_shape,
            pltpu.VMEM((lanes, hidden), BF16),
            pltpu.VMEM((edge_count + table_rows, features), BF16),
        ],
        edge_flops + node_flops,
        "layer_0",
        16,
    )
    tables = [node_full] + neighbour_rows(right, left, coarse, halo)
    edge_late_d = swap(after(edge_late_x, right), 1)
    edge_own, incoming = call(
        functools.partial(late_edge_kernel, len(tables), late_pack),
        [own_edge, full_node],
        [(VMEM, w) for w in (packs, core_packs, edge_late_x, edge_late_d)]
        + [(VMEM, a) for a in (edge_full, edge_own)]
        + [(VMEM, t) for t in tables]
        + [(VMEM, hot), (VMEM, incidence)],
        [
            edge_shape,
            second_shape,
            pltpu.VMEM((lanes, hidden), BF16),
            pltpu.VMEM((table_rows, features), BF16),
        ],
        edge_flops,
        "layer_1_edges",
        16,
    )
    node_late_d = swap(after(node_late_x, *tables[1:]), 1)
    (node_own,) = call(
        functools.partial(late_node_kernel, late_pack + edge_pack),
        [own_node],
        [(VMEM, w) for w in (packs, core_packs, node_late_x, node_late_d)]
        + [(VMEM, a) for a in (node_full, node_own, incoming)],
        [node_shape, second_shape],
        node_flops,
        "layer_1_nodes",
        16,
    )
    return (node_own, edge_own)


def solution(mesh):
    in_specs = (
        P(("groups", "graph"), "mp"),
        P(("groups", "graph"), "mp"),
        P(None, None, "mp"),
        P(None, "mp", None),
        P(None, None, "mp"),
        P(None, "mp", None),
        P("graph"),
        P("graph"),
        P("graph"),
    )
    out_specs = (P(("groups", "graph"), "mp"), P(("groups", "graph"), "mp"))
    return jax.shard_map(
        on_device, mesh=mesh, in_specs=in_specs, out_specs=out_specs, check_vma=False
    )
```

```python
import functools

import jax
import jax.numpy as jnp
from jax import lax
from jax.experimental import pallas as pl
from jax.experimental.pallas import tpu as pltpu
from jax.sharding import PartitionSpec as P

COARSE_DEV = 12
COARSE_PAD = 16
EPS = 1e-05
TILE = 768
HOT_TILE = 256
F32 = jnp.float32
BF16 = jnp.bfloat16


def silu(x):
    half = 0.5 * x
    return half + half * jnp.tanh(half)


def normalize(msg):
    width = msg.shape[1]
    mean = jnp.sum(msg, axis=1, keepdims=True) * (1.0 / width)
    square = jnp.sum(msg * msg, axis=1, keepdims=True) * (1.0 / width)
    return (msg - mean) * lax.rsqrt(square - mean * mean + EPS)


def dot(a, b):
    return jnp.dot(a, b, preferred_element_type=F32)


def own_columns(full, part):
    mine = lax.axis_index("mp")
    out = full[:, 0:part]
    for j in range(1, full.shape[1] // part):
        out = jnp.where(mine == j, full[:, j * part : (j + 1) * part], out)
    return out


class Copies:
    def __init__(self, sems):
        self.sems, self.started = sems, []

    def start(self, source, target):
        copy = pltpu.make_async_copy(source, target, self.sems.at[len(self.started)])
        copy.start()
        self.started.append(copy)

    def wait(self):
        for copy in self.started:
            copy.wait()


class Moves:
    def start(self, source, target):
        target[...] = source[...]

    def wait(self):
        pass


def load_shard(copies, layer, first, second, j, first_ref, second_ref):
    part = second.shape[1]
    copies.start(first.at[layer], first_ref.at[:, pl.ds(j * part, part)])
    copies.start(second.at[layer], second_ref.at[pl.ds(j * part, part)])


def load_packed(copies, packed, base, j, first_ref, second_ref):
    rows = first_ref.shape[0]
    hidden, features = second_ref.shape
    part = hidden // 4
    copies.start(packed.at[pl.ds(base, rows)], first_ref.at[:, pl.ds(j * part, part)])
    for q in range(features // part):
        copies.start(
            packed.at[pl.ds(base + rows + q * part, part)],
            second_ref.at[pl.ds(j * part, part), pl.ds(q * part, part)],
        )


def load_half(copies, packed, base, half, j, first_ref, second_ref):
    rows = first_ref.shape[0] // 2
    hidden, features = second_ref.shape
    part = hidden // 4
    deep = part // 2
    at = pl.multiple_of(half * rows, rows)
    copies.start(packed.at[pl.ds(base, rows)], first_ref.at[pl.ds(at, rows), pl.ds(j * part, part)])
    at = pl.multiple_of(j * part + half * deep, deep)
    for q in range(features // part):
        copies.start(
            packed.at[pl.ds(base + rows + q * deep, deep)],
            second_ref.at[pl.ds(at, deep), pl.ds(q * part, part)],
        )
    return base + rows + features // part * deep


def ride_kernel(ef, es, nf, ns, ride_out, sems):
    y = lax.axis_index("groups")
    part, features = es.shape[1:]
    copies = Copies(sems)
    at = 0
    for first, second in ((ef, es), (nf, ns)):
        rows = first.shape[1] // 2
        source = first.at[0, pl.ds(pl.multiple_of(y * rows, rows), rows)]
        copies.start(source, ride_out.at[pl.ds(at, rows)])
        at += rows
        deep = part // 2
        for q in range(features // part):
            source = second.at[0, pl.ds(pl.multiple_of(y * deep, deep), deep), pl.ds(q * part, part)]
            copies.start(source, ride_out.at[pl.ds(at, deep)])
            at += deep
    copies.wait()


def one_hot(hit):
    return jnp.where(hit, 1.0, 0.0).astype(BF16)


def column(row):
    return jnp.broadcast_to(row, (8, row.shape[1])).T[:, 0:1]


def make_pick(boundary, pick_out):
    halo = boundary.shape[1] // 2
    node_count = pick_out.shape[1]
    wanted = column(boundary)
    lanes = lax.broadcasted_iota(jnp.int32, (halo, node_count), 1)
    number = lax.broadcasted_iota(jnp.int32, (COARSE_PAD, node_count), 0)
    ids = lax.broadcasted_iota(jnp.int32, (COARSE_PAD, node_count), 1)
    coarse = one_hot((ids == number + (node_count - COARSE_DEV)) & (number < COARSE_DEV))
    wide = halo + COARSE_PAD
    pick_out[0:halo, :] = one_hot(lanes == wanted[halo:])
    pick_out[wide : wide + halo, :] = one_hot(lanes == wanted[:halo])
    for at in (halo, wide + halo, 2 * wide):
        pick_out[at : at + COARSE_PAD, :] = coarse


def pack_kernel(ef, es, nf, ns, pack_out, edge_late, node_late, sems):
    part, features = es.shape[1:]
    copies = Copies(sems)

    def pack(first, second, layer, out, at):
        rows = first.shape[1]
        copies.start(first.at[layer], out.at[pl.ds(at, rows)])
        at += rows
        for q in range(features // part):
            copies.start(second.at[layer, :, pl.ds(q * part, part)], out.at[pl.ds(at, part)])
            at += part
        return at

    end = 0
    for layer in range(ef.shape[0]):
        end = pack(nf, ns, layer, pack_out, pack(ef, es, layer, pack_out, end))
    pack(ef, es, 1, edge_late, 0)
    pack(nf, ns, 1, node_late, 0)
    copies.wait()


def prepare_kernel(blocks, halo, table_rows, list_ref, hot_out, incidence_out, pick_out):
    edge_count, lanes_all = hot_out.shape
    node_count = incidence_out.shape[0]
    for at in range(0, edge_count, HOT_TILE):
        senders = table_index(list_ref[:, at : at + HOT_TILE], blocks, node_count, halo)
        receivers = list_ref[:, edge_count + at : edge_count + at + HOT_TILE]
        lanes = lax.broadcasted_iota(jnp.int32, (HOT_TILE, lanes_all), 1)
        hit = (lanes == column(senders)) | (lanes == column(receivers) + table_rows)
        hot_out[at : at + HOT_TILE, :] = one_hot(hit)
        node_ids = lax.broadcasted_iota(jnp.int32, (node_count, HOT_TILE), 0)
        incidence_out[:, at : at + HOT_TILE] = one_hot(node_ids == receivers)
    make_pick(list_ref[:, 2 * edge_count : 2 * edge_count + 2 * halo], pick_out)


def pick_rows(pick_ref, node_bf, outs):
    picked = dot(pick_ref[...], node_bf).astype(BF16)
    start = 0
    for out in outs:
        out[...] = picked[start : start + out.shape[0]]
        start += out.shape[0]


def start_kernel(at, node_ref, list_ref, right, left, coarse, pick_ref):
    make_pick(list_ref[:, at:], pick_ref)
    pick_rows(pick_ref, node_ref[...].astype(BF16), (right, left, coarse))


def latent_kernel(*refs):
    out = refs[-1]
    at = 0
    for piece in refs[:-1]:
        out[at : at + piece.shape[0], :] = piece[...].astype(BF16)
        at += piece.shape[0]


def edge_rows(edge_ref, table, nodes, own_ref, hot_ref, incidence_ref, first_ref, second_ref, product_ref, own_out, full_out):
    features = second_ref.shape[1]
    node_count = nodes.shape[0]
    table_rows = table.shape[0]
    lanes_all = product_ref.shape[0]
    used = table_rows + node_count
    part = own_ref.shape[1]
    product_ref[0:table_rows, :] = dot(table, first_ref[features : 2 * features, :]).astype(BF16)
    product_ref[table_rows:used, :] = dot(
        nodes, first_ref[2 * features : 3 * features, :]
    ).astype(BF16)
    if used < lanes_all:
        product_ref[used:, :] = jnp.zeros((lanes_all - used, features), BF16)
    incoming = jnp.zeros((node_count, features), F32)
    for at in range(0, own_ref.shape[0], TILE):
        rows = slice(at, at + TILE)
        edge_bf = edge_ref[rows, :]
        pre = dot(edge_bf, first_ref[0:features, :]) + dot(hot_ref[rows, :], product_ref[...])
        norm = normalize(dot(silu(pre).astype(BF16), second_ref[...]))
        edge_new = (edge_bf.astype(F32) + norm).astype(BF16)
        if full_out is not None:
            full_out[rows, :] = edge_new
        own_out[rows, :] = own_ref[rows, :] + own_columns(norm, part)
        incoming = incoming + dot(incidence_ref[:, rows], edge_new)
    return incoming.astype(BF16)


def node_rows(node_bf, incoming, own_ref, first_ref, second_ref, own_out):
    features = second_ref.shape[1]
    pre = dot(node_bf, first_ref[0:features, :]) + dot(incoming, first_ref[features:, :])
    norm = normalize(dot(silu(pre).astype(BF16), second_ref[...]))
    own_out[...] = own_ref[...] + own_columns(norm, own_ref.shape[1])
    return (node_bf.astype(F32) + norm).astype(BF16)


def first_kernel(*refs):
    refs = list(refs)
    packs = [refs.pop(0) for _ in range(2)]
    halves = [[refs.pop(0) for _ in range(2)] for _ in range(2)]
    shards = [refs.pop(0) for _ in range(4)]
    edge_own, node_own, hot_ref, incidence_ref, pick_ref = [refs.pop(0) for _ in range(5)]
    edge_out, full_out, node_out, node_full = [refs.pop(0) for _ in range(4)]
    sends = [refs.pop(0) for _ in range(3)]
    edge_w, edge_w2, node_w, node_w2, product_ref, x_ref = refs
    part = edge_own.shape[1]
    edge_count = edge_own.shape[0]
    node_count = node_own.shape[0]
    edge_copies, node_copies = Moves(), Moves()
    for j, shard in enumerate(shards):
        column = pl.multiple_of((lax.axis_index("mp") ^ j) * part, part)
        edge_copies.start(shard, x_ref.at[:, pl.ds(column, part)])
    y = lax.axis_index("groups")
    starts = [0, 0]
    for base, copies, (first, second) in (
        (0, edge_copies, (edge_w, edge_w2)),
        (1, node_copies, (node_w, node_w2)),
    ):
        for j, pack in enumerate(packs):
            load_packed(copies, pack, (0, edge_w.shape[0] + edge_w2.shape[1])[base], j, first, second)
        for j, pair in enumerate(halves):
            for k, piece in enumerate(pair):
                half = y if k == 0 else 1 - y
                end = load_half(copies, piece, starts[base], half, 2 + j, first, second)
        starts[1] = end
    edge_copies.wait()
    nodes = x_ref[edge_count : edge_count + node_count, :]
    incoming = edge_rows(
        x_ref, x_ref[edge_count:, :], nodes, edge_own, hot_ref, incidence_ref,
        edge_w, edge_w2, product_ref, edge_out, full_out,
    )
    node_copies.wait()
    node_new = node_rows(nodes, incoming, node_own, node_w, node_w2, node_out)
    node_full[...] = node_new
    pick_rows(pick_ref, node_new, sends)


def late_weights(weights, base, first, second):
    moves = Moves()
    load_packed(moves, weights[0], base, 0, first, second)
    load_packed(moves, weights[1], base, 1, first, second)
    load_packed(moves, weights[2], 0, 2, first, second)
    load_packed(moves, weights[3], 0, 3, first, second)


def late_edge_kernel(pieces, base, *refs):
    refs = list(refs)
    weights = [refs.pop(0) for _ in range(4)]
    edge_ref, edge_own = [refs.pop(0) for _ in range(2)]
    tables = [refs.pop(0) for _ in range(pieces)]
    hot_ref, incidence_ref, edge_out, incoming_out = [refs.pop(0) for _ in range(4)]
    edge_w, edge_w2, product_ref, table_ref = refs
    late_weights(weights, base, edge_w, edge_w2)
    start = 0
    for table in tables:
        table_ref[start : start + table.shape[0], :] = table[...]
        start += table.shape[0]
    incoming_out[...] = edge_rows(
        edge_ref, table_ref[...], tables[0][...], edge_own, hot_ref, incidence_ref,
        edge_w, edge_w2, product_ref, edge_out, None,
    )


def late_node_kernel(base, *refs):
    weights = refs[:4]
    node_ref, node_own, incoming_ref, node_out, node_w, node_w2 = refs[4:]
    late_weights(weights, base, node_w, node_w2)
    node_rows(node_ref[...], incoming_ref[...], node_own, node_w, node_w2, node_out)


SMEM, VMEM, ANY = pltpu.SMEM, pltpu.VMEM, pl.ANY


def call(kernel, out_shape, args, scratch, flops, name, vmem_mib=8):
    arrays = [a for _, a in args]
    moved = sum(a.size * a.dtype.itemsize for a in arrays + list(out_shape))
    moved = sum(a.size * a.dtype.itemsize for a in arrays + list(out_shape))
    return pl.pallas_call(
        kernel,
        out_shape=out_shape,
        in_specs=[pl.BlockSpec(memory_space=s) for s, _ in args],
        out_specs=[pl.BlockSpec(memory_space=VMEM)] * len(out_shape),
        scratch_shapes=scratch,
        compiler_params=pltpu.CompilerParams(vmem_limit_bytes=vmem_mib * 1024 * 1024),
        cost_estimate=pl.CostEstimate(flops=0, bytes_accessed=0, transcendentals=0),
        name=name,
    )(*arrays)


def swap(x, mask):
    size = lax.axis_size("mp")
    return lax.ppermute(x, "mp", [(i, i ^ mask) for i in range(size)])


def shift(x, by):
    size = lax.axis_size("graph")
    return lax.ppermute(x, "graph", [(i, (i + by) % size) for i in range(size)])


def after(x, *others):
    return lax.optimization_barrier((x, *others))[0]


def neighbour_rows(right, left, coarse, halo):
    if lax.axis_size("graph") == 4:
        return [shift(right, 1), shift(left, -1), shift(coarse, 2)]
    everyone = lax.all_gather(coarse, "graph", axis=0, tiled=True)
    return [shift(right[:halo], 1), shift(left[:halo], -1), everyone]


def table_index(senders, size, node_count, halo):
    coarse_start = node_count + 2 * halo
    number = jnp.maximum(senders - coarse_start, 0)
    block = (number * 43691) >> 19
    row = number - block * COARSE_DEV
    if size != 4:
        return jnp.where(senders < coarse_start, senders, coarse_start + block * COARSE_PAD + row)
    wide = halo + COARSE_PAD
    away = (block - lax.axis_index("graph")) & 3
    starts = (node_count - COARSE_DEV, node_count + wide + halo, node_count + 2 * wide, node_count + halo)
    base = jnp.where(
        away < 2,
        jnp.where(away == 0, starts[0], starts[1]),
        jnp.where(away == 2, starts[2], starts[3]),
    )
    fine = jnp.where(senders < node_count + halo, senders, senders + COARSE_PAD)
    return jnp.where(senders < coarse_start, fine, base + row)


def on_device(
    node_state,
    edge_state,
    edge_first,
    edge_second,
    node_first,
    node_second,
    senders,
    receivers,
    boundary_rows,
):
    node_count, part = node_state.shape
    edge_count = edge_state.shape[0]
    features = edge_second.shape[2]
    hidden = 4 * part
    halo = boundary_rows.shape[0] // 2
    blocks = lax.axis_size("graph")
    shape = jax.ShapeDtypeStruct
    dma = pltpu.SemaphoreType.DMA

    wide = halo + COARSE_PAD

    def sent(width):
        return [shape((n, width), BF16) for n in (wide, wide, COARSE_PAD)]

    weights = (edge_first, edge_second, node_first, node_second)
    edge_pack = edge_first.shape[1] + features
    node_pack = node_first.shape[1] + features
    late_pack = edge_pack + node_pack
    (ride,) = call(
        ride_kernel,
        [shape(((edge_pack + node_pack) // 2, part), BF16)],
        [(ANY, w) for w in weights],
        [dma((10,))],
        0,
        "layer_0_half",
        60,
    )
    near = swap(ride, 2)
    far_rows = 2 * wide + COARSE_PAD if blocks == 4 else 2 * halo + blocks * COARSE_PAD
    table_rows = node_count + far_rows
    lanes = -(-(table_rows + node_count) // 128) * 128
    lists = jnp.concatenate([senders, receivers, boundary_rows])[None, :]
    right, left, coarse = call(
        functools.partial(start_kernel, 2 * edge_count),
        sent(part),
        [(VMEM, after(node_state, ride)), (VMEM, lists)],
        [pltpu.VMEM((2 * wide + COARSE_PAD, node_count), BF16)],
        0,
        "boundary_rows",
    )
    rows = neighbour_rows(right, left, coarse, halo)
    (latents,) = call(
        latent_kernel,
        [shape((edge_count + table_rows, part), BF16)],
        [(VMEM, edge_state), (VMEM, node_state)] + [(VMEM, r) for r in rows],
        [],
        0,
        "latents",
    )
    near = after(near, *rows)
    far_latents = swap(latents, 2)
    far = lax.ppermute(near, "groups", [(0, 1), (1, 0)])
    core_latents = swap(latents, 1)
    packs, edge_late, node_late = call(
        pack_kernel,
        [shape((n, part), BF16) for n in (2 * late_pack, edge_pack, node_pack)],
        [(ANY, after(weights[0], *rows))] + [(ANY, w) for w in weights[1:]],
        [dma((32,))],
        0,
        "packed_weights",
    )
    core_packs = swap(after(packs, near), 1)
    hot, incidence, pick = call(
        functools.partial(prepare_kernel, blocks, halo, table_rows),
        [
            shape((edge_count, lanes), BF16),
            shape((node_count, edge_count), BF16),
            shape((2 * wide + COARSE_PAD, node_count), BF16),
        ],
        [(VMEM, after(lists, core_latents))],
        [],
        0,
        "one_hot",
    )
    core_near = swap(after(near, core_latents), 1)
    core_far = swap(after(far, core_packs), 1)
    edge_late_x = swap(after(edge_late, core_latents, hot), 2)
    node_late_x = swap(after(node_late, far_latents), 2)
    shards = [latents, core_latents, far_latents, swap(after(far_latents, far, core_packs, core_near), 1)]
    pairs = [near, far, core_near, core_far]

    edge_flops = 2 * edge_count * features * (2 * features + lanes + node_count)
    node_flops = 2 * node_count * features * 3 * features
    full_edge = shape((edge_count, features), BF16)
    full_node = shape((node_count, features), BF16)
    own_edge = shape((edge_count, part), F32)
    own_node = shape((node_count, part), F32)
    second_shape = pltpu.VMEM((hidden, features), BF16)
    edge_shape = pltpu.VMEM((edge_first.shape[1], hidden), BF16)
    node_shape = pltpu.VMEM((node_first.shape[1], hidden), BF16)

    edge_own, edge_full, node_own, node_full, right, left, coarse = call(
        first_kernel,
        [own_edge, full_edge, own_node, full_node] + sent(features),
        [(VMEM, w) for w in [packs, core_packs] + pairs + shards]
        + [(VMEM, a) for a in (edge_state, node_state, hot, incidence, pick)],
        [
            edge_shape,
            second_shape,
            node_shape,
            second_shape,
            pltpu.VMEM((lanes, hidden), BF16),
            pltpu.VMEM((edge_count + table_rows, features), BF16),
        ],
        edge_flops + node_flops,
        "layer_0",
        16,
    )
    tables = [node_full] + neighbour_rows(right, left, coarse, halo)
    edge_late_d = swap(after(edge_late_x, right), 1)
    edge_own, incoming = call(
        functools.partial(late_edge_kernel, len(tables), late_pack),
        [own_edge, full_node],
        [(VMEM, w) for w in (packs, core_packs, edge_late_x, edge_late_d)]
        + [(VMEM, a) for a in (edge_full, edge_own)]
        + [(VMEM, t) for t in tables]
        + [(VMEM, hot), (VMEM, incidence)],
        [
            edge_shape,
            second_shape,
            pltpu.VMEM((lanes, hidden), BF16),
            pltpu.VMEM((table_rows, features), BF16),
        ],
        edge_flops,
        "layer_1_edges",
        16,
    )
    node_late_d = swap(after(node_late_x, *tables[1:]), 1)
    (node_own,) = call(
        functools.partial(late_node_kernel, late_pack + edge_pack),
        [own_node],
        [(VMEM, w) for w in (packs, core_packs, node_late_x, node_late_d)]
        + [(VMEM, a) for a in (node_full, node_own, incoming)],
        [node_shape, second_shape],
        node_flops,
        "layer_1_nodes",
        16,
    )
    return (node_own, edge_own)


def solution(mesh):
    in_specs = (
        P(("groups", "graph"), "mp"),
        P(("groups", "graph"), "mp"),
        P(None, None, "mp"),
        P(None, "mp", None),
        P(None, None, "mp"),
        P(None, "mp", None),
        P("graph"),
        P("graph"),
        P("graph"),
    )
    out_specs = (P(("groups", "graph"), "mp"), P(("groups", "graph"), "mp"))
    return jax.shard_map(
        on_device, mesh=mesh, in_specs=in_specs, out_specs=out_specs, check_vma=False
    )
```

```python
import functools

import jax
import jax.numpy as jnp
from jax import lax
from jax.experimental import pallas as pl
from jax.experimental.pallas import tpu as pltpu
from jax.sharding import PartitionSpec as P

COARSE_DEV = 12
COARSE_PAD = 16
EPS = 1e-05
TILE = 768
HOT_TILE = 256
F32 = jnp.float32
BF16 = jnp.bfloat16


def silu(x):
    half = x.astype(BF16) * jnp.asarray(0.5, BF16)
    return half + half * jnp.tanh(half)


def normalize(msg):
    width = msg.shape[1]
    mean = jnp.sum(msg, axis=1, keepdims=True) * (1.0 / width)
    square = jnp.sum(msg * msg, axis=1, keepdims=True) * (1.0 / width)
    return (msg - mean) * lax.rsqrt(square - mean * mean + EPS)


def dot(a, b):
    return jnp.dot(a, b, preferred_element_type=F32)


def own_columns(full, part):
    mine = lax.axis_index("mp")
    out = full[:, 0:part]
    for j in range(1, full.shape[1] // part):
        out = jnp.where(mine == j, full[:, j * part : (j + 1) * part], out)
    return out


class Copies:
    def __init__(self, sems):
        self.sems, self.started = sems, []

    def start(self, source, target):
        copy = pltpu.make_async_copy(source, target, self.sems.at[len(self.started)])
        copy.start()
        self.started.append(copy)

    def wait(self):
        for copy in self.started:
            copy.wait()


class Moves:
    def start(self, source, target):
        target[...] = source[...]

    def wait(self):
        pass


def load_shard(copies, layer, first, second, j, first_ref, second_ref):
    part = second.shape[1]
    copies.start(first.at[layer], first_ref.at[:, pl.ds(j * part, part)])
    copies.start(second.at[layer], second_ref.at[pl.ds(j * part, part)])


def load_packed(copies, packed, base, j, first_ref, second_ref):
    rows = first_ref.shape[0]
    hidden, features = second_ref.shape
    part = hidden // 4
    copies.start(packed.at[pl.ds(base, rows)], first_ref.at[:, pl.ds(j * part, part)])
    for q in range(features // part):
        copies.start(
            packed.at[pl.ds(base + rows + q * part, part)],
            second_ref.at[pl.ds(j * part, part), pl.ds(q * part, part)],
        )


def load_half(copies, packed, base, half, j, first_ref, second_ref):
    rows = first_ref.shape[0] // 2
    hidden, features = second_ref.shape
    part = hidden // 4
    deep = part // 2
    at = pl.multiple_of(half * rows, rows)
    copies.start(packed.at[pl.ds(base, rows)], first_ref.at[pl.ds(at, rows), pl.ds(j * part, part)])
    at = pl.multiple_of(j * part + half * deep, deep)
    for q in range(features // part):
        copies.start(
            packed.at[pl.ds(base + rows + q * deep, deep)],
            second_ref.at[pl.ds(at, deep), pl.ds(q * part, part)],
        )
    return base + rows + features // part * deep


def ride_kernel(ef, es, nf, ns, ride_out, sems):
    y = lax.axis_index("groups")
    part, features = es.shape[1:]
    copies = Copies(sems)
    at = 0
    for first, second in ((ef, es), (nf, ns)):
        rows = first.shape[1] // 2
        source = first.at[0, pl.ds(pl.multiple_of(y * rows, rows), rows)]
        copies.start(source, ride_out.at[pl.ds(at, rows)])
        at += rows
        deep = part // 2
        for q in range(features // part):
            source = second.at[0, pl.ds(pl.multiple_of(y * deep, deep), deep), pl.ds(q * part, part)]
            copies.start(source, ride_out.at[pl.ds(at, deep)])
            at += deep
    copies.wait()


def one_hot(hit):
    return jnp.where(hit, 1.0, 0.0).astype(BF16)


def column(row):
    return jnp.broadcast_to(row, (8, row.shape[1])).T[:, 0:1]


def make_pick(boundary, pick_out):
    halo = boundary.shape[1] // 2
    node_count = pick_out.shape[1]
    wanted = column(boundary)
    lanes = lax.broadcasted_iota(jnp.int32, (halo, node_count), 1)
    number = lax.broadcasted_iota(jnp.int32, (COARSE_PAD, node_count), 0)
    ids = lax.broadcasted_iota(jnp.int32, (COARSE_PAD, node_count), 1)
    coarse = one_hot((ids == number + (node_count - COARSE_DEV)) & (number < COARSE_DEV))
    wide = halo + COARSE_PAD
    pick_out[0:halo, :] = one_hot(lanes == wanted[halo:])
    pick_out[wide : wide + halo, :] = one_hot(lanes == wanted[:halo])
    for at in (halo, wide + halo, 2 * wide):
        pick_out[at : at + COARSE_PAD, :] = coarse


def pack_kernel(ef, es, nf, ns, pack_out, edge_late, node_late, sems):
    part, features = es.shape[1:]
    copies = Copies(sems)

    def pack(first, second, layer, out, at):
        rows = first.shape[1]
        copies.start(first.at[layer], out.at[pl.ds(at, rows)])
        at += rows
        for q in range(features // part):
            copies.start(second.at[layer, :, pl.ds(q * part, part)], out.at[pl.ds(at, part)])
            at += part
        return at

    end = 0
    for layer in range(ef.shape[0]):
        end = pack(nf, ns, layer, pack_out, pack(ef, es, layer, pack_out, end))
    pack(ef, es, 1, edge_late, 0)
    pack(nf, ns, 1, node_late, 0)
    copies.wait()


def prepare_kernel(blocks, halo, table_rows, list_ref, hot_out, incidence_out, pick_out):
    edge_count, lanes_all = hot_out.shape
    node_count = incidence_out.shape[0]
    for at in range(0, edge_count, HOT_TILE):
        senders = table_index(list_ref[:, at : at + HOT_TILE], blocks, node_count, halo)
        receivers = list_ref[:, edge_count + at : edge_count + at + HOT_TILE]
        lanes = lax.broadcasted_iota(jnp.int32, (HOT_TILE, lanes_all), 1)
        hit = (lanes == column(senders)) | (lanes == column(receivers) + table_rows)
        hot_out[at : at + HOT_TILE, :] = one_hot(hit)
        node_ids = lax.broadcasted_iota(jnp.int32, (node_count, HOT_TILE), 0)
        incidence_out[:, at : at + HOT_TILE] = one_hot(node_ids == receivers)
    make_pick(list_ref[:, 2 * edge_count : 2 * edge_count + 2 * halo], pick_out)


def pick_rows(pick_ref, node_bf, outs):
    picked = dot(pick_ref[...], node_bf).astype(BF16)
    start = 0
    for out in outs:
        out[...] = picked[start : start + out.shape[0]]
        start += out.shape[0]


def start_kernel(at, node_ref, list_ref, right, left, coarse, pick_ref):
    make_pick(list_ref[:, at:], pick_ref)
    pick_rows(pick_ref, node_ref[...].astype(BF16), (right, left, coarse))


def latent_kernel(*refs):
    out = refs[-1]
    at = 0
    for piece in refs[:-1]:
        out[at : at + piece.shape[0], :] = piece[...].astype(BF16)
        at += piece.shape[0]


def edge_rows(edge_ref, table, nodes, own_ref, hot_ref, incidence_ref, first_ref, second_ref, product_ref, own_out, full_out):
    features = second_ref.shape[1]
    node_count = nodes.shape[0]
    table_rows = table.shape[0]
    lanes_all = product_ref.shape[0]
    used = table_rows + node_count
    part = own_ref.shape[1]
    product_ref[0:table_rows, :] = dot(table, first_ref[features : 2 * features, :]).astype(BF16)
    product_ref[table_rows:used, :] = dot(
        nodes, first_ref[2 * features : 3 * features, :]
    ).astype(BF16)
    if used < lanes_all:
        product_ref[used:, :] = jnp.zeros((lanes_all - used, features), BF16)
    incoming = jnp.zeros((node_count, features), F32)
    for at in range(0, own_ref.shape[0], TILE):
        rows = slice(at, at + TILE)
        edge_bf = edge_ref[rows, :]
        pre = dot(edge_bf, first_ref[0:features, :]) + dot(hot_ref[rows, :], product_ref[...])
        norm = normalize(dot(silu(pre), second_ref[...]))
        edge_new = (edge_bf.astype(F32) + norm).astype(BF16)
        if full_out is not None:
            full_out[rows, :] = edge_new
        own_out[rows, :] = own_ref[rows, :] + own_columns(norm, part)
        incoming = incoming + dot(incidence_ref[:, rows], edge_new)
    return incoming.astype(BF16)


def node_rows(node_bf, incoming, own_ref, first_ref, second_ref, own_out):
    features = second_ref.shape[1]
    pre = dot(node_bf, first_ref[0:features, :]) + dot(incoming, first_ref[features:, :])
    norm = normalize(dot(silu(pre), second_ref[...]))
    own_out[...] = own_ref[...] + own_columns(norm, own_ref.shape[1])
    return (node_bf.astype(F32) + norm).astype(BF16)


def first_kernel(*refs):
    refs = list(refs)
    packs = [refs.pop(0) for _ in range(2)]
    halves = [[refs.pop(0) for _ in range(2)] for _ in range(2)]
    shards = [refs.pop(0) for _ in range(4)]
    edge_own, node_own, hot_ref, incidence_ref, pick_ref = [refs.pop(0) for _ in range(5)]
    edge_out, full_out, node_out, node_full = [refs.pop(0) for _ in range(4)]
    sends = [refs.pop(0) for _ in range(3)]
    edge_w, edge_w2, node_w, node_w2, product_ref, x_ref = refs
    part = edge_own.shape[1]
    edge_count = edge_own.shape[0]
    node_count = node_own.shape[0]
    edge_copies, node_copies = Moves(), Moves()
    for j, shard in enumerate(shards):
        column = pl.multiple_of((lax.axis_index("mp") ^ j) * part, part)
        edge_copies.start(shard, x_ref.at[:, pl.ds(column, part)])
    y = lax.axis_index("groups")
    starts = [0, 0]
    for base, copies, (first, second) in (
        (0, edge_copies, (edge_w, edge_w2)),
        (1, node_copies, (node_w, node_w2)),
    ):
        for j, pack in enumerate(packs):
            load_packed(copies, pack, (0, edge_w.shape[0] + edge_w2.shape[1])[base], j, first, second)
        for j, pair in enumerate(halves):
            for k, piece in enumerate(pair):
                half = y if k == 0 else 1 - y
                end = load_half(copies, piece, starts[base], half, 2 + j, first, second)
        starts[1] = end
    edge_copies.wait()
    nodes = x_ref[edge_count : edge_count + node_count, :]
    incoming = edge_rows(
        x_ref, x_ref[edge_count:, :], nodes, edge_own, hot_ref, incidence_ref,
        edge_w, edge_w2, product_ref, edge_out, full_out,
    )
    node_copies.wait()
    node_new = node_rows(nodes, incoming, node_own, node_w, node_w2, node_out)
    node_full[...] = node_new
    pick_rows(pick_ref, node_new, sends)


def late_weights(weights, base, first, second):
    moves = Moves()
    load_packed(moves, weights[0], base, 0, first, second)
    load_packed(moves, weights[1], base, 1, first, second)
    load_packed(moves, weights[2], 0, 2, first, second)
    load_packed(moves, weights[3], 0, 3, first, second)


def late_edge_kernel(pieces, base, *refs):
    refs = list(refs)
    weights = [refs.pop(0) for _ in range(4)]
    edge_ref, edge_own = [refs.pop(0) for _ in range(2)]
    tables = [refs.pop(0) for _ in range(pieces)]
    hot_ref, incidence_ref, edge_out, incoming_out = [refs.pop(0) for _ in range(4)]
    edge_w, edge_w2, product_ref, table_ref = refs
    late_weights(weights, base, edge_w, edge_w2)
    start = 0
    for table in tables:
        table_ref[start : start + table.shape[0], :] = table[...]
        start += table.shape[0]
    incoming_out[...] = edge_rows(
        edge_ref, table_ref[...], tables[0][...], edge_own, hot_ref, incidence_ref,
        edge_w, edge_w2, product_ref, edge_out, None,
    )


def late_node_kernel(base, *refs):
    weights = refs[:4]
    node_ref, node_own, incoming_ref, node_out, node_w, node_w2 = refs[4:]
    late_weights(weights, base, node_w, node_w2)
    node_rows(node_ref[...], incoming_ref[...], node_own, node_w, node_w2, node_out)


SMEM, VMEM, ANY = pltpu.SMEM, pltpu.VMEM, pl.ANY


def call(kernel, out_shape, args, scratch, flops, name, vmem_mib=8):
    arrays = [a for _, a in args]
    moved = sum(a.size * a.dtype.itemsize for a in arrays + list(out_shape))
    moved = sum(a.size * a.dtype.itemsize for a in arrays + list(out_shape))
    return pl.pallas_call(
        kernel,
        out_shape=out_shape,
        in_specs=[pl.BlockSpec(memory_space=s) for s, _ in args],
        out_specs=[pl.BlockSpec(memory_space=VMEM)] * len(out_shape),
        scratch_shapes=scratch,
        compiler_params=pltpu.CompilerParams(vmem_limit_bytes=vmem_mib * 1024 * 1024),
        cost_estimate=pl.CostEstimate(flops=0, bytes_accessed=0, transcendentals=0),
        name=name,
    )(*arrays)


def swap(x, mask):
    size = lax.axis_size("mp")
    return lax.ppermute(x, "mp", [(i, i ^ mask) for i in range(size)])


def shift(x, by):
    size = lax.axis_size("graph")
    return lax.ppermute(x, "graph", [(i, (i + by) % size) for i in range(size)])


def after(x, *others):
    return lax.optimization_barrier((x, *others))[0]


def neighbour_rows(right, left, coarse, halo):
    if lax.axis_size("graph") == 4:
        return [shift(right, 1), shift(left, -1), shift(coarse, 2)]
    everyone = lax.all_gather(coarse, "graph", axis=0, tiled=True)
    return [shift(right[:halo], 1), shift(left[:halo], -1), everyone]


def table_index(senders, size, node_count, halo):
    coarse_start = node_count + 2 * halo
    number = jnp.maximum(senders - coarse_start, 0)
    block = (number * 43691) >> 19
    row = number - block * COARSE_DEV
    if size != 4:
        return jnp.where(senders < coarse_start, senders, coarse_start + block * COARSE_PAD + row)
    wide = halo + COARSE_PAD
    away = (block - lax.axis_index("graph")) & 3
    starts = (node_count - COARSE_DEV, node_count + wide + halo, node_count + 2 * wide, node_count + halo)
    base = jnp.where(
        away < 2,
        jnp.where(away == 0, starts[0], starts[1]),
        jnp.where(away == 2, starts[2], starts[3]),
    )
    fine = jnp.where(senders < node_count + halo, senders, senders + COARSE_PAD)
    return jnp.where(senders < coarse_start, fine, base + row)


def on_device(
    node_state,
    edge_state,
    edge_first,
    edge_second,
    node_first,
    node_second,
    senders,
    receivers,
    boundary_rows,
):
    node_count, part = node_state.shape
    edge_count = edge_state.shape[0]
    features = edge_second.shape[2]
    hidden = 4 * part
    halo = boundary_rows.shape[0] // 2
    blocks = lax.axis_size("graph")
    shape = jax.ShapeDtypeStruct
    dma = pltpu.SemaphoreType.DMA

    wide = halo + COARSE_PAD

    def sent(width):
        return [shape((n, width), BF16) for n in (wide, wide, COARSE_PAD)]

    weights = (edge_first, edge_second, node_first, node_second)
    edge_pack = edge_first.shape[1] + features
    node_pack = node_first.shape[1] + features
    late_pack = edge_pack + node_pack
    (ride,) = call(
        ride_kernel,
        [shape(((edge_pack + node_pack) // 2, part), BF16)],
        [(ANY, w) for w in weights],
        [dma((10,))],
        0,
        "layer_0_half",
        60,
    )
    near = swap(ride, 2)
    far_rows = 2 * wide + COARSE_PAD if blocks == 4 else 2 * halo + blocks * COARSE_PAD
    table_rows = node_count + far_rows
    lanes = -(-(table_rows + node_count) // 128) * 128
    lists = jnp.concatenate([senders, receivers, boundary_rows])[None, :]
    right, left, coarse = call(
        functools.partial(start_kernel, 2 * edge_count),
        sent(part),
        [(VMEM, after(node_state, ride)), (VMEM, lists)],
        [pltpu.VMEM((2 * wide + COARSE_PAD, node_count), BF16)],
        0,
        "boundary_rows",
    )
    rows = neighbour_rows(right, left, coarse, halo)
    (latents,) = call(
        latent_kernel,
        [shape((edge_count + table_rows, part), BF16)],
        [(VMEM, edge_state), (VMEM, node_state)] + [(VMEM, r) for r in rows],
        [],
        0,
        "latents",
    )
    near = after(near, *rows)
    far_latents = swap(latents, 2)
    far = lax.ppermute(near, "groups", [(0, 1), (1, 0)])
    core_latents = swap(latents, 1)
    packs, edge_late, node_late = call(
        pack_kernel,
        [shape((n, part), BF16) for n in (2 * late_pack, edge_pack, node_pack)],
        [(ANY, after(weights[0], *rows))] + [(ANY, w) for w in weights[1:]],
        [dma((32,))],
        0,
        "packed_weights",
    )
    core_packs = swap(after(packs, near), 1)
    hot, incidence, pick = call(
        functools.partial(prepare_kernel, blocks, halo, table_rows),
        [
            shape((edge_count, lanes), BF16),
            shape((node_count, edge_count), BF16),
            shape((2 * wide + COARSE_PAD, node_count), BF16),
        ],
        [(VMEM, after(lists, core_latents))],
        [],
        0,
        "one_hot",
    )
    core_near = swap(after(near, core_latents), 1)
    core_far = swap(after(far, core_packs), 1)
    edge_late_x = swap(after(edge_late, core_latents, hot), 2)
    node_late_x = swap(after(node_late, far_latents), 2)
    shards = [latents, core_latents, far_latents, swap(after(far_latents, far, core_packs, core_near), 1)]
    pairs = [near, far, core_near, core_far]

    edge_flops = 2 * edge_count * features * (2 * features + lanes + node_count)
    node_flops = 2 * node_count * features * 3 * features
    full_edge = shape((edge_count, features), BF16)
    full_node = shape((node_count, features), BF16)
    own_edge = shape((edge_count, part), F32)
    own_node = shape((node_count, part), F32)
    second_shape = pltpu.VMEM((hidden, features), BF16)
    edge_shape = pltpu.VMEM((edge_first.shape[1], hidden), BF16)
    node_shape = pltpu.VMEM((node_first.shape[1], hidden), BF16)

    edge_own, edge_full, node_own, node_full, right, left, coarse = call(
        first_kernel,
        [own_edge, full_edge, own_node, full_node] + sent(features),
        [(VMEM, w) for w in [packs, core_packs] + pairs + shards]
        + [(VMEM, a) for a in (edge_state, node_state, hot, incidence, pick)],
        [
            edge_shape,
            second_shape,
            node_shape,
            second_shape,
            pltpu.VMEM((lanes, hidden), BF16),
            pltpu.VMEM((edge_count + table_rows, features), BF16),
        ],
        edge_flops + node_flops,
        "layer_0",
        16,
    )
    tables = [node_full] + neighbour_rows(right, left, coarse, halo)
    edge_late_d = swap(after(edge_late_x, right), 1)
    edge_own, incoming = call(
        functools.partial(late_edge_kernel, len(tables), late_pack),
        [own_edge, full_node],
        [(VMEM, w) for w in (packs, core_packs, edge_late_x, edge_late_d)]
        + [(VMEM, a) for a in (edge_full, edge_own)]
        + [(VMEM, t) for t in tables]
        + [(VMEM, hot), (VMEM, incidence)],
        [
            edge_shape,
            second_shape,
            pltpu.VMEM((lanes, hidden), BF16),
            pltpu.VMEM((table_rows, features), BF16),
        ],
        edge_flops,
        "layer_1_edges",
        16,
    )
    node_late_d = swap(after(node_late_x, *tables[1:]), 1)
    (node_own,) = call(
        functools.partial(late_node_kernel, late_pack + edge_pack),
        [own_node],
        [(VMEM, w) for w in (packs, core_packs, node_late_x, node_late_d)]
        + [(VMEM, a) for a in (node_full, node_own, incoming)],
        [node_shape, second_shape],
        node_flops,
        "layer_1_nodes",
        16,
    )
    return (node_own, edge_own)


def solution(mesh):
    in_specs = (
        P(("groups", "graph"), "mp"),
        P(("groups", "graph"), "mp"),
        P(None, None, "mp"),
        P(None, "mp", None),
        P(None, None, "mp"),
        P(None, "mp", None),
        P("graph"),
        P("graph"),
        P("graph"),
    )
    out_specs = (P(("groups", "graph"), "mp"), P(("groups", "graph"), "mp"))
    return jax.shard_map(
        on_device, mesh=mesh, in_specs=in_specs, out_specs=out_specs, check_vma=False
    )
```

```python
import functools

import jax
import jax.numpy as jnp
from jax import lax
from jax.experimental import pallas as pl
from jax.experimental.pallas import tpu as pltpu
from jax.sharding import PartitionSpec as P

COARSE_DEV = 12
COARSE_PAD = 16
EPS = 1e-05
TILE = 768
HOT_TILE = 256
F32 = jnp.float32
BF16 = jnp.bfloat16


def silu(x):
    half = x.astype(BF16) * jnp.asarray(0.5, BF16)
    return half + half * jnp.tanh(half)


def normalize(msg):
    width = msg.shape[1]
    mean = jnp.sum(msg, axis=1, keepdims=True) * (1.0 / width)
    square = jnp.sum(msg * msg, axis=1, keepdims=True) * (1.0 / width)
    return (msg - mean) * lax.rsqrt(square - mean * mean + EPS)


def dot(a, b):
    return jnp.dot(a, b, preferred_element_type=F32)


def own_columns(full, part):
    mine = lax.axis_index("mp")
    out = full[:, 0:part]
    for j in range(1, full.shape[1] // part):
        out = jnp.where(mine == j, full[:, j * part : (j + 1) * part], out)
    return out


class Copies:
    def __init__(self, sems):
        self.sems, self.started = sems, []

    def start(self, source, target):
        copy = pltpu.make_async_copy(source, target, self.sems.at[len(self.started)])
        copy.start()
        self.started.append(copy)

    def wait(self):
        for copy in self.started:
            copy.wait()


class Moves:
    def start(self, source, target):
        target[...] = source[...]

    def wait(self):
        pass


def load_shard(copies, layer, first, second, j, first_ref, second_ref):
    part = second.shape[1]
    copies.start(first.at[layer], first_ref.at[:, pl.ds(j * part, part)])
    copies.start(second.at[layer], second_ref.at[pl.ds(j * part, part)])


def load_packed(copies, packed, base, j, first_ref, second_ref):
    rows = first_ref.shape[0]
    hidden, features = second_ref.shape
    part = hidden // 4
    copies.start(packed.at[pl.ds(base, rows)], first_ref.at[:, pl.ds(j * part, part)])
    for q in range(features // part):
        copies.start(
            packed.at[pl.ds(base + rows + q * part, part)],
            second_ref.at[pl.ds(j * part, part), pl.ds(q * part, part)],
        )


def load_half(copies, packed, base, half, j, first_ref, second_ref):
    rows = first_ref.shape[0] // 2
    hidden, features = second_ref.shape
    part = hidden // 4
    deep = part // 2
    at = pl.multiple_of(half * rows, rows)
    copies.start(packed.at[pl.ds(base, rows)], first_ref.at[pl.ds(at, rows), pl.ds(j * part, part)])
    at = pl.multiple_of(j * part + half * deep, deep)
    for q in range(features // part):
        copies.start(
            packed.at[pl.ds(base + rows + q * deep, deep)],
            second_ref.at[pl.ds(at, deep), pl.ds(q * part, part)],
        )
    return base + rows + features // part * deep


def ride_kernel(ef, es, nf, ns, ride_out, sems):
    y = lax.axis_index("groups")
    part, features = es.shape[1:]
    copies = Copies(sems)
    at = 0
    for first, second in ((ef, es), (nf, ns)):
        rows = first.shape[1] // 2
        source = first.at[0, pl.ds(pl.multiple_of(y * rows, rows), rows)]
        copies.start(source, ride_out.at[pl.ds(at, rows)])
        at += rows
        deep = part // 2
        for q in range(features // part):
            source = second.at[0, pl.ds(pl.multiple_of(y * deep, deep), deep), pl.ds(q * part, part)]
            copies.start(source, ride_out.at[pl.ds(at, deep)])
            at += deep
    copies.wait()


def one_hot(hit):
    return jnp.where(hit, 1.0, 0.0).astype(BF16)


def column(row):
    return jnp.broadcast_to(row, (8, row.shape[1])).T[:, 0:1]


def make_pick(boundary, pick_out):
    halo = boundary.shape[1] // 2
    node_count = pick_out.shape[1]
    wanted = column(boundary)
    lanes = lax.broadcasted_iota(jnp.int32, (halo, node_count), 1)
    number = lax.broadcasted_iota(jnp.int32, (COARSE_PAD, node_count), 0)
    ids = lax.broadcasted_iota(jnp.int32, (COARSE_PAD, node_count), 1)
    coarse = one_hot((ids == number + (node_count - COARSE_DEV)) & (number < COARSE_DEV))
    wide = halo + COARSE_PAD
    pick_out[0:halo, :] = one_hot(lanes == wanted[halo:])
    pick_out[wide : wide + halo, :] = one_hot(lanes == wanted[:halo])
    for at in (halo, wide + halo, 2 * wide):
        pick_out[at : at + COARSE_PAD, :] = coarse


def pack_kernel(ef, es, nf, ns, pack_out, edge_late, node_late, sems):
    part, features = es.shape[1:]
    copies = Copies(sems)

    def pack(first, second, layer, out, at):
        rows = first.shape[1]
        copies.start(first.at[layer], out.at[pl.ds(at, rows)])
        at += rows
        for q in range(features // part):
            copies.start(second.at[layer, :, pl.ds(q * part, part)], out.at[pl.ds(at, part)])
            at += part
        return at

    end = 0
    for layer in range(ef.shape[0]):
        end = pack(nf, ns, layer, pack_out, pack(ef, es, layer, pack_out, end))
    pack(ef, es, 1, edge_late, 0)
    pack(nf, ns, 1, node_late, 0)
    copies.wait()


def prepare_kernel(blocks, halo, table_rows, list_ref, hot_out, incidence_out, pick_out):
    edge_count, lanes_all = hot_out.shape
    node_count = incidence_out.shape[0]
    for at in range(0, edge_count, HOT_TILE):
        senders = table_index(list_ref[:, at : at + HOT_TILE], blocks, node_count, halo)
        receivers = list_ref[:, edge_count + at : edge_count + at + HOT_TILE]
        lanes = lax.broadcasted_iota(jnp.int32, (HOT_TILE, lanes_all), 1)
        hit = (lanes == column(senders)) | (lanes == column(receivers) + table_rows)
        hot_out[at : at + HOT_TILE, :] = one_hot(hit)
        node_ids = lax.broadcasted_iota(jnp.int32, (node_count, HOT_TILE), 0)
        incidence_out[:, at : at + HOT_TILE] = one_hot(node_ids == receivers)
    make_pick(list_ref[:, 2 * edge_count : 2 * edge_count + 2 * halo], pick_out)


def pick_rows(pick_ref, node_bf, outs):
    picked = dot(pick_ref[...], node_bf).astype(BF16)
    start = 0
    for out in outs:
        out[...] = picked[start : start + out.shape[0]]
        start += out.shape[0]


def start_kernel(at, node_ref, list_ref, right, left, coarse, pick_ref):
    make_pick(list_ref[:, at:], pick_ref)
    pick_rows(pick_ref, node_ref[...].astype(BF16), (right, left, coarse))


def latent_kernel(*refs):
    out = refs[-1]
    at = 0
    for piece in refs[:-1]:
        out[at : at + piece.shape[0], :] = piece[...].astype(BF16)
        at += piece.shape[0]


def edge_rows(edge_ref, table, nodes, own_ref, hot_ref, incidence_ref, first_ref, second_ref, product_ref, own_out, full_out):
    features = second_ref.shape[1]
    node_count = nodes.shape[0]
    table_rows = table.shape[0]
    lanes_all = product_ref.shape[0]
    used = table_rows + node_count
    part = own_ref.shape[1]
    product_ref[0:table_rows, :] = dot(table, first_ref[features : 2 * features, :]).astype(BF16)
    product_ref[table_rows:used, :] = dot(
        nodes, first_ref[2 * features : 3 * features, :]
    ).astype(BF16)
    if used < lanes_all:
        product_ref[used:, :] = jnp.zeros((lanes_all - used, features), BF16)
    incoming = jnp.zeros((node_count, features), F32)
    for at in range(0, own_ref.shape[0], TILE):
        rows = slice(at, at + TILE)
        edge_bf = edge_ref[rows, :]
        pre = dot(edge_bf, first_ref[0:features, :]) + dot(hot_ref[rows, :], product_ref[...])
        norm = normalize(dot(silu(pre), second_ref[...]))
        edge_new = (edge_bf.astype(F32) + norm).astype(BF16)
        if full_out is not None:
            full_out[rows, :] = edge_new
        own_out[rows, :] = own_ref[rows, :] + own_columns(norm, part)
        incoming = incoming + dot(incidence_ref[:, rows], edge_new)
    return incoming.astype(BF16)


def node_rows(node_bf, incoming, own_ref, first_ref, second_ref, own_out):
    features = second_ref.shape[1]
    pre = dot(node_bf, first_ref[0:features, :]) + dot(incoming, first_ref[features:, :])
    norm = normalize(dot(silu(pre), second_ref[...]))
    own_out[...] = own_ref[...] + own_columns(norm, own_ref.shape[1])
    return (node_bf.astype(F32) + norm).astype(BF16)


def first_kernel(*refs):
    refs = list(refs)
    packs = [refs.pop(0) for _ in range(2)]
    halves = [[refs.pop(0) for _ in range(2)] for _ in range(2)]
    shards = [refs.pop(0) for _ in range(4)]
    edge_own, node_own, hot_ref, incidence_ref, pick_ref = [refs.pop(0) for _ in range(5)]
    edge_out, full_out, node_out, node_full = [refs.pop(0) for _ in range(4)]
    sends = [refs.pop(0) for _ in range(3)]
    edge_w, edge_w2, node_w, node_w2, product_ref, x_ref = refs
    part = edge_own.shape[1]
    edge_count = edge_own.shape[0]
    node_count = node_own.shape[0]
    edge_copies, node_copies = Moves(), Moves()
    for j, shard in enumerate(shards):
        column = pl.multiple_of((lax.axis_index("mp") ^ j) * part, part)
        edge_copies.start(shard, x_ref.at[:, pl.ds(column, part)])
    y = lax.axis_index("groups")
    starts = [0, 0]
    for base, copies, (first, second) in (
        (0, edge_copies, (edge_w, edge_w2)),
        (1, node_copies, (node_w, node_w2)),
    ):
        for j, pack in enumerate(packs):
            load_packed(copies, pack, (0, edge_w.shape[0] + edge_w2.shape[1])[base], j, first, second)
        for j, pair in enumerate(halves):
            for k, piece in enumerate(pair):
                half = y if k == 0 else 1 - y
                end = load_half(copies, piece, starts[base], half, 2 + j, first, second)
        starts[1] = end
    edge_copies.wait()
    nodes = x_ref[edge_count : edge_count + node_count, :]
    incoming = edge_rows(
        x_ref, x_ref[edge_count:, :], nodes, edge_own, hot_ref, incidence_ref,
        edge_w, edge_w2, product_ref, edge_out, full_out,
    )
    node_copies.wait()
    node_new = node_rows(nodes, incoming, node_own, node_w, node_w2, node_out)
    node_full[...] = node_new
    pick_rows(pick_ref, node_new, sends)


def late_weights(weights, base, first, second):
    moves = Moves()
    load_packed(moves, weights[0], base, 0, first, second)
    load_packed(moves, weights[1], base, 1, first, second)
    load_packed(moves, weights[2], 0, 2, first, second)
    load_packed(moves, weights[3], 0, 3, first, second)


def late_edge_kernel(pieces, base, *refs):
    refs = list(refs)
    weights = [refs.pop(0) for _ in range(4)]
    edge_ref, edge_own = [refs.pop(0) for _ in range(2)]
    tables = [refs.pop(0) for _ in range(pieces)]
    hot_ref, incidence_ref, edge_out, incoming_out = [refs.pop(0) for _ in range(4)]
    edge_w, edge_w2, product_ref, table_ref = refs
    late_weights(weights, base, edge_w, edge_w2)
    start = 0
    for table in tables:
        table_ref[start : start + table.shape[0], :] = table[...]
        start += table.shape[0]
    incoming_out[...] = edge_rows(
        edge_ref, table_ref[...], tables[0][...], edge_own, hot_ref, incidence_ref,
        edge_w, edge_w2, product_ref, edge_out, None,
    )


def late_node_kernel(base, *refs):
    weights = refs[:4]
    node_ref, node_own, incoming_ref, node_out, node_w, node_w2 = refs[4:]
    late_weights(weights, base, node_w, node_w2)
    node_rows(node_ref[...], incoming_ref[...], node_own, node_w, node_w2, node_out)


SMEM, VMEM, ANY = pltpu.SMEM, pltpu.VMEM, pl.ANY


def call(kernel, out_shape, args, scratch, flops, name, vmem_mib=8):
    arrays = [a for _, a in args]
    moved = sum(a.size * a.dtype.itemsize for a in arrays + list(out_shape))
    moved = sum(a.size * a.dtype.itemsize for a in arrays + list(out_shape))
    return pl.pallas_call(
        kernel,
        out_shape=out_shape,
        in_specs=[pl.BlockSpec(memory_space=s) for s, _ in args],
        out_specs=[pl.BlockSpec(memory_space=VMEM)] * len(out_shape),
        scratch_shapes=scratch,
        compiler_params=pltpu.CompilerParams(vmem_limit_bytes=vmem_mib * 1024 * 1024),
        cost_estimate=pl.CostEstimate(flops=0, bytes_accessed=0, transcendentals=0),
        name=name,
    )(*arrays)


def swap(x, mask):
    size = lax.axis_size("mp")
    return lax.ppermute(x, "mp", [(i, i ^ mask) for i in range(size)])


def shift(x, by):
    size = lax.axis_size("graph")
    return lax.ppermute(x, "graph", [(i, (i + by) % size) for i in range(size)])


def after(x, *others):
    return lax.optimization_barrier((x, *others))[0]


def neighbour_rows(right, left, coarse, halo):
    if lax.axis_size("graph") == 4:
        return [shift(right, 1), shift(left, -1), shift(coarse, 2)]
    everyone = lax.all_gather(coarse, "graph", axis=0, tiled=True)
    return [shift(right[:halo], 1), shift(left[:halo], -1), everyone]


def table_index(senders, size, node_count, halo):
    coarse_start = node_count + 2 * halo
    number = jnp.maximum(senders - coarse_start, 0)
    block = (number * 43691) >> 19
    row = number - block * COARSE_DEV
    if size != 4:
        return jnp.where(senders < coarse_start, senders, coarse_start + block * COARSE_PAD + row)
    wide = halo + COARSE_PAD
    away = (block - lax.axis_index("graph")) & 3
    starts = (node_count - COARSE_DEV, node_count + wide + halo, node_count + 2 * wide, node_count + halo)
    base = jnp.where(
        away < 2,
        jnp.where(away == 0, starts[0], starts[1]),
        jnp.where(away == 2, starts[2], starts[3]),
    )
    fine = jnp.where(senders < node_count + halo, senders, senders + COARSE_PAD)
    return jnp.where(senders < coarse_start, fine, base + row)


def on_device(
    node_state,
    edge_state,
    edge_first,
    edge_second,
    node_first,
    node_second,
    senders,
    receivers,
    boundary_rows,
):
    node_count, part = node_state.shape
    edge_count = edge_state.shape[0]
    features = edge_second.shape[2]
    hidden = 4 * part
    halo = boundary_rows.shape[0] // 2
    blocks = lax.axis_size("graph")
    shape = jax.ShapeDtypeStruct
    dma = pltpu.SemaphoreType.DMA

    wide = halo + COARSE_PAD

    def sent(width):
        return [shape((n, width), BF16) for n in (wide, wide, COARSE_PAD)]

    weights = (edge_first, edge_second, node_first, node_second)
    edge_pack = edge_first.shape[1] + features
    node_pack = node_first.shape[1] + features
    late_pack = edge_pack + node_pack
    (ride,) = call(
        ride_kernel,
        [shape(((edge_pack + node_pack) // 2, part), BF16)],
        [(ANY, w) for w in weights],
        [dma((10,))],
        0,
        "layer_0_half",
        60,
    )
    near = swap(ride, 2)
    far_rows = 2 * wide + COARSE_PAD if blocks == 4 else 2 * halo + blocks * COARSE_PAD
    table_rows = node_count + far_rows
    lanes = -(-(table_rows + node_count) // 128) * 128
    lists = jnp.concatenate([senders, receivers, boundary_rows])[None, :]
    right, left, coarse = call(
        functools.partial(start_kernel, 2 * edge_count),
        sent(part),
        [(VMEM, after(node_state, ride)), (VMEM, lists)],
        [pltpu.VMEM((2 * wide + COARSE_PAD, node_count), BF16)],
        0,
        "boundary_rows",
    )
    rows = neighbour_rows(right, left, coarse, halo)
    (latents,) = call(
        latent_kernel,
        [shape((edge_count + table_rows, part), BF16)],
        [(VMEM, edge_state), (VMEM, node_state)] + [(VMEM, r) for r in rows],
        [],
        0,
        "latents",
    )
    near = after(near, *rows)
    far_latents = swap(latents, 2)
    far = lax.ppermute(near, "groups", [(0, 1), (1, 0)])
    core_latents = swap(latents, 1)
    packs, edge_late, node_late = call(
        pack_kernel,
        [shape((n, part), BF16) for n in (2 * late_pack, edge_pack, node_pack)],
        [(ANY, after(weights[0], *rows))] + [(ANY, w) for w in weights[1:]],
        [dma((32,))],
        0,
        "packed_weights",
    )
    core_packs = swap(after(packs, near), 1)
    hot, incidence, pick = call(
        functools.partial(prepare_kernel, blocks, halo, table_rows),
        [
            shape((edge_count, lanes), BF16),
            shape((node_count, edge_count), BF16),
            shape((2 * wide + COARSE_PAD, node_count), BF16),
        ],
        [(VMEM, after(lists, near))],
        [],
        0,
        "one_hot",
    )
    core_near = swap(near, 1)
    core_far = swap(after(far, core_packs), 1)
    edge_late_x = swap(after(edge_late, near, hot), 2)
    node_late_x = swap(after(node_late, far_latents), 2)
    shards = [latents, core_latents, far_latents, swap(after(far_latents, far, core_packs, core_near), 1)]
    pairs = [near, far, core_near, core_far]

    edge_flops = 2 * edge_count * features * (2 * features + lanes + node_count)
    node_flops = 2 * node_count * features * 3 * features
    full_edge = shape((edge_count, features), BF16)
    full_node = shape((node_count, features), BF16)
    own_edge = shape((edge_count, part), F32)
    own_node = shape((node_count, part), F32)
    second_shape = pltpu.VMEM((hidden, features), BF16)
    edge_shape = pltpu.VMEM((edge_first.shape[1], hidden), BF16)
    node_shape = pltpu.VMEM((node_first.shape[1], hidden), BF16)

    edge_own, edge_full, node_own, node_full, right, left, coarse = call(
        first_kernel,
        [own_edge, full_edge, own_node, full_node] + sent(features),
        [(VMEM, w) for w in [packs, core_packs] + pairs + shards]
        + [(VMEM, a) for a in (edge_state, node_state, hot, incidence, pick)],
        [
            edge_shape,
            second_shape,
            node_shape,
            second_shape,
            pltpu.VMEM((lanes, hidden), BF16),
            pltpu.VMEM((edge_count + table_rows, features), BF16),
        ],
        edge_flops + node_flops,
        "layer_0",
        16,
    )
    tables = [node_full] + neighbour_rows(right, left, coarse, halo)
    edge_late_d = swap(after(edge_late_x, right), 1)
    edge_own, incoming = call(
        functools.partial(late_edge_kernel, len(tables), late_pack),
        [own_edge, full_node],
        [(VMEM, w) for w in (packs, core_packs, edge_late_x, edge_late_d)]
        + [(VMEM, a) for a in (edge_full, edge_own)]
        + [(VMEM, t) for t in tables]
        + [(VMEM, hot), (VMEM, incidence)],
        [
            edge_shape,
            second_shape,
            pltpu.VMEM((lanes, hidden), BF16),
            pltpu.VMEM((table_rows, features), BF16),
        ],
        edge_flops,
        "layer_1_edges",
        16,
    )
    node_late_d = swap(after(node_late_x, *tables[1:]), 1)
    (node_own,) = call(
        functools.partial(late_node_kernel, late_pack + edge_pack),
        [own_node],
        [(VMEM, w) for w in (packs, core_packs, node_late_x, node_late_d)]
        + [(VMEM, a) for a in (node_full, node_own, incoming)],
        [node_shape, second_shape],
        node_flops,
        "layer_1_nodes",
        16,
    )
    return (node_own, edge_own)


def solution(mesh):
    in_specs = (
        P(("groups", "graph"), "mp"),
        P(("groups", "graph"), "mp"),
        P(None, None, "mp"),
        P(None, "mp", None),
        P(None, None, "mp"),
        P(None, "mp", None),
        P("graph"),
        P("graph"),
        P("graph"),
    )
    out_specs = (P(("groups", "graph"), "mp"), P(("groups", "graph"), "mp"))
    return jax.shard_map(
        on_device, mesh=mesh, in_specs=in_specs, out_specs=out_specs, check_vma=False
    )
```

```python
import functools

import jax
import jax.numpy as jnp
from jax import lax
from jax.experimental import pallas as pl
from jax.experimental.pallas import tpu as pltpu
from jax.sharding import PartitionSpec as P

COARSE_DEV = 12
COARSE_PAD = 16
EPS = 1e-05
TILE = 768
HOT_TILE = 256
F32 = jnp.float32
BF16 = jnp.bfloat16


def silu(x):
    half = x.astype(BF16) * jnp.asarray(0.5, BF16)
    return half + half * jnp.tanh(half)


def normalize(msg):
    width = msg.shape[1]
    mean = jnp.sum(msg, axis=1, keepdims=True) * (1.0 / width)
    square = jnp.sum(msg * msg, axis=1, keepdims=True) * (1.0 / width)
    return (msg - mean) * lax.rsqrt(square - mean * mean + EPS)


def dot(a, b):
    return jnp.dot(a, b, preferred_element_type=F32)


def own_columns(full, part):
    mine = lax.axis_index("mp")
    out = full[:, 0:part]
    for j in range(1, full.shape[1] // part):
        out = jnp.where(mine == j, full[:, j * part : (j + 1) * part], out)
    return out


class Copies:
    def __init__(self, sems):
        self.sems, self.started = sems, []

    def start(self, source, target):
        copy = pltpu.make_async_copy(source, target, self.sems.at[len(self.started)])
        copy.start()
        self.started.append(copy)

    def wait(self):
        for copy in self.started:
            copy.wait()


class Moves:
    def start(self, source, target):
        target[...] = source[...]

    def wait(self):
        pass


def load_shard(copies, layer, first, second, j, first_ref, second_ref):
    part = second.shape[1]
    copies.start(first.at[layer], first_ref.at[:, pl.ds(j * part, part)])
    copies.start(second.at[layer], second_ref.at[pl.ds(j * part, part)])


def load_packed(copies, packed, base, j, first_ref, second_ref):
    rows = first_ref.shape[0]
    hidden, features = second_ref.shape
    part = hidden // 4
    copies.start(packed.at[pl.ds(base, rows)], first_ref.at[:, pl.ds(j * part, part)])
    for q in range(features // part):
        copies.start(
            packed.at[pl.ds(base + rows + q * part, part)],
            second_ref.at[pl.ds(j * part, part), pl.ds(q * part, part)],
        )


def load_half(copies, packed, base, half, j, first_ref, second_ref):
    rows = first_ref.shape[0] // 2
    hidden, features = second_ref.shape
    part = hidden // 4
    deep = part // 2
    at = pl.multiple_of(half * rows, rows)
    copies.start(packed.at[pl.ds(base, rows)], first_ref.at[pl.ds(at, rows), pl.ds(j * part, part)])
    at = pl.multiple_of(j * part + half * deep, deep)
    for q in range(features // part):
        copies.start(
            packed.at[pl.ds(base + rows + q * deep, deep)],
            second_ref.at[pl.ds(at, deep), pl.ds(q * part, part)],
        )
    return base + rows + features // part * deep


def ride_kernel(ef, es, nf, ns, ride_out, sems):
    y = lax.axis_index("groups")
    part, features = es.shape[1:]
    copies = Copies(sems)
    at = 0
    for first, second in ((ef, es), (nf, ns)):
        rows = first.shape[1] // 2
        source = first.at[0, pl.ds(pl.multiple_of(y * rows, rows), rows)]
        copies.start(source, ride_out.at[pl.ds(at, rows)])
        at += rows
        deep = part // 2
        for q in range(features // part):
            source = second.at[0, pl.ds(pl.multiple_of(y * deep, deep), deep), pl.ds(q * part, part)]
            copies.start(source, ride_out.at[pl.ds(at, deep)])
            at += deep
    copies.wait()


def one_hot(hit):
    return jnp.where(hit, 1.0, 0.0).astype(BF16)


def column(row):
    return jnp.broadcast_to(row, (8, row.shape[1])).T[:, 0:1]


def make_pick(boundary, pick_out):
    halo = boundary.shape[1] // 2
    node_count = pick_out.shape[1]
    wanted = column(boundary)
    lanes = lax.broadcasted_iota(jnp.int32, (halo, node_count), 1)
    number = lax.broadcasted_iota(jnp.int32, (COARSE_PAD, node_count), 0)
    ids = lax.broadcasted_iota(jnp.int32, (COARSE_PAD, node_count), 1)
    coarse = one_hot((ids == number + (node_count - COARSE_DEV)) & (number < COARSE_DEV))
    wide = halo + COARSE_PAD
    pick_out[0:halo, :] = one_hot(lanes == wanted[halo:])
    pick_out[wide : wide + halo, :] = one_hot(lanes == wanted[:halo])
    for at in (halo, wide + halo, 2 * wide):
        pick_out[at : at + COARSE_PAD, :] = coarse


def pack_kernel(ef, es, nf, ns, pack_out, edge_late, node_late, sems):
    part, features = es.shape[1:]
    copies = Copies(sems)

    def pack(first, second, layer, out, at):
        rows = first.shape[1]
        copies.start(first.at[layer], out.at[pl.ds(at, rows)])
        at += rows
        for q in range(features // part):
            copies.start(second.at[layer, :, pl.ds(q * part, part)], out.at[pl.ds(at, part)])
            at += part
        return at

    end = 0
    for layer in range(ef.shape[0]):
        end = pack(nf, ns, layer, pack_out, pack(ef, es, layer, pack_out, end))
    pack(ef, es, 1, edge_late, 0)
    pack(nf, ns, 1, node_late, 0)
    copies.wait()


def prepare_kernel(blocks, halo, table_rows, list_ref, hot_out, incidence_out, pick_out):
    edge_count, lanes_all = hot_out.shape
    node_count = incidence_out.shape[0]
    for at in range(0, edge_count, HOT_TILE):
        senders = table_index(list_ref[:, at : at + HOT_TILE], blocks, node_count, halo)
        receivers = list_ref[:, edge_count + at : edge_count + at + HOT_TILE]
        lanes = lax.broadcasted_iota(jnp.int32, (HOT_TILE, lanes_all), 1)
        hit = (lanes == column(senders)) | (lanes == column(receivers) + table_rows)
        hot_out[at : at + HOT_TILE, :] = one_hot(hit)
        node_ids = lax.broadcasted_iota(jnp.int32, (node_count, HOT_TILE), 0)
        incidence_out[:, at : at + HOT_TILE] = one_hot(node_ids == receivers)
    make_pick(list_ref[:, 2 * edge_count : 2 * edge_count + 2 * halo], pick_out)


def pick_rows(pick_ref, node_bf, outs):
    picked = dot(pick_ref[...], node_bf).astype(BF16)
    start = 0
    for out in outs:
        out[...] = picked[start : start + out.shape[0]]
        start += out.shape[0]


def start_kernel(at, node_ref, list_ref, right, left, coarse, pick_ref):
    make_pick(list_ref[:, at:], pick_ref)
    pick_rows(pick_ref, node_ref[...].astype(BF16), (right, left, coarse))


def latent_kernel(*refs):
    out = refs[-1]
    at = 0
    for piece in refs[:-1]:
        out[at : at + piece.shape[0], :] = piece[...].astype(BF16)
        at += piece.shape[0]


def edge_rows(edge_ref, table, nodes, own_ref, hot_ref, incidence_ref, first_ref, second_ref, product_ref, own_out, full_out):
    features = second_ref.shape[1]
    node_count = nodes.shape[0]
    table_rows = table.shape[0]
    lanes_all = product_ref.shape[0]
    used = table_rows + node_count
    part = own_ref.shape[1]
    product_ref[0:table_rows, :] = dot(table, first_ref[features : 2 * features, :]).astype(BF16)
    product_ref[table_rows:used, :] = dot(
        nodes, first_ref[2 * features : 3 * features, :]
    ).astype(BF16)
    if used < lanes_all:
        product_ref[used:, :] = jnp.zeros((lanes_all - used, features), BF16)
    incoming = jnp.zeros((node_count, features), F32)
    for at in range(0, own_ref.shape[0], TILE):
        rows = slice(at, at + TILE)
        edge_bf = edge_ref[rows, :]
        pre = dot(edge_bf, first_ref[0:features, :]) + dot(hot_ref[rows, :], product_ref[...])
        norm = normalize(dot(silu(pre), second_ref[...]))
        edge_new = (edge_bf.astype(F32) + norm).astype(BF16)
        if full_out is not None:
            full_out[rows, :] = edge_new
        own_out[rows, :] = own_ref[rows, :] + own_columns(norm, part)
        incoming = incoming + dot(incidence_ref[:, rows], edge_new)
    return incoming.astype(BF16)


def node_rows(node_bf, incoming, own_ref, first_ref, second_ref, own_out):
    features = second_ref.shape[1]
    pre = dot(node_bf, first_ref[0:features, :]) + dot(incoming, first_ref[features:, :])
    norm = normalize(dot(silu(pre), second_ref[...]))
    own_out[...] = own_ref[...] + own_columns(norm, own_ref.shape[1])
    return (node_bf.astype(F32) + norm).astype(BF16)


def first_kernel(*refs):
    refs = list(refs)
    packs = [refs.pop(0) for _ in range(2)]
    halves = [[refs.pop(0) for _ in range(2)] for _ in range(2)]
    shards = [refs.pop(0) for _ in range(4)]
    edge_own, node_own, hot_ref, incidence_ref, pick_ref = [refs.pop(0) for _ in range(5)]
    edge_out, full_out, node_out, node_full = [refs.pop(0) for _ in range(4)]
    sends = [refs.pop(0) for _ in range(3)]
    edge_w, edge_w2, node_w, node_w2, product_ref, x_ref = refs
    part = edge_own.shape[1]
    edge_count = edge_own.shape[0]
    node_count = node_own.shape[0]
    edge_copies, node_copies = Moves(), Moves()
    for j, shard in enumerate(shards):
        column = pl.multiple_of((lax.axis_index("mp") ^ j) * part, part)
        edge_copies.start(shard, x_ref.at[:, pl.ds(column, part)])
    y = lax.axis_index("groups")
    starts = [0, 0]
    for base, copies, (first, second) in (
        (0, edge_copies, (edge_w, edge_w2)),
        (1, node_copies, (node_w, node_w2)),
    ):
        for j, pack in enumerate(packs):
            load_packed(copies, pack, (0, edge_w.shape[0] + edge_w2.shape[1])[base], j, first, second)
        for j, pair in enumerate(halves):
            for k, piece in enumerate(pair):
                half = y if k == 0 else 1 - y
                end = load_half(copies, piece, starts[base], half, 2 + j, first, second)
        starts[1] = end
    edge_copies.wait()
    nodes = x_ref[edge_count : edge_count + node_count, :]
    incoming = edge_rows(
        x_ref, x_ref[edge_count:, :], nodes, edge_own, hot_ref, incidence_ref,
        edge_w, edge_w2, product_ref, edge_out, full_out,
    )
    node_copies.wait()
    node_new = node_rows(nodes, incoming, node_own, node_w, node_w2, node_out)
    node_full[...] = node_new
    pick_rows(pick_ref, node_new, sends)


def late_weights(weights, base, first, second):
    moves = Moves()
    load_packed(moves, weights[0], base, 0, first, second)
    load_packed(moves, weights[1], base, 1, first, second)
    load_packed(moves, weights[2], 0, 2, first, second)
    load_packed(moves, weights[3], 0, 3, first, second)


def late_edge_kernel(pieces, base, *refs):
    refs = list(refs)
    weights = [refs.pop(0) for _ in range(4)]
    edge_ref, edge_own = [refs.pop(0) for _ in range(2)]
    tables = [refs.pop(0) for _ in range(pieces)]
    hot_ref, incidence_ref, edge_out, incoming_out = [refs.pop(0) for _ in range(4)]
    edge_w, edge_w2, product_ref, table_ref = refs
    late_weights(weights, base, edge_w, edge_w2)
    start = 0
    for table in tables:
        table_ref[start : start + table.shape[0], :] = table[...]
        start += table.shape[0]
    incoming_out[...] = edge_rows(
        edge_ref, table_ref[...], tables[0][...], edge_own, hot_ref, incidence_ref,
        edge_w, edge_w2, product_ref, edge_out, None,
    )


def late_node_kernel(base, *refs):
    weights = refs[:4]
    node_ref, node_own, incoming_ref, node_out, node_w, node_w2 = refs[4:]
    late_weights(weights, base, node_w, node_w2)
    node_rows(node_ref[...], incoming_ref[...], node_own, node_w, node_w2, node_out)


SMEM, VMEM, ANY = pltpu.SMEM, pltpu.VMEM, pl.ANY


def call(kernel, out_shape, args, scratch, flops, name, vmem_mib=8):
    arrays = [a for _, a in args]
    moved = sum(a.size * a.dtype.itemsize for a in arrays + list(out_shape))
    moved = sum(a.size * a.dtype.itemsize for a in arrays + list(out_shape))
    return pl.pallas_call(
        kernel,
        out_shape=out_shape,
        in_specs=[pl.BlockSpec(memory_space=s) for s, _ in args],
        out_specs=[pl.BlockSpec(memory_space=VMEM)] * len(out_shape),
        scratch_shapes=scratch,
        compiler_params=pltpu.CompilerParams(vmem_limit_bytes=vmem_mib * 1024 * 1024),
        cost_estimate=pl.CostEstimate(flops=0, bytes_accessed=0, transcendentals=0),
        name=name,
    )(*arrays)


def swap(x, mask):
    size = lax.axis_size("mp")
    return lax.ppermute(x, "mp", [(i, i ^ mask) for i in range(size)])


def shift(x, by):
    size = lax.axis_size("graph")
    return lax.ppermute(x, "graph", [(i, (i + by) % size) for i in range(size)])


def after(x, *others):
    return lax.optimization_barrier((x, *others))[0]


def neighbour_rows(right, left, coarse, halo):
    if lax.axis_size("graph") == 4:
        return [shift(right, 1), shift(left, -1), shift(coarse, 2)]
    everyone = lax.all_gather(coarse, "graph", axis=0, tiled=True)
    return [shift(right[:halo], 1), shift(left[:halo], -1), everyone]


def table_index(senders, size, node_count, halo):
    coarse_start = node_count + 2 * halo
    number = jnp.maximum(senders - coarse_start, 0)
    block = (number * 43691) >> 19
    row = number - block * COARSE_DEV
    if size != 4:
        return jnp.where(senders < coarse_start, senders, coarse_start + block * COARSE_PAD + row)
    wide = halo + COARSE_PAD
    away = (block - lax.axis_index("graph")) & 3
    starts = (node_count - COARSE_DEV, node_count + wide + halo, node_count + 2 * wide, node_count + halo)
    base = jnp.where(
        away < 2,
        jnp.where(away == 0, starts[0], starts[1]),
        jnp.where(away == 2, starts[2], starts[3]),
    )
    fine = jnp.where(senders < node_count + halo, senders, senders + COARSE_PAD)
    return jnp.where(senders < coarse_start, fine, base + row)


def on_device(
    node_state,
    edge_state,
    edge_first,
    edge_second,
    node_first,
    node_second,
    senders,
    receivers,
    boundary_rows,
):
    node_count, part = node_state.shape
    edge_count = edge_state.shape[0]
    features = edge_second.shape[2]
    hidden = 4 * part
    halo = boundary_rows.shape[0] // 2
    blocks = lax.axis_size("graph")
    shape = jax.ShapeDtypeStruct
    dma = pltpu.SemaphoreType.DMA

    wide = halo + COARSE_PAD

    def sent(width):
        return [shape((n, width), BF16) for n in (wide, wide, COARSE_PAD)]

    weights = (edge_first, edge_second, node_first, node_second)
    edge_pack = edge_first.shape[1] + features
    node_pack = node_first.shape[1] + features
    late_pack = edge_pack + node_pack
    (ride,) = call(
        ride_kernel,
        [shape(((edge_pack + node_pack) // 2, part), BF16)],
        [(ANY, w) for w in weights],
        [dma((10,))],
        0,
        "layer_0_half",
        60,
    )
    near = swap(ride, 2)
    far_rows = 2 * wide + COARSE_PAD if blocks == 4 else 2 * halo + blocks * COARSE_PAD
    table_rows = node_count + far_rows
    lanes = -(-(table_rows + node_count) // 128) * 128
    lists = jnp.concatenate([senders, receivers, boundary_rows])[None, :]
    right, left, coarse = call(
        functools.partial(start_kernel, 2 * edge_count),
        sent(part),
        [(VMEM, after(node_state, ride)), (VMEM, lists)],
        [pltpu.VMEM((2 * wide + COARSE_PAD, node_count), BF16)],
        0,
        "boundary_rows",
    )
    rows = neighbour_rows(right, left, coarse, halo)
    (latents,) = call(
        latent_kernel,
        [shape((edge_count + table_rows, part), BF16)],
        [(VMEM, edge_state), (VMEM, node_state)] + [(VMEM, r) for r in rows],
        [],
        0,
        "latents",
    )
    near = after(near, *rows)
    far_latents = swap(latents, 2)
    far = lax.ppermute(near, "groups", [(0, 1), (1, 0)])
    core_latents = swap(latents, 1)
    packs, edge_late, node_late = call(
        pack_kernel,
        [shape((n, part), BF16) for n in (2 * late_pack, edge_pack, node_pack)],
        [(ANY, after(weights[0], *rows))] + [(ANY, w) for w in weights[1:]],
        [dma((32,))],
        0,
        "packed_weights",
    )
    core_packs = swap(after(packs, near), 1)
    hot, incidence, pick = call(
        functools.partial(prepare_kernel, blocks, halo, table_rows),
        [
            shape((edge_count, lanes), BF16),
            shape((node_count, edge_count), BF16),
            shape((2 * wide + COARSE_PAD, node_count), BF16),
        ],
        [(VMEM, after(lists, near))],
        [],
        0,
        "one_hot",
    )
    core_near = swap(near, 1)
    core_far = swap(after(far, core_packs), 1)
    edge_late_x = swap(after(edge_late, near, hot), 2)
    node_late_x = swap(after(node_late, far_latents), 2)
    shards = [latents, core_latents, far_latents, swap(after(far_latents, far, core_packs, core_near), 1)]
    pairs = [near, far, core_near, core_far]

    edge_flops = 2 * edge_count * features * (2 * features + lanes + node_count)
    node_flops = 2 * node_count * features * 3 * features
    full_edge = shape((edge_count, features), BF16)
    full_node = shape((node_count, features), BF16)
    own_edge = shape((edge_count, part), F32)
    own_node = shape((node_count, part), F32)
    second_shape = pltpu.VMEM((hidden, features), BF16)
    edge_shape = pltpu.VMEM((edge_first.shape[1], hidden), BF16)
    node_shape = pltpu.VMEM((node_first.shape[1], hidden), BF16)

    edge_own, edge_full, node_own, node_full, right, left, coarse = call(
        first_kernel,
        [own_edge, full_edge, own_node, full_node] + sent(features),
        [(VMEM, w) for w in [packs, core_packs] + pairs + shards]
        + [(VMEM, a) for a in (edge_state, node_state, hot, incidence, pick)],
        [
            edge_shape,
            second_shape,
            node_shape,
            second_shape,
            pltpu.VMEM((lanes, hidden), BF16),
            pltpu.VMEM((edge_count + table_rows, features), BF16),
        ],
        edge_flops + node_flops,
        "layer_0",
        16,
    )
    tables = [node_full] + neighbour_rows(right, left, coarse, halo)
    edge_late_d = swap(after(edge_late_x, right), 1)
    edge_own, incoming = call(
        functools.partial(late_edge_kernel, len(tables), late_pack),
        [own_edge, full_node],
        [(VMEM, w) for w in (packs, core_packs, edge_late_x, edge_late_d)]
        + [(VMEM, a) for a in (edge_full, edge_own)]
        + [(VMEM, t) for t in tables]
        + [(VMEM, hot), (VMEM, incidence)],
        [
            edge_shape,
            second_shape,
            pltpu.VMEM((lanes, hidden), BF16),
            pltpu.VMEM((table_rows, features), BF16),
        ],
        edge_flops,
        "layer_1_edges",
        16,
    )
    node_late_d = swap(after(node_late_x, incoming), 1)
    (node_own,) = call(
        functools.partial(late_node_kernel, late_pack + edge_pack),
        [own_node],
        [(VMEM, w) for w in (packs, core_packs, node_late_x, node_late_d)]
        + [(VMEM, a) for a in (node_full, node_own, incoming)],
        [node_shape, second_shape],
        node_flops,
        "layer_1_nodes",
        16,
    )
    return (node_own, edge_own)


def solution(mesh):
    in_specs = (
        P(("groups", "graph"), "mp"),
        P(("groups", "graph"), "mp"),
        P(None, None, "mp"),
        P(None, "mp", None),
        P(None, None, "mp"),
        P(None, "mp", None),
        P("graph"),
        P("graph"),
        P("graph"),
    )
    out_specs = (P(("groups", "graph"), "mp"), P(("groups", "graph"), "mp"))
    return jax.shard_map(
        on_device, mesh=mesh, in_specs=in_specs, out_specs=out_specs, check_vma=False
    )
```

```python
import functools

import jax
import jax.numpy as jnp
from jax import lax
from jax.experimental import pallas as pl
from jax.experimental.pallas import tpu as pltpu
from jax.sharding import PartitionSpec as P

COARSE_DEV = 12
COARSE_PAD = 16
EPS = 1e-05
TILE = 768
HOT_TILE = 256
F32 = jnp.float32
BF16 = jnp.bfloat16


def silu(x):
    half = x.astype(BF16) * jnp.asarray(0.5, BF16)
    return half + half * jnp.tanh(half)


def normalize(msg):
    width = msg.shape[1]
    mean = jnp.sum(msg, axis=1, keepdims=True) * (1.0 / width)
    square = jnp.sum(msg * msg, axis=1, keepdims=True) * (1.0 / width)
    return (msg - mean) * lax.rsqrt(square - mean * mean + EPS)


def dot(a, b):
    return jnp.dot(a, b, preferred_element_type=F32)


def own_columns(full, part):
    mine = lax.axis_index("mp")
    out = full[:, 0:part]
    for j in range(1, full.shape[1] // part):
        out = jnp.where(mine == j, full[:, j * part : (j + 1) * part], out)
    return out


class Copies:
    def __init__(self, sems):
        self.sems, self.started = sems, []

    def start(self, source, target):
        copy = pltpu.make_async_copy(source, target, self.sems.at[len(self.started)])
        copy.start()
        self.started.append(copy)

    def wait(self):
        for copy in self.started:
            copy.wait()


class Moves:
    def start(self, source, target):
        target[...] = source[...]

    def wait(self):
        pass


def load_shard(copies, layer, first, second, j, first_ref, second_ref):
    part = second.shape[1]
    copies.start(first.at[layer], first_ref.at[:, pl.ds(j * part, part)])
    copies.start(second.at[layer], second_ref.at[pl.ds(j * part, part)])


def load_packed(copies, packed, base, j, first_ref, second_ref):
    rows = first_ref.shape[0]
    hidden, features = second_ref.shape
    part = hidden // 4
    copies.start(packed.at[pl.ds(base, rows)], first_ref.at[:, pl.ds(j * part, part)])
    for q in range(features // part):
        copies.start(
            packed.at[pl.ds(base + rows + q * part, part)],
            second_ref.at[pl.ds(j * part, part), pl.ds(q * part, part)],
        )


def load_half(copies, packed, base, half, j, first_ref, second_ref):
    rows = first_ref.shape[0] // 2
    hidden, features = second_ref.shape
    part = hidden // 4
    deep = part // 2
    at = pl.multiple_of(half * rows, rows)
    copies.start(packed.at[pl.ds(base, rows)], first_ref.at[pl.ds(at, rows), pl.ds(j * part, part)])
    at = pl.multiple_of(j * part + half * deep, deep)
    for q in range(features // part):
        copies.start(
            packed.at[pl.ds(base + rows + q * deep, deep)],
            second_ref.at[pl.ds(at, deep), pl.ds(q * part, part)],
        )
    return base + rows + features // part * deep


def ride_kernel(ef, es, nf, ns, ride_out, sems):
    y = lax.axis_index("groups")
    part, features = es.shape[1:]
    copies = Copies(sems)
    at = 0
    for first, second in ((ef, es), (nf, ns)):
        rows = first.shape[1] // 2
        source = first.at[0, pl.ds(pl.multiple_of(y * rows, rows), rows)]
        copies.start(source, ride_out.at[pl.ds(at, rows)])
        at += rows
        deep = part // 2
        for q in range(features // part):
            source = second.at[0, pl.ds(pl.multiple_of(y * deep, deep), deep), pl.ds(q * part, part)]
            copies.start(source, ride_out.at[pl.ds(at, deep)])
            at += deep
    copies.wait()


def one_hot(hit):
    return jnp.where(hit, 1.0, 0.0).astype(BF16)


def column(row):
    return jnp.broadcast_to(row, (8, row.shape[1])).T[:, 0:1]


def make_pick(boundary, pick_out):
    halo = boundary.shape[1] // 2
    node_count = pick_out.shape[1]
    wanted = column(boundary)
    lanes = lax.broadcasted_iota(jnp.int32, (halo, node_count), 1)
    number = lax.broadcasted_iota(jnp.int32, (COARSE_PAD, node_count), 0)
    ids = lax.broadcasted_iota(jnp.int32, (COARSE_PAD, node_count), 1)
    coarse = one_hot((ids == number + (node_count - COARSE_DEV)) & (number < COARSE_DEV))
    wide = halo + COARSE_PAD
    pick_out[0:halo, :] = one_hot(lanes == wanted[halo:])
    pick_out[wide : wide + halo, :] = one_hot(lanes == wanted[:halo])
    for at in (halo, wide + halo, 2 * wide):
        pick_out[at : at + COARSE_PAD, :] = coarse


def pack_kernel(ef, es, nf, ns, pack_out, edge_late, node_late, sems):
    part, features = es.shape[1:]
    copies = Copies(sems)

    def pack(first, second, layer, out, at):
        rows = first.shape[1]
        copies.start(first.at[layer], out.at[pl.ds(at, rows)])
        at += rows
        for q in range(features // part):
            copies.start(second.at[layer, :, pl.ds(q * part, part)], out.at[pl.ds(at, part)])
            at += part
        return at

    end = 0
    for layer in range(ef.shape[0]):
        end = pack(nf, ns, layer, pack_out, pack(ef, es, layer, pack_out, end))
    pack(ef, es, 1, edge_late, 0)
    pack(nf, ns, 1, node_late, 0)
    copies.wait()


def prepare_kernel(blocks, halo, table_rows, list_ref, hot_out, incidence_out, pick_out):
    edge_count, lanes_all = hot_out.shape
    node_count = incidence_out.shape[0]
    for at in range(0, edge_count, HOT_TILE):
        senders = table_index(list_ref[:, at : at + HOT_TILE], blocks, node_count, halo)
        receivers = list_ref[:, edge_count + at : edge_count + at + HOT_TILE]
        lanes = lax.broadcasted_iota(jnp.int32, (HOT_TILE, lanes_all), 1)
        hit = (lanes == column(senders)) | (lanes == column(receivers) + table_rows)
        hot_out[at : at + HOT_TILE, :] = one_hot(hit)
        node_ids = lax.broadcasted_iota(jnp.int32, (node_count, HOT_TILE), 0)
        incidence_out[:, at : at + HOT_TILE] = one_hot(node_ids == receivers)
    make_pick(list_ref[:, 2 * edge_count : 2 * edge_count + 2 * halo], pick_out)


def pick_rows(pick_ref, node_bf, outs):
    picked = dot(pick_ref[...], node_bf).astype(BF16)
    start = 0
    for out in outs:
        out[...] = picked[start : start + out.shape[0]]
        start += out.shape[0]


def start_kernel(at, node_ref, list_ref, right, left, coarse, pick_ref):
    make_pick(list_ref[:, at:], pick_ref)
    pick_rows(pick_ref, node_ref[...].astype(BF16), (right, left, coarse))


def latent_kernel(*refs):
    out = refs[-1]
    at = 0
    for piece in refs[:-1]:
        out[at : at + piece.shape[0], :] = piece[...].astype(BF16)
        at += piece.shape[0]


def edge_rows(edge_ref, table, nodes, own_ref, hot_ref, incidence_ref, first_ref, second_ref, product_ref, own_out, full_out):
    features = second_ref.shape[1]
    node_count = nodes.shape[0]
    table_rows = table.shape[0]
    lanes_all = product_ref.shape[0]
    used = table_rows + node_count
    part = own_ref.shape[1]
    product_ref[0:table_rows, :] = dot(table, first_ref[features : 2 * features, :]).astype(BF16)
    product_ref[table_rows:used, :] = dot(
        nodes, first_ref[2 * features : 3 * features, :]
    ).astype(BF16)
    if used < lanes_all:
        product_ref[used:, :] = jnp.zeros((lanes_all - used, features), BF16)
    incoming = jnp.zeros((node_count, features), F32)
    for at in range(0, own_ref.shape[0], TILE):
        rows = slice(at, at + TILE)
        edge_bf = edge_ref[rows, :]
        pre = dot(edge_bf, first_ref[0:features, :]) + dot(hot_ref[rows, :], product_ref[...])
        norm = normalize(dot(silu(pre), second_ref[...]))
        edge_new = edge_bf + norm.astype(BF16)
        if full_out is not None:
            full_out[rows, :] = edge_new
        own_out[rows, :] = own_ref[rows, :] + own_columns(norm, part)
        incoming = incoming + dot(incidence_ref[:, rows], edge_new)
    return incoming.astype(BF16)


def node_rows(node_bf, incoming, own_ref, first_ref, second_ref, own_out):
    features = second_ref.shape[1]
    pre = dot(node_bf, first_ref[0:features, :]) + dot(incoming, first_ref[features:, :])
    norm = normalize(dot(silu(pre), second_ref[...]))
    own_out[...] = own_ref[...] + own_columns(norm, own_ref.shape[1])
    return (node_bf.astype(F32) + norm).astype(BF16)


def first_kernel(*refs):
    refs = list(refs)
    packs = [refs.pop(0) for _ in range(2)]
    halves = [[refs.pop(0) for _ in range(2)] for _ in range(2)]
    shards = [refs.pop(0) for _ in range(4)]
    edge_own, node_own, hot_ref, incidence_ref, pick_ref = [refs.pop(0) for _ in range(5)]
    edge_out, full_out, node_out, node_full = [refs.pop(0) for _ in range(4)]
    sends = [refs.pop(0) for _ in range(3)]
    edge_w, edge_w2, node_w, node_w2, product_ref, x_ref = refs
    part = edge_own.shape[1]
    edge_count = edge_own.shape[0]
    node_count = node_own.shape[0]
    edge_copies, node_copies = Moves(), Moves()
    for j, shard in enumerate(shards):
        column = pl.multiple_of((lax.axis_index("mp") ^ j) * part, part)
        edge_copies.start(shard, x_ref.at[:, pl.ds(column, part)])
    y = lax.axis_index("groups")
    starts = [0, 0]
    for base, copies, (first, second) in (
        (0, edge_copies, (edge_w, edge_w2)),
        (1, node_copies, (node_w, node_w2)),
    ):
        for j, pack in enumerate(packs):
            load_packed(copies, pack, (0, edge_w.shape[0] + edge_w2.shape[1])[base], j, first, second)
        for j, pair in enumerate(halves):
            for k, piece in enumerate(pair):
                half = y if k == 0 else 1 - y
                end = load_half(copies, piece, starts[base], half, 2 + j, first, second)
        starts[1] = end
    edge_copies.wait()
    nodes = x_ref[edge_count : edge_count + node_count, :]
    incoming = edge_rows(
        x_ref, x_ref[edge_count:, :], nodes, edge_own, hot_ref, incidence_ref,
        edge_w, edge_w2, product_ref, edge_out, full_out,
    )
    node_copies.wait()
    node_new = node_rows(nodes, incoming, node_own, node_w, node_w2, node_out)
    node_full[...] = node_new
    pick_rows(pick_ref, node_new, sends)


def late_weights(weights, base, first, second):
    moves = Moves()
    load_packed(moves, weights[0], base, 0, first, second)
    load_packed(moves, weights[1], base, 1, first, second)
    load_packed(moves, weights[2], 0, 2, first, second)
    load_packed(moves, weights[3], 0, 3, first, second)


def late_edge_kernel(pieces, base, *refs):
    refs = list(refs)
    weights = [refs.pop(0) for _ in range(4)]
    edge_ref, edge_own = [refs.pop(0) for _ in range(2)]
    tables = [refs.pop(0) for _ in range(pieces)]
    hot_ref, incidence_ref, edge_out, incoming_out = [refs.pop(0) for _ in range(4)]
    edge_w, edge_w2, product_ref, table_ref = refs
    late_weights(weights, base, edge_w, edge_w2)
    start = 0
    for table in tables:
        table_ref[start : start + table.shape[0], :] = table[...]
        start += table.shape[0]
    incoming_out[...] = edge_rows(
        edge_ref, table_ref[...], tables[0][...], edge_own, hot_ref, incidence_ref,
        edge_w, edge_w2, product_ref, edge_out, None,
    )


def late_node_kernel(base, *refs):
    weights = refs[:4]
    node_ref, node_own, incoming_ref, node_out, node_w, node_w2 = refs[4:]
    late_weights(weights, base, node_w, node_w2)
    node_rows(node_ref[...], incoming_ref[...], node_own, node_w, node_w2, node_out)


SMEM, VMEM, ANY = pltpu.SMEM, pltpu.VMEM, pl.ANY


def call(kernel, out_shape, args, scratch, flops, name, vmem_mib=8):
    arrays = [a for _, a in args]
    moved = sum(a.size * a.dtype.itemsize for a in arrays + list(out_shape))
    moved = sum(a.size * a.dtype.itemsize for a in arrays + list(out_shape))
    return pl.pallas_call(
        kernel,
        out_shape=out_shape,
        in_specs=[pl.BlockSpec(memory_space=s) for s, _ in args],
        out_specs=[pl.BlockSpec(memory_space=VMEM)] * len(out_shape),
        scratch_shapes=scratch,
        compiler_params=pltpu.CompilerParams(vmem_limit_bytes=vmem_mib * 1024 * 1024),
        cost_estimate=pl.CostEstimate(flops=0, bytes_accessed=0, transcendentals=0),
        name=name,
    )(*arrays)


def swap(x, mask):
    size = lax.axis_size("mp")
    return lax.ppermute(x, "mp", [(i, i ^ mask) for i in range(size)])


def shift(x, by):
    size = lax.axis_size("graph")
    return lax.ppermute(x, "graph", [(i, (i + by) % size) for i in range(size)])


def after(x, *others):
    return lax.optimization_barrier((x, *others))[0]


def neighbour_rows(right, left, coarse, halo):
    if lax.axis_size("graph") == 4:
        return [shift(right, 1), shift(left, -1), shift(coarse, 2)]
    everyone = lax.all_gather(coarse, "graph", axis=0, tiled=True)
    return [shift(right[:halo], 1), shift(left[:halo], -1), everyone]


def table_index(senders, size, node_count, halo):
    coarse_start = node_count + 2 * halo
    number = jnp.maximum(senders - coarse_start, 0)
    block = (number * 43691) >> 19
    row = number - block * COARSE_DEV
    if size != 4:
        return jnp.where(senders < coarse_start, senders, coarse_start + block * COARSE_PAD + row)
    wide = halo + COARSE_PAD
    away = (block - lax.axis_index("graph")) & 3
    starts = (node_count - COARSE_DEV, node_count + wide + halo, node_count + 2 * wide, node_count + halo)
    base = jnp.where(
        away < 2,
        jnp.where(away == 0, starts[0], starts[1]),
        jnp.where(away == 2, starts[2], starts[3]),
    )
    fine = jnp.where(senders < node_count + halo, senders, senders + COARSE_PAD)
    return jnp.where(senders < coarse_start, fine, base + row)


def on_device(
    node_state,
    edge_state,
    edge_first,
    edge_second,
    node_first,
    node_second,
    senders,
    receivers,
    boundary_rows,
):
    node_count, part = node_state.shape
    edge_count = edge_state.shape[0]
    features = edge_second.shape[2]
    hidden = 4 * part
    halo = boundary_rows.shape[0] // 2
    blocks = lax.axis_size("graph")
    shape = jax.ShapeDtypeStruct
    dma = pltpu.SemaphoreType.DMA

    wide = halo + COARSE_PAD

    def sent(width):
        return [shape((n, width), BF16) for n in (wide, wide, COARSE_PAD)]

    weights = (edge_first, edge_second, node_first, node_second)
    edge_pack = edge_first.shape[1] + features
    node_pack = node_first.shape[1] + features
    late_pack = edge_pack + node_pack
    (ride,) = call(
        ride_kernel,
        [shape(((edge_pack + node_pack) // 2, part), BF16)],
        [(ANY, w) for w in weights],
        [dma((10,))],
        0,
        "layer_0_half",
        60,
    )
    near = swap(ride, 2)
    far_rows = 2 * wide + COARSE_PAD if blocks == 4 else 2 * halo + blocks * COARSE_PAD
    table_rows = node_count + far_rows
    lanes = -(-(table_rows + node_count) // 128) * 128
    lists = jnp.concatenate([senders, receivers, boundary_rows])[None, :]
    right, left, coarse = call(
        functools.partial(start_kernel, 2 * edge_count),
        sent(part),
        [(VMEM, after(node_state, ride)), (VMEM, lists)],
        [pltpu.VMEM((2 * wide + COARSE_PAD, node_count), BF16)],
        0,
        "boundary_rows",
    )
    rows = neighbour_rows(right, left, coarse, halo)
    (latents,) = call(
        latent_kernel,
        [shape((edge_count + table_rows, part), BF16)],
        [(VMEM, edge_state), (VMEM, node_state)] + [(VMEM, r) for r in rows],
        [],
        0,
        "latents",
    )
    near = after(near, *rows)
    far_latents = swap(latents, 2)
    far = lax.ppermute(near, "groups", [(0, 1), (1, 0)])
    core_latents = swap(latents, 1)
    packs, edge_late, node_late = call(
        pack_kernel,
        [shape((n, part), BF16) for n in (2 * late_pack, edge_pack, node_pack)],
        [(ANY, after(weights[0], *rows))] + [(ANY, w) for w in weights[1:]],
        [dma((32,))],
        0,
        "packed_weights",
    )
    core_packs = swap(after(packs, near), 1)
    hot, incidence, pick = call(
        functools.partial(prepare_kernel, blocks, halo, table_rows),
        [
            shape((edge_count, lanes), BF16),
            shape((node_count, edge_count), BF16),
            shape((2 * wide + COARSE_PAD, node_count), BF16),
        ],
        [(VMEM, after(lists, near))],
        [],
        0,
        "one_hot",
    )
    core_near = swap(near, 1)
    core_far = swap(after(far, core_packs), 1)
    edge_late_x = swap(after(edge_late, near, hot), 2)
    node_late_x = swap(after(node_late, far_latents), 2)
    shards = [latents, core_latents, far_latents, swap(after(far_latents, far, core_packs, core_near), 1)]
    pairs = [near, far, core_near, core_far]

    edge_flops = 2 * edge_count * features * (2 * features + lanes + node_count)
    node_flops = 2 * node_count * features * 3 * features
    full_edge = shape((edge_count, features), BF16)
    full_node = shape((node_count, features), BF16)
    own_edge = shape((edge_count, part), F32)
    own_node = shape((node_count, part), F32)
    second_shape = pltpu.VMEM((hidden, features), BF16)
    edge_shape = pltpu.VMEM((edge_first.shape[1], hidden), BF16)
    node_shape = pltpu.VMEM((node_first.shape[1], hidden), BF16)

    edge_own, edge_full, node_own, node_full, right, left, coarse = call(
        first_kernel,
        [own_edge, full_edge, own_node, full_node] + sent(features),
        [(VMEM, w) for w in [packs, core_packs] + pairs + shards]
        + [(VMEM, a) for a in (edge_state, node_state, hot, incidence, pick)],
        [
            edge_shape,
            second_shape,
            node_shape,
            second_shape,
            pltpu.VMEM((lanes, hidden), BF16),
            pltpu.VMEM((edge_count + table_rows, features), BF16),
        ],
        edge_flops + node_flops,
        "layer_0",
        16,
    )
    tables = [node_full] + neighbour_rows(right, left, coarse, halo)
    edge_late_d = swap(after(edge_late_x, right), 1)
    edge_own, incoming = call(
        functools.partial(late_edge_kernel, len(tables), late_pack),
        [own_edge, full_node],
        [(VMEM, w) for w in (packs, core_packs, edge_late_x, edge_late_d)]
        + [(VMEM, a) for a in (edge_full, edge_own)]
        + [(VMEM, t) for t in tables]
        + [(VMEM, hot), (VMEM, incidence)],
        [
            edge_shape,
            second_shape,
            pltpu.VMEM((lanes, hidden), BF16),
            pltpu.VMEM((table_rows, features), BF16),
        ],
        edge_flops,
        "layer_1_edges",
        16,
    )
    node_late_d = swap(after(node_late_x, *tables[1:]), 1)
    (node_own,) = call(
        functools.partial(late_node_kernel, late_pack + edge_pack),
        [own_node],
        [(VMEM, w) for w in (packs, core_packs, node_late_x, node_late_d)]
        + [(VMEM, a) for a in (node_full, node_own, incoming)],
        [node_shape, second_shape],
        node_flops,
        "layer_1_nodes",
        16,
    )
    return (node_own, edge_own)


def solution(mesh):
    in_specs = (
        P(("groups", "graph"), "mp"),
        P(("groups", "graph"), "mp"),
        P(None, None, "mp"),
        P(None, "mp", None),
        P(None, None, "mp"),
        P(None, "mp", None),
        P("graph"),
        P("graph"),
        P("graph"),
    )
    out_specs = (P(("groups", "graph"), "mp"), P(("groups", "graph"), "mp"))
    return jax.shard_map(
        on_device, mesh=mesh, in_specs=in_specs, out_specs=out_specs, check_vma=False
    )
```
